32 devices in a mesh: dp: 8 (over y, x, core), tensor: 4 (over z).
Axes of the slice: x: 2, y: 2, z: 4, core: 2. Of those that a mesh axis runs over, the one named last changes fastest.
Arguments:
- tokens: bfloat16 [64, 128, 1024], P('dp', 'tensor'), may hold values from -6 to 6
- enc_states: bfloat16 [64, 256, 1024], P('dp', 'tensor'), may hold values from -6 to 6
- cotangent: bfloat16 [64, 128, 1024], P('dp', 'tensor'), may hold values from -6 to 6
- tok_len: int32 [64], replicated, may hold values from 16 to 128, as said below
- enc_len: int32 [64], replicated, may hold values from 128 to 256, as said below
- deal: int32 [64], replicated, may hold values from 0 to 63, as said below
- w_q_self: bfloat16 [1024, 1024], P(None, 'tensor'), may hold values from -0.1875 to 0.1875
- w_k_self: bfloat16 [1024, 1024], P(None, 'tensor'), may hold values from -0.1875 to 0.1875
- w_v_self: bfloat16 [1024, 1024], P(None, 'tensor'), may hold values from -0.1875 to 0.1875
- w_o_self: bfloat16 [1024, 1024], P('tensor'), may hold values from -1 to 1
- w_q_cross: bfloat16 [1024, 1024], P(None, 'tensor'), may hold values from -0.1875 to 0.1875
- w_k_cross: bfloat16 [1024, 1024], P(None, 'tensor'), may hold values from -0.1875 to 0.1875
- w_v_cross: bfloat16 [1024, 1024], P(None, 'tensor'), may hold values from -0.1875 to 0.1875
- w_o_cross: bfloat16 [1024, 1024], P('tensor'), may hold values from -2 to 2
- w_in: bfloat16 [1024, 4096], P(None, 'tensor'), may hold values from -0.1875 to 0.1875
- w_out: bfloat16 [4096, 1024], P('tensor'), may hold values from -0.09375 to 0.09375
- norm_gain: float32 [3, 1024], replicated, may hold values from 0.5 to 1.5
- norm_bias: float32 [3, 1024], replicated, may hold values from -1.75 to 1.75
Outputs:
- result: bfloat16 [64, 128, 1024], P('dp', 'tensor')
- d_tokens: bfloat16 [64, 128, 1024], P('dp', 'tensor')
- encoder_state_gradient: bfloat16 [64, 256, 1024], P('dp', 'tensor')
- d_w_q_self: float32 [1024, 1024], P('dp', 'tensor')
- d_w_k_self: float32 [1024, 1024], P('dp', 'tensor')
- d_w_v_self: float32 [1024, 1024], P('dp', 'tensor')
- d_w_o_self: float32 [1024, 1024], P('tensor', 'dp')
- d_w_q_cross: float32 [1024, 1024], P('dp', 'tensor')
- d_w_k_cross: float32 [1024, 1024], P('dp', 'tensor')
- d_w_v_cross: float32 [1024, 1024], P('dp', 'tensor')
- d_w_o_cross: float32 [1024, 1024], P('tensor', 'dp')
- d_w_in: float32 [1024, 4096], P('dp', 'tensor')
- d_w_out: float32 [4096, 1024], P('tensor', 'dp')
- d_norm_gain: float32 [3, 1024], replicated
- d_norm_bias: float32 [3, 1024], replicated
The draws below stay inside these ranges and needn't reach their ends.
Inputs may be any that keep to these rules, and one draw needn't show every extreme that they name: `tok_len`: some sequence has exactly 128 tokens. `enc_len`: some sequence has exactly 256 encoder states. deal is a permutation; deal[p] % 8 == p % 8; the 8 dealt positions of one index of dp hold sequences of 8 different indices of dp.
All inputs are finite; a program needn't handle non-finite values.
Results may differ from the reference program's by a relative error of at most 0.02.
Values may be sent and summed in bfloat16 or wider, within the bound.
A program may use at most 128 MiB of HBM per device.

```python
import math
import jax
import jax.numpy as jnp
from jax import lax

D = 1024
HEAD_DIM = 64
FF = 4096
SEQ_LEN = 128
ENC = 256
SEQ_DEV = 8
SEQS = 64


def draw_tok_len(key, part):
    first_key, second_key = jax.random.split(jax.random.fold_in(key, 11))
    sequence_lengths = jax.random.randint(first_key, (SEQS,), SEQ_LEN // 8, SEQ_LEN + 1)
    longest = jax.random.randint(second_key, (), 0, SEQS)
    return jnp.where(jnp.arange(SEQS) == longest, SEQ_LEN, sequence_lengths).astype(jnp.int32)


def draw_enc_len(key, part):
    first_key, second_key = jax.random.split(jax.random.fold_in(key, 23))
    sequence_lengths = jax.random.randint(first_key, (SEQS,), ENC // 2, ENC + 1)
    longest = jax.random.randint(second_key, (), 0, SEQS)
    return jnp.where(jnp.arange(SEQS) == longest, ENC, sequence_lengths).astype(jnp.int32)


def draw_deal(key, part):
    first_key, second_key = jax.random.split(jax.random.fold_in(key, 37))
    device_count = SEQS // SEQ_DEV
    ordering = jax.random.permutation(first_key, device_count)
    offsets = jax.random.permutation(second_key, device_count)[:SEQ_DEV]
    device_ids = jnp.arange(SEQS) // SEQ_DEV
    slot_ids = jnp.arange(SEQS) % SEQ_DEV
    sources = ordering[(device_ids - offsets[slot_ids]) % device_count]
    return (sources * SEQ_DEV + slot_ids).astype(jnp.int32)


def level_of(key, dims, shards, smallest, high):
    factor_of = 1.0
    for axis_at, shards_of in shards:
        heights = jax.random.uniform(jax.random.fold_in(jax.random.fold_in(key, 6), axis_at), (shards_of,), jnp.float32, smallest / len(shards), high / len(shards))
        factor_of = factor_of * jnp.repeat(jnp.exp(heights), dims[axis_at] // shards_of).reshape((-1,) + (1,) * (len(dims) - 1 - axis_at))
    return factor_of


def scatter_about(stream_key, extent, spread, most, pieces=(), kind=jnp.bfloat16):
    drawn = jax.random.normal(stream_key, extent, jnp.float32) * spread
    if len(pieces) > 0:
        drawn = level_of(stream_key, extent, pieces, -0.22, 0.18) * drawn
    return jnp.clip(drawn, min=-most, max=most).astype(kind)


def setup_inputs(seed: int = 0) -> dict:
    key_list = jax.random.split(jax.random.key(seed), 19)
    tokens = scatter_about(key_list[0], (SEQS, SEQ_LEN, D), 1.0, 6.0, ((0, 8), (1, 4)))
    enc_states = scatter_about(key_list[1], (SEQS, ENC, D), 1.0, 6.0, ((0, 8), (1, 4)))
    cotangent = scatter_about(key_list[2], (SEQS, SEQ_LEN, D), 1.0, 6.0, ((0, 8), (1, 4)))
    tok_len = draw_tok_len(jax.random.fold_in(key_list[18], 71), 0)
    enc_len = draw_enc_len(jax.random.fold_in(key_list[18], 71), 0)
    deal = draw_deal(jax.random.fold_in(key_list[18], 71), 0)
    w_q_self = scatter_about(key_list[6], (D, D), D ** -0.5, 0.1875, ((1, 4),))
    w_k_self = scatter_about(key_list[7], (D, D), D ** -0.5, 0.1875, ((1, 4),))
    w_v_self = scatter_about(key_list[8], (D, D), D ** -0.5, 0.1875, ((1, 4),))
    w_o_self = scatter_about(key_list[9], (D, D), (max(1, D * 4 // SEQ_LEN)) ** -0.5, 1.0, ((0, 4),))
    w_q_cross = scatter_about(key_list[10], (D, D), D ** -0.5, 0.1875, ((1, 4),))
    w_k_cross = scatter_about(key_list[11], (D, D), D ** -0.5, 0.1875, ((1, 4),))
    w_v_cross = scatter_about(key_list[12], (D, D), D ** -0.5, 0.1875, ((1, 4),))
    w_o_cross = scatter_about(key_list[13], (D, D), (max(1, D * 2 // ENC)) ** -0.5, 2.0, ((0, 4),))
    w_in = scatter_about(key_list[14], (D, FF), D ** -0.5, 0.1875, ((1, 4),))
    w_out = scatter_about(key_list[15], (FF, D), FF ** -0.5, 0.09375, ((0, 4),))
    norm_gain = jnp.clip(1.0 + 0.1 * jax.random.normal(key_list[16], (3, D), jnp.float32), 0.5, 1.5)
    norm_bias = scatter_about(key_list[17], (3, D), 0.3, 1.75, (), jnp.float32)
    return dict(tokens=tokens, enc_states=enc_states, cotangent=cotangent, tok_len=tok_len, enc_len=enc_len, deal=deal, w_q_self=w_q_self, w_k_self=w_k_self, w_v_self=w_v_self, w_o_self=w_o_self, w_q_cross=w_q_cross, w_k_cross=w_k_cross, w_v_cross=w_v_cross, w_o_cross=w_o_cross, w_in=w_in, w_out=w_out, norm_gain=norm_gain, norm_bias=norm_bias)


HIGHEST = lax.Precision.HIGHEST
MASKED = -1e+30
EPSILON = 1e-05

@jax.custom_vjp
def low(v):
    return lax.optimization_barrier(v.astype(jnp.bfloat16)).astype(jnp.float32)

@jax.custom_vjp
def low_back(v):
    return v

def low_keep(v):
    return (low(v), None)

def low_pass(kept, grad):
    return (grad,)

def back_keep(v):
    return (v, None)

def back_low(kept, grad):
    return (low(grad),)
low.defvjp(low_keep, low_pass)
low_back.defvjp(back_keep, back_low)

def layer_norm(value_entries, gain_row, bias_row):
    row_mean = lax.optimization_barrier(jnp.mean(value_entries, axis=-1, keepdims=True))
    variance = lax.optimization_barrier(jnp.mean(value_entries * value_entries, axis=-1, keepdims=True)) - row_mean * row_mean
    normed = (value_entries - row_mean) * lax.rsqrt(variance + EPSILON)
    return normed * gain_row + bias_row

def project(value_entries, weight_matrix):
    return jnp.einsum('...d,de->...e', value_entries, weight_matrix, precision=HIGHEST)

def attend_one(queries, key_rows, value_rows, key_limit, causal):
    head_count = queries.shape[-1] // HEAD_DIM
    query_heads = queries.reshape(queries.shape[0], head_count, HEAD_DIM)
    key_heads = key_rows.reshape(key_rows.shape[0], head_count, HEAD_DIM)
    value_heads = value_rows.reshape(value_rows.shape[0], head_count, HEAD_DIM)
    key_pos = jnp.arange(key_rows.shape[0], dtype=jnp.int32)
    limit_here = key_limit.astype(jnp.int32)
    allowed = jnp.broadcast_to(key_pos[None, :] < limit_here, (queries.shape[0], key_rows.shape[0]))
    if causal:
        query_pos = jnp.arange(queries.shape[0], dtype=jnp.int32)
        allowed = allowed & (key_pos[None, :] <= query_pos[:, None])
    raw_scores = low_back(jnp.einsum('qhd,khd->hqk', query_heads, key_heads, precision=HIGHEST))
    scores = jnp.where(allowed[None], raw_scores * (1.0 / math.sqrt(HEAD_DIM)), MASKED)
    row_max = lax.optimization_barrier(jnp.max(scores, axis=-1, keepdims=True))
    shifted = jnp.exp(scores - row_max)
    weights = low(shifted / lax.optimization_barrier(jnp.sum(shifted, axis=-1, keepdims=True)))
    output = jnp.einsum('hqk,khd->qhd', weights, value_heads, precision=HIGHEST)
    return output.reshape(queries.shape[0], -1)

def decoder_layer(tokens_in, states_in, sequence_lengths, limits, params):
    w_q_self, w_k_self, w_v_self, w_o_self, w_q_cross, w_k_cross, w_v_cross, w_o_cross, w_in, w_out, norm_gain, norm_bias = params
    positions = jnp.arange(tokens_in.shape[1], dtype=jnp.int32)
    row_mask = (positions[None, :] < sequence_lengths[:, None]).astype(tokens_in.dtype)[:, :, None]
    normed_one = low(layer_norm(tokens_in, norm_gain[0], norm_bias[0]))
    query_one = low_back(low(project(normed_one, w_q_self)))
    key_one = low_back(low(project(normed_one, w_k_self)))
    value_one = low_back(low(project(normed_one, w_v_self)))
    self_fn = jax.checkpoint(lambda operands: attend_one(*operands, True))
    attended_one = low_back(low(lax.map(self_fn, (query_one, key_one, value_one, sequence_lengths))))
    hidden_one = tokens_in + low_back(project(attended_one, w_o_self))
    normed_two = low(layer_norm(hidden_one, norm_gain[1], norm_bias[1]))
    query_two = low_back(low(project(normed_two, w_q_cross)))
    key_two = low_back(low(project(states_in, w_k_cross)))
    value_two = low_back(low(project(states_in, w_v_cross)))
    cross_fn = jax.checkpoint(lambda operands: attend_one(*operands, False))
    attended_two = low_back(low(lax.map(cross_fn, (query_two, key_two, value_two, limits))))
    hidden_two = hidden_one + low_back(project(attended_two, w_o_cross))
    normed_three = low(layer_norm(hidden_two, norm_gain[2], norm_bias[2]))
    pre_act = low_back(project(normed_three, w_in))
    activated = low(jax.nn.silu(pre_act))
    return (hidden_two + low_back(project(activated, w_out))) * row_mask

def reference(tokens, enc_states, cotangent, tok_len, enc_len, deal, w_q_self, w_k_self, w_v_self, w_o_self, w_q_cross, w_k_cross, w_v_cross, w_o_cross, w_in, w_out, norm_gain, norm_bias):
    params = tuple((weight_matrix.astype(jnp.float32) for weight_matrix in (w_q_self, w_k_self, w_v_self, w_o_self, w_q_cross, w_k_cross, w_v_cross, w_o_cross, w_in, w_out, norm_gain, norm_bias)))
    deal_index = deal.astype(jnp.int32)
    dealt_tokens = tokens[deal_index].astype(jnp.float32)
    dealt_states = enc_states[deal_index].astype(jnp.float32)
    dealt_grads = cotangent.astype(jnp.float32)
    dealt_lengths = tok_len.astype(jnp.int32)[deal_index]
    dealt_limits = enc_len.astype(jnp.int32)[deal_index]
    group_size = 4 if SEQS % 4 == 0 else 1
    group_count = SEQS // group_size

    def regroup(array):
        return array.reshape((group_count, group_size) + array.shape[1:])

    def advance(totals, slices):
        part_tokens, part_states, part_grads, part_lengths, part_limits = slices

        def forward(tokens_in, states_in, weights_in):
            return decoder_layer(tokens_in, states_in, part_lengths.astype(jnp.int32), part_limits.astype(jnp.int32), weights_in)
        output, pullback = jax.vjp(forward, part_tokens, part_states, params)
        grad_tokens, grad_states, grad_params = pullback(part_grads.astype(output.dtype))
        summed = jax.tree.map(lambda total, grad: total + grad.astype(total.dtype), totals, grad_params)
        return (summed, (output, grad_tokens, grad_states))
    zero_grads = jax.tree.map(lambda weight_matrix: jnp.zeros_like(weight_matrix), params)
    totals, stacked = lax.scan(advance, zero_grads, tuple((regroup(array) for array in (dealt_tokens, dealt_states, dealt_grads, dealt_lengths, dealt_limits))))
    outputs, grad_tokens, grad_states = stacked
    result = outputs.reshape(SEQS, SEQ_LEN, D).astype(jnp.bfloat16)
    flat_tokens = grad_tokens.reshape(SEQS, SEQ_LEN, D)
    flat_states = grad_states.reshape(SEQS, ENC, D)
    d_tokens = jnp.zeros_like(flat_tokens).at[deal_index].set(flat_tokens).astype(jnp.bfloat16)
    d_states = jnp.zeros_like(flat_states).at[deal_index].set(flat_states).astype(jnp.bfloat16)
    return (result, d_tokens, d_states, totals[0], totals[1], totals[2], totals[3], totals[4], totals[5], totals[6], totals[7], totals[8], totals[9], totals[10], totals[11])
```

```python
import functools

import jax
import jax.numpy as jnp
from jax import lax
from jax.experimental import pallas as pl
from jax.experimental.pallas import tpu as pltpu
from jax.sharding import PartitionSpec as P

HEAD_DIM = 64
SCALE = 0.125
MASKED = -1e30
EPSILON = 1e-05
MESH = pl.DeviceIdType.MESH
VMEM_LIMIT = 60 * 1024 * 1024
BF16 = jnp.bfloat16
F32 = jnp.float32


def dot_nn(a, b):
    return lax.dot_general(a, b, (((1,), (0,)), ((), ())), preferred_element_type=F32)


def dot_nt(a, b):
    return lax.dot_general(a, b, (((1,), (1,)), ((), ())), preferred_element_type=F32)


def dot_tn(a, b):
    return lax.dot_general(a, b, (((0,), (0,)), ((), ())), preferred_element_type=F32)


def norm_parts(v):
    mu = jnp.mean(v, axis=-1, keepdims=True)
    var = jnp.mean(v * v, axis=-1, keepdims=True) - mu * mu
    rstd = lax.rsqrt(var + EPSILON)
    return (v - mu) * rstd, rstd


def norm_back(dn, nh, rstd, gain):
    c = dn * gain
    return rstd * (
        c - jnp.mean(c, axis=-1, keepdims=True) - nh * jnp.mean(c * nh, axis=-1, keepdims=True)
    )


def head_stack(a, heads):
    lane = lax.broadcasted_iota(jnp.int32, a.shape, 1) // HEAD_DIM
    zero = jnp.zeros_like(a)
    return jnp.concatenate([jnp.where(lane == h, a, zero) for h in range(heads)], axis=0)


def attn_probs(q, k, limit, causal):
    heads = q.shape[1] // HEAD_DIM
    qs = head_stack(q, heads)
    s = dot_nt(qs, k) * SCALE
    key = lax.broadcasted_iota(jnp.int32, s.shape, 1)
    allowed = key < limit
    if causal:
        row = lax.rem(lax.broadcasted_iota(jnp.int32, s.shape, 0), q.shape[0])
        allowed = allowed & (key <= row)
    s = jnp.where(allowed, s, MASKED)
    e = jnp.exp(s - jnp.max(s, axis=-1, keepdims=True))
    return qs, e / jnp.sum(e, axis=-1, keepdims=True)


def lane_stack(a, heads):
    rows = a.shape[0] // heads
    return jnp.concatenate([a[h * rows : (h + 1) * rows] for h in range(heads)], axis=1)


def attn_fwd(q, k, v, limit, causal):
    heads = q.shape[1] // HEAD_DIM
    _, p = attn_probs(q, k, limit, causal)
    return dot_nn(lane_stack(p.astype(BF16), heads), head_stack(v, heads)).astype(BF16)


def attn_bwd(q, k, v, do, limit, causal):
    heads = q.shape[1] // HEAD_DIM
    qs, p = attn_probs(q, k, limit, causal)
    dos = head_stack(do, heads)
    dp = dot_nt(dos, v)
    delta = jnp.sum(p * dp, axis=-1, keepdims=True)
    ds = (p * (dp - delta) * SCALE).astype(BF16)
    dq = dot_nn(lane_stack(ds, heads), head_stack(k, heads)).astype(BF16)
    dk = dot_tn(ds, qs).astype(BF16)
    dv = dot_tn(p.astype(BF16), dos).astype(BF16)
    return dq, dk, dv


def params(steps):
    return pltpu.CompilerParams(
        dimension_semantics=("arbitrary",) * steps, vmem_limit_bytes=VMEM_LIMIT
    )


def whole(shape):
    return pl.BlockSpec(shape, lambda *_: (0,) * len(shape))


SMEM = pl.BlockSpec(memory_space=pltpu.SMEM)


def self_fwd_kernel(spd, lens, x_ref, gain, bias, w_ref, n1_ref, q_ref, k_ref, v_ref, o_ref, h_ref):
    j = pl.program_id(0)
    seq = x_ref.shape[0] // spd
    hc = q_ref.shape[2]

    @pl.when(j == 0)
    def _():
        x = x_ref[...].astype(F32)
        nh, _ = norm_parts(x)
        n1_ref[...] = (nh * gain[0:1] + bias[0:1]).astype(BF16)
        h_ref[...] = x

    w = w_ref.at[0, 0]
    qkv = dot_nn(n1_ref[...], w[:, : 3 * hc]).astype(BF16)
    q_ref[0] = qkv[:, :hc]
    k_ref[0] = qkv[:, hc : 2 * hc]
    v_ref[0] = qkv[:, 2 * hc :]
    for i in range(spd):
        rows = slice(i * seq, (i + 1) * seq)
        o_ref[0, rows] = attn_fwd(
            q_ref[0, rows], k_ref[0, rows], v_ref[0, rows], lens[i], True
        )
    h_ref[...] += dot_nt(o_ref[0], w[:, 3 * hc :])


def self_fwd(lens, x, gain, bias, wg, spd, nt):
    n, dim = x.shape
    hc = wg.shape[3] // 4
    part = pl.BlockSpec((1, n, hc), lambda j: (j, 0, 0))
    shaped = jax.ShapeDtypeStruct((nt, n, hc), BF16)
    return pl.pallas_call(
        functools.partial(self_fwd_kernel, spd),
        grid=(nt,),
        in_specs=[
            SMEM,
            whole((n, dim)),
            whole(gain.shape),
            whole(bias.shape),
            pl.BlockSpec((1, 1, dim, 4 * hc), lambda j: (j, 0, 0, 0)),
        ],
        out_specs=[whole((n, dim)), part, part, part, part, whole((n, dim))],
        out_shape=[
            jax.ShapeDtypeStruct((n, dim), BF16),
            shaped,
            shaped,
            shaped,
            shaped,
            jax.ShapeDtypeStruct((n, dim), F32),
        ],
        compiler_params=params(1),
        name="self_fwd",
    )(lens, x, gain, bias, wg)


def cross_fwd_kernel(
    spd, lens, h1_ref, ed_ref, gain, bias, w_ref, n2_ref, q_ref, k_ref, v_ref, o_ref, h_ref
):
    j = pl.program_id(0)
    seq = h1_ref.shape[0] // spd
    enc = ed_ref.shape[0] // spd
    hc = q_ref.shape[2]

    @pl.when(j == 0)
    def _():
        h = h1_ref[...]
        nh, _ = norm_parts(h)
        n2_ref[...] = (nh * gain[1:2] + bias[1:2]).astype(BF16)
        h_ref[...] = h

    w = w_ref.at[0, 0]
    q_ref[0] = dot_nn(n2_ref[...], w[:, :hc]).astype(BF16)
    kv = dot_nn(ed_ref[...], w[:, hc : 3 * hc]).astype(BF16)
    k_ref[0] = kv[:, :hc]
    v_ref[0] = kv[:, hc:]
    for i in range(spd):
        rows = slice(i * seq, (i + 1) * seq)
        keys = slice(i * enc, (i + 1) * enc)
        o_ref[0, rows] = attn_fwd(
            q_ref[0, rows], k_ref[0, keys], v_ref[0, keys], lens[i], False
        )
    h_ref[...] += dot_nt(o_ref[0], w[:, 3 * hc :])


def cross_fwd(lens, h1, ed, gain, bias, wg, spd, nt):
    n, dim = h1.shape
    m = ed.shape[0]
    hc = wg.shape[3] // 4
    part = pl.BlockSpec((1, n, hc), lambda j: (j, 0, 0))
    keys = pl.BlockSpec((1, m, hc), lambda j: (j, 0, 0))
    shaped = jax.ShapeDtypeStruct((nt, n, hc), BF16)
    long = jax.ShapeDtypeStruct((nt, m, hc), BF16)
    return pl.pallas_call(
        functools.partial(cross_fwd_kernel, spd),
        grid=(nt,),
        in_specs=[
            SMEM,
            whole((n, dim)),
            whole((m, dim)),
            whole(gain.shape),
            whole(bias.shape),
            pl.BlockSpec((1, 1, dim, 4 * hc), lambda j: (j, 1, 0, 0)),
        ],
        out_specs=[whole((n, dim)), part, keys, keys, part, whole((n, dim))],
        out_shape=[
            jax.ShapeDtypeStruct((n, dim), BF16),
            shaped,
            long,
            long,
            shaped,
            jax.ShapeDtypeStruct((n, dim), F32),
        ],
        compiler_params=params(1),
        name="cross_fwd",
    )(lens, h1, ed, gain, bias, wg)


def row_valid(lens, spd, n):
    row = lax.broadcasted_iota(jnp.int32, (n, 1), 0)
    seq = n // spd
    end = jnp.full((n, 1), lens[0], jnp.int32)
    for i in range(1, spd):
        end = jnp.where(row >= i * seq, i * seq + lens[i], end)
    return row < end


def feed_kernel(
    spd,
    lens,
    h2_ref,
    cot_ref,
    gain,
    bias,
    win_ref,
    wout_ref,
    res_ref,
    dh_ref,
    sums_ref,
    dw_in_ref,
    dw_out_ref,
    n3,
    n3t,
    g3,
    g3t,
    out_acc,
    dn_acc,
):
    step = pl.program_id(0) * pl.num_programs(1) + pl.program_id(1)
    last = pl.num_programs(0) * pl.num_programs(1) - 1
    n = h2_ref.shape[0]

    @pl.when(step == 0)
    def _():
        nh, _ = norm_parts(h2_ref[...])
        low = nh * gain[2:3] + bias[2:3]
        n3[...] = low.astype(BF16)
        n3t[...] = low.T.astype(BF16)
        keep = row_valid(lens, spd, n)
        dh = jnp.where(keep, cot_ref[...].astype(F32), 0.0)
        g3[...] = dh.astype(BF16)
        g3t[...] = dh.T.astype(BF16)
        out_acc[...] = jnp.zeros_like(out_acc)
        dn_acc[...] = jnp.zeros_like(dn_acc)

    win = win_ref[0, 0]
    wout = wout_ref[0, 0]
    u = dot_nn(n3[...], win)
    ga = dot_nn(g3[...], wout)
    sg = 1.0 / (1.0 + jnp.exp(-u))
    r = (u * sg).astype(BF16)
    du = (ga * (sg * (1.0 + u * (1.0 - sg)))).astype(BF16)
    out_acc[...] += dot_nt(r, wout)
    dn_acc[...] += dot_nt(du, win)
    dw_in_ref[0] = dot_nn(n3t[...], du).astype(BF16)
    dw_out_ref[0] = dot_nn(g3t[...], r).astype(BF16)

    @pl.when(step == last)
    def _():
        keep = row_valid(lens, spd, n)
        h2 = h2_ref[...]
        res_ref[...] = jnp.where(keep, h2 + out_acc[...], 0.0).astype(BF16)
        dh = jnp.where(keep, cot_ref[...].astype(F32), 0.0)
        nh, rstd = norm_parts(h2)
        dn = dn_acc[...]
        dh_ref[...] = dh + norm_back(dn, nh, rstd, gain[2:3])
        sums_ref[0:1] = jnp.sum(dn * nh, axis=0, keepdims=True)
        sums_ref[1:2] = jnp.sum(dn, axis=0, keepdims=True)


def feed(lens, h2, cot, gain, bias, wg, spd, nt):
    n, dim = h2.shape
    fc = wg.shape[3]
    block = min(512, fc)
    subs = fc // block
    dw = pl.BlockSpec((1, dim, block), lambda j, i: (j, 0, i))
    return pl.pallas_call(
        functools.partial(feed_kernel, spd),
        grid=(nt, subs),
        in_specs=[
            SMEM,
            whole((n, dim)),
            whole((n, dim)),
            whole(gain.shape),
            whole(bias.shape),
            pl.BlockSpec((1, 1, dim, block), lambda j, i: (j, 2, 0, i)),
            pl.BlockSpec((1, 1, dim, block), lambda j, i: (j, 3, 0, i)),
        ],
        out_specs=[whole((n, dim)), whole((n, dim)), whole((2, dim)), dw, dw],
        out_shape=[
            jax.ShapeDtypeStruct((n, dim), BF16),
            jax.ShapeDtypeStruct((n, dim), F32),
            jax.ShapeDtypeStruct((2, dim), F32),
            jax.ShapeDtypeStruct((nt, dim, fc), BF16),
            jax.ShapeDtypeStruct((nt, dim, fc), BF16),
        ],
        scratch_shapes=[
            pltpu.VMEM((n, dim), BF16),
            pltpu.VMEM((dim, n), BF16),
            pltpu.VMEM((n, dim), BF16),
            pltpu.VMEM((dim, n), BF16),
            pltpu.VMEM((n, dim), F32),
            pltpu.VMEM((n, dim), F32),
        ],
        compiler_params=params(2),
        name="feed_forward",
    )(lens, h2, cot, gain, bias, wg, wg)


def cross_bwd_kernel(
    spd,
    lens,
    dh2_ref,
    h1_ref,
    n2_ref,
    ed_ref,
    gain,
    q_ref,
    k_ref,
    v_ref,
    o_ref,
    w_ref,
    ded_ref,
    dh1_ref,
    sums_ref,
    dw_ref,
    g2,
    g2t,
    n2t,
    edt,
    dn_acc,
    ded_acc,
    dq,
    dk,
    dv,
):
    j = pl.program_id(0)
    n = h1_ref.shape[0]
    seq = n // spd
    enc = ed_ref.shape[0] // spd
    hc = q_ref.shape[2]

    @pl.when(j == 0)
    def _():
        dh = dh2_ref[...]
        g2[...] = dh.astype(BF16)
        g2t[...] = dh.T.astype(BF16)
        n2t[...] = n2_ref[...].T
        edt[...] = ed_ref[...].T
        dn_acc[...] = jnp.zeros_like(dn_acc)
        ded_acc[...] = jnp.zeros_like(ded_acc)

    w = w_ref.at[0, 0]
    do = dot_nn(g2[...], w[:, 3 * hc :]).astype(BF16)
    for i in range(spd):
        rows = slice(i * seq, (i + 1) * seq)
        keys = slice(i * enc, (i + 1) * enc)
        a, b, c = attn_bwd(
            q_ref[0, rows], k_ref[0, keys], v_ref[0, keys], do[rows], lens[i], False
        )
        dq[rows] = a
        dk[keys] = b
        dv[keys] = c
    dn_acc[...] += dot_nt(dq[...], w[:, :hc])
    ded_acc[...] += dot_nt(dk[...], w[:, hc : 2 * hc]) + dot_nt(dv[...], w[:, 2 * hc : 3 * hc])
    dw_ref[0, :, :hc] = dot_nn(n2t[...], dq[...]).astype(BF16)
    dw_ref[0, :, hc : 2 * hc] = dot_nn(edt[...], dk[...]).astype(BF16)
    dw_ref[0, :, 2 * hc : 3 * hc] = dot_nn(edt[...], dv[...]).astype(BF16)
    dw_ref[0, :, 3 * hc :] = dot_nn(g2t[...], o_ref[0]).astype(BF16)

    @pl.when(j == pl.num_programs(0) - 1)
    def _():
        ded_ref[...] = ded_acc[...].astype(BF16)
        nh, rstd = norm_parts(h1_ref[...])
        dn = dn_acc[...]
        dh1_ref[...] = dh2_ref[...] + norm_back(dn, nh, rstd, gain[1:2])
        sums_ref[0:1] = jnp.sum(dn * nh, axis=0, keepdims=True)
        sums_ref[1:2] = jnp.sum(dn, axis=0, keepdims=True)


def cross_bwd(lens, dh2, h1, n2, ed, gain, q, k, v, o, wg, spd, nt):
    n, dim = h1.shape
    m = ed.shape[0]
    hc = wg.shape[3] // 4
    part = pl.BlockSpec((1, n, hc), lambda j: (j, 0, 0))
    keys = pl.BlockSpec((1, m, hc), lambda j: (j, 0, 0))
    return pl.pallas_call(
        functools.partial(cross_bwd_kernel, spd),
        grid=(nt,),
        in_specs=[
            SMEM,
            whole((n, dim)),
            whole((n, dim)),
            whole((n, dim)),
            whole((m, dim)),
            whole(gain.shape),
            part,
            keys,
            keys,
            part,
            pl.BlockSpec((1, 1, dim, 4 * hc), lambda j: (j, 1, 0, 0)),
        ],
        out_specs=[
            whole((m, dim)),
            whole((n, dim)),
            whole((2, dim)),
            pl.BlockSpec((1, dim, 4 * hc), lambda j: (j, 0, 0)),
        ],
        out_shape=[
            jax.ShapeDtypeStruct((m, dim), BF16),
            jax.ShapeDtypeStruct((n, dim), F32),
            jax.ShapeDtypeStruct((2, dim), F32),
            jax.ShapeDtypeStruct((nt, dim, 4 * hc), BF16),
        ],
        scratch_shapes=[
            pltpu.VMEM((n, dim), BF16),
            pltpu.VMEM((dim, n), BF16),
            pltpu.VMEM((dim, n), BF16),
            pltpu.VMEM((dim, m), BF16),
            pltpu.VMEM((n, dim), F32),
            pltpu.VMEM((m, dim), F32),
            pltpu.VMEM((n, hc), BF16),
            pltpu.VMEM((m, hc), BF16),
            pltpu.VMEM((m, hc), BF16),
        ],
        compiler_params=params(1),
        name="cross_bwd",
    )(lens, dh2, h1, n2, ed, gain, q, k, v, o, wg)


def self_bwd_kernel(
    spd,
    lens,
    dh1_ref,
    x_ref,
    n1_ref,
    gain,
    q_ref,
    k_ref,
    v_ref,
    o_ref,
    w_ref,
    dx_ref,
    sums_ref,
    dw_ref,
    g1,
    g1t,
    n1t,
    dn_acc,
    dqkv,
):
    j = pl.program_id(0)
    n = x_ref.shape[0]
    seq = n // spd
    hc = q_ref.shape[2]

    @pl.when(j == 0)
    def _():
        dh = dh1_ref[...]
        g1[...] = dh.astype(BF16)
        g1t[...] = dh.T.astype(BF16)
        n1t[...] = n1_ref[...].T
        dn_acc[...] = jnp.zeros_like(dn_acc)

    w = w_ref.at[0, 0]
    do = dot_nn(g1[...], w[:, 3 * hc :]).astype(BF16)
    for i in range(spd):
        rows = slice(i * seq, (i + 1) * seq)
        a, b, c = attn_bwd(q_ref[0, rows], k_ref[0, rows], v_ref[0, rows], do[rows], lens[i], True)
        dqkv[rows, :hc] = a
        dqkv[rows, hc : 2 * hc] = b
        dqkv[rows, 2 * hc :] = c
    dn_acc[...] += dot_nt(dqkv[...], w[:, : 3 * hc])
    dw_ref[0, :, : 3 * hc] = dot_nn(n1t[...], dqkv[...]).astype(BF16)
    dw_ref[0, :, 3 * hc :] = dot_nn(g1t[...], o_ref[0]).astype(BF16)

    @pl.when(j == pl.num_programs(0) - 1)
    def _():
        nh, rstd = norm_parts(x_ref[...].astype(F32))
        dn = dn_acc[...]
        dx_ref[...] = (dh1_ref[...] + norm_back(dn, nh, rstd, gain[0:1])).astype(BF16)
        sums_ref[0:1] = jnp.sum(dn * nh, axis=0, keepdims=True)
        sums_ref[1:2] = jnp.sum(dn, axis=0, keepdims=True)


def self_bwd(lens, dh1, x, n1, gain, q, k, v, o, wg, spd, nt):
    n, dim = x.shape
    hc = wg.shape[3] // 4
    part = pl.BlockSpec((1, n, hc), lambda j: (j, 0, 0))
    return pl.pallas_call(
        functools.partial(self_bwd_kernel, spd),
        grid=(nt,),
        in_specs=[
            SMEM,
            whole((n, dim)),
            whole((n, dim)),
            whole((n, dim)),
            whole(gain.shape),
            part,
            part,
            part,
            part,
            pl.BlockSpec((1, 1, dim, 4 * hc), lambda j: (j, 0, 0, 0)),
        ],
        out_specs=[
            whole((n, dim)),
            whole((2, dim)),
            pl.BlockSpec((1, dim, 4 * hc), lambda j: (j, 0, 0)),
        ],
        out_shape=[
            jax.ShapeDtypeStruct((n, dim), BF16),
            jax.ShapeDtypeStruct((2, dim), F32),
            jax.ShapeDtypeStruct((nt, dim, 4 * hc), BF16),
        ],
        scratch_shapes=[
            pltpu.VMEM((n, dim), BF16),
            pltpu.VMEM((dim, n), BF16),
            pltpu.VMEM((dim, n), BF16),
            pltpu.VMEM((n, dim), F32),
            pltpu.VMEM((n, 3 * hc), BF16),
        ],
        compiler_params=params(1),
        name="self_bwd",
    )(lens, dh1, x, n1, gain, q, k, v, o, wg)


def flip(index, mask):
    out = index
    bit = 1
    while bit <= mask:
        if mask & bit:
            out = out + bit - 2 * bit * lax.rem(lax.div(index, bit), 2)
        bit *= 2
    return out


def greet(peers):
    barrier = pltpu.get_barrier_semaphore()
    for peer in peers:
        pl.semaphore_signal(barrier, inc=1, device_id=peer, device_id_type=MESH)
    pl.semaphore_wait(barrier, len(peers))


def gather_kernel(ndp, nt, own_ref, out_ref, own_sem, send_sems, recv_sems):
    d = lax.axis_index("dp")
    t = lax.axis_index("tensor")
    groups = own_ref.shape[0]
    half = own_ref.shape[2] // 2
    bits = ndp.bit_length() - 1
    chip_bits = [1 << b for b in range(1, bits)]
    orders = (chip_bits, chip_bits[::-1])

    def dp_peer(bit):
        return (flip(d, bit), t)

    def t_peer(j):
        return (d, flip(t, j))

    greet([dp_peer(1 << b) for b in range(bits)] + [t_peer(j) for j in range(1, nt)])
    own = pltpu.make_async_copy(own_ref, out_ref.at[0], own_sem)
    own.start()

    chunks = [(g, j) for g in range(groups) for j in range(1, nt)]
    started = []

    def send(c, slot, src, dst, peer):
        copy = pltpu.make_async_remote_copy(
            src_ref=src,
            dst_ref=dst,
            send_sem=send_sems.at[c, slot],
            recv_sem=recv_sems.at[c, slot],
            device_id=peer,
            device_id_type=MESH,
        )
        copy.start()
        started.append(copy)
        return copy

    first = [
        send(c, 0, own_ref.at[g, d], out_ref.at[j, g, d], t_peer(j))
        for c, (g, j) in enumerate(chunks)
    ]
    pending = {}

    def spread(c, level):
        g, j = chunks[c]
        if level == 0:
            first[c].wait_recv()
        else:
            for copy in pending.pop((c, level)):
                copy.wait_recv()
        slot = 1 + 2 * ((1 << level) - 1)
        copies = []
        if level < len(chip_bits):
            for side, order in enumerate(orders):
                held = [0]
                for bit in order[:level]:
                    held += [e ^ bit for e in held]
                rows = pl.ds(side * half, half)
                for e in held:
                    at = out_ref.at[j, g, flip(d, e), rows]
                    copies.append(send(c, slot, at, at, dp_peer(order[level])))
                    slot += 1
        else:
            for e in range(0, ndp, 2):
                at = out_ref.at[j, g, flip(d, e)]
                copies.append(send(c, slot, at, at, dp_peer(1)))
                slot += 1
        pending[(c, level + 1)] = copies

    levels = len(chip_bits) + 1
    for tick in range(len(chunks) + levels - 1):
        for level in range(levels):
            c = tick - level
            if 0 <= c < len(chunks):
                spread(c, level)
    for copies in pending.values():
        for copy in copies:
            copy.wait_recv()
    for copy in started:
        copy.wait_send()
    own.wait()


def gather_weights(own, ndp, nt):
    groups, dim, width = own.shape
    rows = dim // ndp
    count = groups * (nt - 1)
    slots = 1 + 2 * (ndp // 2 - 1) + ndp // 2
    out = pl.pallas_call(
        functools.partial(gather_kernel, ndp, nt),
        in_specs=[pl.BlockSpec(memory_space=pl.ANY)],
        out_specs=pl.BlockSpec(memory_space=pl.ANY),
        out_shape=jax.ShapeDtypeStruct((nt, groups, ndp, rows, width), BF16),
        scratch_shapes=[
            pltpu.SemaphoreType.DMA,
            pltpu.SemaphoreType.DMA((count, slots)),
            pltpu.SemaphoreType.DMA((count, slots)),
        ],
        compiler_params=pltpu.CompilerParams(
            collective_id=0, has_side_effects=True, vmem_limit_bytes=VMEM_LIMIT
        ),
        name="gather_weights",
    )(own.reshape(groups, ndp, rows, width))
    return out.reshape(nt, groups, dim, width)


def reduce_kernel(
    ndp,
    nt,
    dws_ref,
    dwc_ref,
    dwi_ref,
    dwo_ref,
    sums_ref,
    out_ref,
    norm_ref,
    got_core,
    got_chip,
    got_z,
    got_sum,
    mine,
    work,
    final,
    total,
    load_sems,
    send_sems,
    recv_sems,
    z_send,
    z_recv,
    sum_send,
    sum_recv,
):
    d = lax.axis_index("dp")
    t = lax.axis_index("tensor")
    bits = ndp.bit_length() - 1
    tbits = nt.bit_length() - 1
    chips = ndp // 2
    rows, width = out_ref.shape[1], out_ref.shape[2]
    half = rows // 2
    core = lax.rem(d, 2)
    chip = lax.div(d, 2)
    chip_bits = [1 << b for b in range(bits - 1)]
    orders = (chip_bits, chip_bits[::-1])
    levels = len(chip_bits)

    def dp_peer(bit):
        return (flip(d, bit), t)

    def t_peer(j):
        return (d, flip(t, j))

    greet([dp_peer(1 << b) for b in range(bits)] + [t_peer(j) for j in range(1, nt)])

    sources = [dwo_ref, dwi_ref, dwc_ref, dws_ref]
    target = [3, 2, 1, 0]
    chunks = [(s, j) for s in range(4) for j in list(range(1, nt)) + [0]]
    started = []

    def send(src, dst, ssem, rsem, peer):
        copy = pltpu.make_async_remote_copy(
            src_ref=src,
            dst_ref=dst,
            send_sem=ssem,
            recv_sem=rsem,
            device_id=peer,
            device_id_type=MESH,
        )
        copy.start()
        started.append(copy)
        return copy

    state = {}

    def core_send(c):
        s, j = chunks[c]
        src = sources[s].at[j, :, 1 - core]
        return send(src, got_core.at[c], send_sems.at[c, 0], recv_sems.at[c, 0], dp_peer(1))

    def core_load(c):
        s, j = chunks[c]
        copy = pltpu.make_async_copy(
            sources[s].at[j, :, core], mine.at[c % 2], load_sems.at[c % 2]
        )
        copy.start()
        return copy

    def core_add(c):
        core_copies[c].wait_recv()
        load_copies[c].wait()
        slot = c % levels
        if c >= levels:
            for copy in state.pop(("busy", c - levels)):
                copy.wait_send()
                started[:] = [one for one in started if one is not copy]

        def body(e, carry):
            a = mine[c % 2, e].astype(F32) + got_core[c, e].astype(F32)
            work[slot, e] = a.astype(BF16)
            return carry

        lax.fori_loop(0, chips, body, 0)
        if c + 2 < len(chunks):
            load_copies[c + 2] = core_load(c + 2)
        state[("busy", c)] = []
        chip_step(c, 0)

    def chip_step(c, level):
        slot = 1 + 2 * ((chips - (chips >> level)))
        base = 2 * (chips - (chips >> level))
        copies = []
        for side, order in enumerate(orders):
            rest = [0]
            for bit in order[level + 1 :]:
                rest += [e ^ bit for e in rest]
            for e in rest:
                far = flip(chip, order[level] ^ e)
                copies.append(
                    send(
                        work.at[c % levels, far, pl.ds(side * half, half)],
                        got_chip.at[c, base + len(copies)],
                        send_sems.at[c, slot + len(copies)],
                        recv_sems.at[c, slot + len(copies)],
                        dp_peer(2 * order[level]),
                    )
                )
        state[("busy", c)] += copies
        state[(c, level)] = copies

    def chip_add(c, level):
        base = 2 * (chips - (chips >> level))
        at = 0
        for copy in state[(c, level)]:
            copy.wait_recv()
        last = level == len(chip_bits) - 1
        s, j = chunks[c]
        for side, order in enumerate(orders):
            rest = [0]
            for bit in order[level + 1 :]:
                rest += [e ^ bit for e in rest]
            span = pl.ds(side * half, half)
            for e in rest:
                near = flip(chip, e)
                a = work[c % levels, near, span].astype(F32) + got_chip[c, base + at].astype(F32)
                at += 1
                if last:
                    final[c, span] = a.astype(BF16)
                else:
                    work[c % levels, near, span] = a.astype(BF16)
        if last:
            if j:
                state[("z", s, j)] = send(
                    final.at[c],
                    got_z.at[s, j - 1],
                    z_send.at[s, j - 1],
                    z_recv.at[s, j - 1],
                    t_peer(j),
                )
        else:
            chip_step(c, level + 1)

    def finish(s):
        c = chunks.index((s, 0))
        a = final[c].astype(F32)
        for j in range(1, nt):
            state[("z", s, j)].wait_recv()
            a = a + got_z[s, j - 1].astype(F32)
        out_ref[target[s]] = a

    sum_peers = [dp_peer(1 << b) for b in range(bits)] + [t_peer(1 << b) for b in range(tbits)]
    sum_copies = {}

    def sum_start(i):
        sum_copies[i] = send(
            total.at[i], got_sum.at[i], sum_send.at[i], sum_recv.at[i], sum_peers[i]
        )

    def sum_finish(i):
        sum_copies[i].wait_recv()
        total[i + 1] = total[i] + got_sum[i]

    total[0] = sums_ref[...]
    core_copies = [core_send(c) for c in range(len(chunks))]
    load_copies = {c: core_load(c) for c in range(2)}
    ticks = len(chunks) + levels
    for tick in range(ticks + 1):
        if tick < len(sum_peers):
            sum_start(tick)
        for stage in range(levels, -1, -1):
            c = tick - stage
            if 0 <= c < len(chunks):
                if stage == 0:
                    core_add(c)
                else:
                    chip_add(c, stage - 1)
        if tick < len(sum_peers):
            sum_finish(tick)
        c = tick - levels - 1
        if 0 <= c < len(chunks) and chunks[c][1] == 0:
            finish(chunks[c][0])
    norm_ref[...] = total[len(sum_peers)]
    for copy in started:
        copy.wait_send()


def reduce_grads(dws, dwc, dwi, dwo, sums, ndp, nt):
    dim, width = dws.shape[1:]
    rows, chips = dim // ndp, ndp // 2
    levels = chips.bit_length() - 1
    count = 4 * nt
    steps = (ndp.bit_length() - 1) + (nt.bit_length() - 1)
    view = (nt, chips, 2, rows, width)
    any_space = pl.BlockSpec(memory_space=pl.ANY)
    vmem = pl.BlockSpec(memory_space=pltpu.VMEM)
    slots = 1 + 2 * (chips - 1)
    return pl.pallas_call(
        functools.partial(reduce_kernel, ndp, nt),
        in_specs=[any_space] * 4 + [vmem],
        out_specs=[vmem, vmem],
        out_shape=[
            jax.ShapeDtypeStruct((4, rows, width), F32),
            jax.ShapeDtypeStruct(sums.shape, F32),
        ],
        scratch_shapes=[
            pltpu.VMEM((count, chips, rows, width), BF16),
            pltpu.VMEM((count, 2 * (chips - 1), rows // 2, width), BF16),
            pltpu.VMEM((4, nt - 1, rows, width), BF16),
            pltpu.VMEM((steps,) + sums.shape, F32),
            pltpu.VMEM((2, chips, rows, width), BF16),
            pltpu.VMEM((levels, chips, rows, width), BF16),
            pltpu.VMEM((count, rows, width), BF16),
            pltpu.VMEM((steps + 1,) + sums.shape, F32),
            pltpu.SemaphoreType.DMA((2,)),
            pltpu.SemaphoreType.DMA((count, slots)),
            pltpu.SemaphoreType.DMA((count, slots)),
            pltpu.SemaphoreType.DMA((4, nt - 1)),
            pltpu.SemaphoreType.DMA((4, nt - 1)),
            pltpu.SemaphoreType.DMA((steps,)),
            pltpu.SemaphoreType.DMA((steps,)),
        ],
        compiler_params=pltpu.CompilerParams(
            collective_id=1, has_side_effects=True, vmem_limit_bytes=VMEM_LIMIT
        ),
        name="reduce_grads",
    )(dws.reshape(view), dwc.reshape(view), dwi.reshape(view), dwo.reshape(view), sums)


def select_rows(lookup, positions):
    matches = positions[:, None] == jnp.arange(lookup.shape[0], dtype=jnp.int32)[None, :]
    return jnp.sum(jnp.where(matches, lookup[None, :], 0), axis=1)


def route_rows(selector, value_entries):
    return jnp.einsum(
        "kj,jrd->krd", selector, value_entries, preferred_element_type=F32
    ).astype(BF16)


def swap_dp(selector_out, selector_in, a):
    sent = lax.all_to_all(
        route_rows(selector_out, a), "dp", split_axis=0, concat_axis=0, tiled=True
    )
    return route_rows(selector_in, sent)


def to_sequences(a):
    return lax.all_to_all(a, "tensor", split_axis=0, concat_axis=1, tiled=True)


def to_positions(a):
    return lax.all_to_all(a, "tensor", split_axis=1, concat_axis=0, tiled=True)


def per_device(
    ndp,
    nt,
    tokens,
    enc_states,
    cotangent,
    tok_len,
    enc_len,
    deal,
    w_q_self,
    w_k_self,
    w_v_self,
    w_o_self,
    w_q_cross,
    w_k_cross,
    w_v_cross,
    w_o_cross,
    w_in,
    w_out,
    gain,
    bias,
):
    d = lax.axis_index("dp")
    t = lax.axis_index("tensor")
    seqs, _, dim = tokens.shape
    spd = seqs // nt
    hc = w_q_self.shape[1]
    slots = d * seqs + jnp.arange(seqs, dtype=jnp.int32)
    sources = select_rows(deal, slots)
    every = jnp.arange(deal.shape[0], dtype=jnp.int32)
    targets = jnp.sum(jnp.where(deal[None, :] == slots[:, None], every[None, :], 0), axis=1)
    peers = jnp.arange(ndp, dtype=jnp.int32)
    outward = (targets[None, :] // seqs == peers[:, None]).astype(BF16)
    inward = (sources[:, None] // seqs == peers[None, :]).astype(BF16)
    tok_lens = lax.dynamic_slice(select_rows(tok_len, sources), (t * spd,), (spd,))
    enc_lens = lax.dynamic_slice(select_rows(enc_len, sources), (t * spd,), (spd,))

    x = to_sequences(swap_dp(outward, inward, tokens)).reshape(-1, dim)
    ed = to_sequences(swap_dp(outward, inward, enc_states)).reshape(-1, dim)
    cot = to_sequences(cotangent).reshape(-1, dim)

    own = jnp.stack(
        [
            jnp.concatenate([w_q_self, w_k_self, w_v_self, w_o_self.T], axis=1),
            jnp.concatenate([w_q_cross, w_k_cross, w_v_cross, w_o_cross.T], axis=1),
            w_in,
            w_out.T,
        ]
    )
    wg = gather_weights(own, ndp, nt)

    n1, q1, k1, v1, o1, h1 = self_fwd(tok_lens, x, gain, bias, wg, spd, nt)
    n2, q2, k2, v2, o2, h2 = cross_fwd(enc_lens, h1, ed, gain, bias, wg, spd, nt)
    res, dh2, sums3, dwi, dwo = feed(tok_lens, h2, cot, gain, bias, wg, spd, nt)
    ded, dh1, sums2, dwc = cross_bwd(
        enc_lens, dh2, h1, n2, ed, gain, q2, k2, v2, o2, wg, spd, nt
    )
    dx, sums1, dws = self_bwd(tok_lens, dh1, x, n1, gain, q1, k1, v1, o1, wg, spd, nt)

    sums = jnp.concatenate(
        [sums1[:1], sums2[:1], sums3[:1], sums1[1:], sums2[1:], sums3[1:], jnp.zeros((2, dim), F32)]
    )
    grads, norm = reduce_grads(dws, dwc, dwi, dwo, sums, ndp, nt)

    def back(a):
        return swap_dp(inward.T, outward.T, to_positions(a.reshape(spd, -1, dim)))

    def attention(g):
        return (g[:, :hc], g[:, hc : 2 * hc], g[:, 2 * hc : 3 * hc], g[:, 3 * hc :].T)

    return (
        to_positions(res.reshape(spd, -1, dim)),
        back(dx),
        back(ded),
        *attention(grads[0]),
        *attention(grads[1]),
        grads[2],
        grads[3].T,
        norm[0:3],
        norm[3:6],
    )


def solution(mesh):
    ndp, nt = mesh.shape["dp"], mesh.shape["tensor"]
    rows = P("dp", "tensor", None)
    columns = P(None, "tensor")
    split = P("tensor", None)
    grad = P("dp", "tensor")
    turned = P("tensor", "dp")
    return jax.shard_map(
        functools.partial(per_device, ndp, nt),
        mesh=mesh,
        in_specs=(
            (rows,) * 3
            + (P(),) * 3
            + (columns, columns, columns, split) * 2
            + (columns, split, P(), P())
        ),
        out_specs=(
            (rows,) * 3 + (grad, grad, grad, turned) * 2 + (grad, turned) + (P(), P())
        ),
        check_vma=False,
    )
```

```python
import functools

import jax
import jax.numpy as jnp
from jax import lax
from jax.experimental import pallas as pl
from jax.experimental.pallas import tpu as pltpu
from jax.sharding import PartitionSpec as P

HEAD_DIM = 64
SCALE = 0.125
MASKED = -1e30
EPSILON = 1e-05
MESH = pl.DeviceIdType.MESH
VMEM_LIMIT = 60 * 1024 * 1024
BF16 = jnp.bfloat16
F32 = jnp.float32


def dot_nn(a, b):
    return lax.dot_general(a, b, (((1,), (0,)), ((), ())), preferred_element_type=F32)


def dot_nt(a, b):
    return lax.dot_general(a, b, (((1,), (1,)), ((), ())), preferred_element_type=F32)


def dot_tn(a, b):
    return lax.dot_general(a, b, (((0,), (0,)), ((), ())), preferred_element_type=F32)


def norm_parts(v):
    mu = jnp.mean(v, axis=-1, keepdims=True)
    var = jnp.mean(v * v, axis=-1, keepdims=True) - mu * mu
    rstd = lax.rsqrt(var + EPSILON)
    return (v - mu) * rstd, rstd


def norm_back(dn, nh, rstd, gain):
    c = dn * gain
    return rstd * (
        c - jnp.mean(c, axis=-1, keepdims=True) - nh * jnp.mean(c * nh, axis=-1, keepdims=True)
    )


def head_stack(a, heads):
    lane = lax.broadcasted_iota(jnp.int32, a.shape, 1) // HEAD_DIM
    zero = jnp.zeros_like(a)
    return jnp.concatenate([jnp.where(lane == h, a, zero) for h in range(heads)], axis=0)


def attn_probs(q, k, limit, causal):
    heads = q.shape[1] // HEAD_DIM
    qs = head_stack(q, heads)
    s = dot_nt(qs, k) * SCALE
    key = lax.broadcasted_iota(jnp.int32, s.shape, 1)
    allowed = key < limit
    if causal:
        row = lax.rem(lax.broadcasted_iota(jnp.int32, s.shape, 0), q.shape[0])
        allowed = allowed & (key <= row)
    s = jnp.where(allowed, s, MASKED)
    e = jnp.exp(s - jnp.max(s, axis=-1, keepdims=True))
    return qs, e / jnp.sum(e, axis=-1, keepdims=True)


def lane_stack(a, heads):
    rows = a.shape[0] // heads
    return jnp.concatenate([a[h * rows : (h + 1) * rows] for h in range(heads)], axis=1)


def attn_fwd(q, k, v, limit, causal):
    heads = q.shape[1] // HEAD_DIM
    _, p = attn_probs(q, k, limit, causal)
    return dot_nn(lane_stack(p.astype(BF16), heads), head_stack(v, heads)).astype(BF16)


def attn_bwd(q, k, v, do, limit, causal):
    heads = q.shape[1] // HEAD_DIM
    qs, p = attn_probs(q, k, limit, causal)
    dos = head_stack(do, heads)
    dp = dot_nt(dos, v)
    delta = jnp.sum(p * dp, axis=-1, keepdims=True)
    ds = (p * (dp - delta) * SCALE).astype(BF16)
    dq = dot_nn(lane_stack(ds, heads), head_stack(k, heads)).astype(BF16)
    dk = dot_tn(ds, qs).astype(BF16)
    dv = dot_tn(p.astype(BF16), dos).astype(BF16)
    return dq, dk, dv


def params(steps):
    return pltpu.CompilerParams(
        dimension_semantics=("arbitrary",) * steps, vmem_limit_bytes=VMEM_LIMIT
    )


def whole(shape):
    return pl.BlockSpec(shape, lambda *_: (0,) * len(shape))


SMEM = pl.BlockSpec(memory_space=pltpu.SMEM)


def row_valid(lens, spd, n):
    row = lax.broadcasted_iota(jnp.int32, (n, 1), 0)
    seq = n // spd
    end = jnp.full((n, 1), lens[0], jnp.int32)
    for i in range(1, spd):
        end = jnp.where(row >= i * seq, i * seq + lens[i], end)
    return row < end


def feed_kernel(
    spd,
    lens,
    h2_ref,
    cot_ref,
    gain,
    bias,
    win_ref,
    wout_ref,
    res_ref,
    dh_ref,
    sums_ref,
    dw_in_ref,
    dw_out_ref,
    n3,
    n3t,
    g3,
    g3t,
    out_acc,
    dn_acc,
):
    step = pl.program_id(0) * pl.num_programs(1) + pl.program_id(1)
    last = pl.num_programs(0) * pl.num_programs(1) - 1
    n = h2_ref.shape[0]

    @pl.when(step == 0)
    def _():
        nh, _ = norm_parts(h2_ref[...])
        low = nh * gain[2:3] + bias[2:3]
        n3[...] = low.astype(BF16)
        n3t[...] = low.T.astype(BF16)
        keep = row_valid(lens, spd, n)
        dh = jnp.where(keep, cot_ref[...].astype(F32), 0.0)
        g3[...] = dh.astype(BF16)
        g3t[...] = dh.T.astype(BF16)
        out_acc[...] = jnp.zeros_like(out_acc)
        dn_acc[...] = jnp.zeros_like(dn_acc)

    win = win_ref[0, 0]
    wout = wout_ref[0, 0]
    u = dot_nn(n3[...], win)
    ga = dot_nn(g3[...], wout)
    sg = 1.0 / (1.0 + jnp.exp(-u))
    r = (u * sg).astype(BF16)
    du = (ga * (sg * (1.0 + u * (1.0 - sg)))).astype(BF16)
    out_acc[...] += dot_nt(r, wout)
    dn_acc[...] += dot_nt(du, win)
    dw_in_ref[0] = dot_nn(n3t[...], du).astype(BF16)
    dw_out_ref[0] = dot_nn(g3t[...], r).astype(BF16)

    @pl.when(step == last)
    def _():
        keep = row_valid(lens, spd, n)
        h2 = h2_ref[...]
        res_ref[...] = jnp.where(keep, h2 + out_acc[...], 0.0).astype(BF16)
        dh = jnp.where(keep, cot_ref[...].astype(F32), 0.0)
        nh, rstd = norm_parts(h2)
        dn = dn_acc[...]
        dh_ref[...] = dh + norm_back(dn, nh, rstd, gain[2:3])
        sums_ref[0:1] = jnp.sum(dn * nh, axis=0, keepdims=True)
        sums_ref[1:2] = jnp.sum(dn, axis=0, keepdims=True)


def feed(lens, h2, cot, gain, bias, wg, spd, nt):
    n, dim = h2.shape
    fc = wg.shape[3]
    block = min(512, fc)
    subs = fc // block
    dw = pl.BlockSpec((1, dim, block), lambda j, i: (j, 0, i))
    return pl.pallas_call(
        functools.partial(feed_kernel, spd),
        grid=(nt, subs),
        in_specs=[
            SMEM,
            whole((n, dim)),
            whole((n, dim)),
            whole(gain.shape),
            whole(bias.shape),
            pl.BlockSpec((1, 1, dim, block), lambda j, i: (j, 2, 0, i)),
            pl.BlockSpec((1, 1, dim, block), lambda j, i: (j, 3, 0, i)),
        ],
        out_specs=[whole((n, dim)), whole((n, dim)), whole((2, dim)), dw, dw],
        out_shape=[
            jax.ShapeDtypeStruct((n, dim), BF16),
            jax.ShapeDtypeStruct((n, dim), F32),
            jax.ShapeDtypeStruct((2, dim), F32),
            jax.ShapeDtypeStruct((nt, dim, fc), BF16),
            jax.ShapeDtypeStruct((nt, dim, fc), BF16),
        ],
        scratch_shapes=[
            pltpu.VMEM((n, dim), BF16),
            pltpu.VMEM((dim, n), BF16),
            pltpu.VMEM((n, dim), BF16),
            pltpu.VMEM((dim, n), BF16),
            pltpu.VMEM((n, dim), F32),
            pltpu.VMEM((n, dim), F32),
        ],
        compiler_params=params(2),
        name="feed_forward",
    )(lens, h2, cot, gain, bias, wg, wg)


def cross_bwd_kernel(
    spd,
    lens,
    dh2_ref,
    h1_ref,
    n2_ref,
    ed_ref,
    gain,
    q_ref,
    k_ref,
    v_ref,
    o_ref,
    w_ref,
    ded_ref,
    dh1_ref,
    sums_ref,
    dw_ref,
    g2,
    g2t,
    n2t,
    edt,
    dn_acc,
    ded_acc,
    dq,
    dk,
    dv,
):
    j = pl.program_id(0)
    n = h1_ref.shape[0]
    seq = n // spd
    enc = ed_ref.shape[0] // spd
    hc = q_ref.shape[2]

    @pl.when(j == 0)
    def _():
        dh = dh2_ref[...]
        g2[...] = dh.astype(BF16)
        g2t[...] = dh.T.astype(BF16)
        n2t[...] = n2_ref[...].T
        edt[...] = ed_ref[...].T
        dn_acc[...] = jnp.zeros_like(dn_acc)
        ded_acc[...] = jnp.zeros_like(ded_acc)

    w = w_ref.at[0, 0]
    do = dot_nn(g2[...], w[:, 3 * hc :]).astype(BF16)
    for i in range(spd):
        rows = slice(i * seq, (i + 1) * seq)
        keys = slice(i * enc, (i + 1) * enc)
        a, b, c = attn_bwd(
            q_ref[0, rows], k_ref[0, keys], v_ref[0, keys], do[rows], lens[i], False
        )
        dq[rows] = a
        dk[keys] = b
        dv[keys] = c
    dn_acc[...] += dot_nt(dq[...], w[:, :hc])
    ded_acc[...] += dot_nt(dk[...], w[:, hc : 2 * hc]) + dot_nt(dv[...], w[:, 2 * hc : 3 * hc])
    dw_ref[0, :, :hc] = dot_nn(n2t[...], dq[...]).astype(BF16)
    dw_ref[0, :, hc : 2 * hc] = dot_nn(edt[...], dk[...]).astype(BF16)
    dw_ref[0, :, 2 * hc : 3 * hc] = dot_nn(edt[...], dv[...]).astype(BF16)
    dw_ref[0, :, 3 * hc :] = dot_nn(g2t[...], o_ref[0]).astype(BF16)

    @pl.when(j == pl.num_programs(0) - 1)
    def _():
        ded_ref[...] = ded_acc[...].astype(BF16)
        nh, rstd = norm_parts(h1_ref[...])
        dn = dn_acc[...]
        dh1_ref[...] = dh2_ref[...] + norm_back(dn, nh, rstd, gain[1:2])
        sums_ref[0:1] = jnp.sum(dn * nh, axis=0, keepdims=True)
        sums_ref[1:2] = jnp.sum(dn, axis=0, keepdims=True)


def cross_bwd(lens, dh2, h1, n2, ed, gain, q, k, v, o, wg, spd, nt):
    n, dim = h1.shape
    m = ed.shape[0]
    hc = wg.shape[3] // 4
    part = pl.BlockSpec((1, n, hc), lambda j: (j, 0, 0))
    keys = pl.BlockSpec((1, m, hc), lambda j: (j, 0, 0))
    return pl.pallas_call(
        functools.partial(cross_bwd_kernel, spd),
        grid=(nt,),
        in_specs=[
            SMEM,
            whole((n, dim)),
            whole((n, dim)),
            whole((n, dim)),
            whole((m, dim)),
            whole(gain.shape),
            part,
            keys,
            keys,
            part,
            pl.BlockSpec((1, 1, dim, 4 * hc), lambda j: (j, 1, 0, 0)),
        ],
        out_specs=[
            whole((m, dim)),
            whole((n, dim)),
            whole((2, dim)),
            pl.BlockSpec((1, dim, 4 * hc), lambda j: (j, 0, 0)),
        ],
        out_shape=[
            jax.ShapeDtypeStruct((m, dim), BF16),
            jax.ShapeDtypeStruct((n, dim), F32),
            jax.ShapeDtypeStruct((2, dim), F32),
            jax.ShapeDtypeStruct((nt, dim, 4 * hc), BF16),
        ],
        scratch_shapes=[
            pltpu.VMEM((n, dim), BF16),
            pltpu.VMEM((dim, n), BF16),
            pltpu.VMEM((dim, n), BF16),
            pltpu.VMEM((dim, m), BF16),
            pltpu.VMEM((n, dim), F32),
            pltpu.VMEM((m, dim), F32),
            pltpu.VMEM((n, hc), BF16),
            pltpu.VMEM((m, hc), BF16),
            pltpu.VMEM((m, hc), BF16),
        ],
        compiler_params=params(1),
        name="cross_bwd",
    )(lens, dh2, h1, n2, ed, gain, q, k, v, o, wg)


def self_bwd_kernel(
    spd,
    lens,
    dh1_ref,
    x_ref,
    n1_ref,
    gain,
    q_ref,
    k_ref,
    v_ref,
    o_ref,
    w_ref,
    dx_ref,
    sums_ref,
    dw_ref,
    g1,
    g1t,
    n1t,
    dn_acc,
    dqkv,
):
    j = pl.program_id(0)
    n = x_ref.shape[0]
    seq = n // spd
    hc = q_ref.shape[2]

    @pl.when(j == 0)
    def _():
        dh = dh1_ref[...]
        g1[...] = dh.astype(BF16)
        g1t[...] = dh.T.astype(BF16)
        n1t[...] = n1_ref[...].T
        dn_acc[...] = jnp.zeros_like(dn_acc)

    w = w_ref.at[0, 0]
    do = dot_nn(g1[...], w[:, 3 * hc :]).astype(BF16)
    for i in range(spd):
        rows = slice(i * seq, (i + 1) * seq)
        a, b, c = attn_bwd(q_ref[0, rows], k_ref[0, rows], v_ref[0, rows], do[rows], lens[i], True)
        dqkv[rows, :hc] = a
        dqkv[rows, hc : 2 * hc] = b
        dqkv[rows, 2 * hc :] = c
    dn_acc[...] += dot_nt(dqkv[...], w[:, : 3 * hc])
    dw_ref[0, :, : 3 * hc] = dot_nn(n1t[...], dqkv[...]).astype(BF16)
    dw_ref[0, :, 3 * hc :] = dot_nn(g1t[...], o_ref[0]).astype(BF16)

    @pl.when(j == pl.num_programs(0) - 1)
    def _():
        nh, rstd = norm_parts(x_ref[...].astype(F32))
        dn = dn_acc[...]
        dx_ref[...] = (dh1_ref[...] + norm_back(dn, nh, rstd, gain[0:1])).astype(BF16)
        sums_ref[0:1] = jnp.sum(dn * nh, axis=0, keepdims=True)
        sums_ref[1:2] = jnp.sum(dn, axis=0, keepdims=True)


def self_bwd(lens, dh1, x, n1, gain, q, k, v, o, wg, spd, nt):
    n, dim = x.shape
    hc = wg.shape[3] // 4
    part = pl.BlockSpec((1, n, hc), lambda j: (j, 0, 0))
    return pl.pallas_call(
        functools.partial(self_bwd_kernel, spd),
        grid=(nt,),
        in_specs=[
            SMEM,
            whole((n, dim)),
            whole((n, dim)),
            whole((n, dim)),
            whole(gain.shape),
            part,
            part,
            part,
            part,
            pl.BlockSpec((1, 1, dim, 4 * hc), lambda j: (j, 0, 0, 0)),
        ],
        out_specs=[
            whole((n, dim)),
            whole((2, dim)),
            pl.BlockSpec((1, dim, 4 * hc), lambda j: (j, 0, 0)),
        ],
        out_shape=[
            jax.ShapeDtypeStruct((n, dim), BF16),
            jax.ShapeDtypeStruct((2, dim), F32),
            jax.ShapeDtypeStruct((nt, dim, 4 * hc), BF16),
        ],
        scratch_shapes=[
            pltpu.VMEM((n, dim), BF16),
            pltpu.VMEM((dim, n), BF16),
            pltpu.VMEM((dim, n), BF16),
            pltpu.VMEM((n, dim), F32),
            pltpu.VMEM((n, 3 * hc), BF16),
        ],
        compiler_params=params(1),
        name="self_bwd",
    )(lens, dh1, x, n1, gain, q, k, v, o, wg)


def flip(index, mask):
    out = index
    bit = 1
    while bit <= mask:
        if mask & bit:
            out = out + bit - 2 * bit * lax.rem(lax.div(index, bit), 2)
        bit *= 2
    return out


def xor_of(a, b, size):
    out = 0
    bit = 1
    while bit < size:
        out = out + bit * lax.rem(lax.div(a, bit) + lax.div(b, bit), 2)
        bit *= 2
    return out


def greet(peers):
    barrier = pltpu.get_barrier_semaphore()
    for peer in peers:
        pl.semaphore_signal(barrier, inc=1, device_id=peer, device_id_type=MESH)
    pl.semaphore_wait(barrier, len(peers))


def front_kernel(
    ndp,
    nt,
    spd,
    tok_lens,
    enc_lens,
    in_peer,
    tok_blocks,
    enc_blocks,
    cot_ref,
    w_refs,
    gain,
    bias,
    wg,
    x_ref,
    ed_ref,
    cots_ref,
    n1_ref,
    q1_ref,
    k1_ref,
    v1_ref,
    o1_ref,
    h1_ref,
    n2_ref,
    q2_ref,
    k2_ref,
    v2_ref,
    o2_ref,
    h2_ref,
    rx_tok,
    rx_enc,
    zs_tok,
    zs_enc,
    own,
    raw_o,
    raw_out,
    wbuf,
    load_sems,
    own_sem,
    wbuf_sems,
    tok_send,
    tok_recv,
    enc_send,
    enc_recv,
    zt_send,
    zt_recv,
    ze_send,
    ze_recv,
    zc_send,
    zc_recv,
    line_send,
    pass_send,
    send_sems,
    recv_sems,
):
    d = lax.axis_index("dp")
    t = lax.axis_index("tensor")
    dim, width = own.shape[1:]
    hc = width // 4
    rows_each = dim // ndp
    half = rows_each // 2
    bits = ndp.bit_length() - 1
    chip_bits = [1 << b for b in range(1, bits)]
    orders = (chip_bits, chip_bits[::-1])
    levels = len(chip_bits)
    seqs, lr = cot_ref.shape[0], cot_ref.shape[1]
    le = enc_blocks.shape[1]
    seq, enc = nt * lr, nt * le
    n, m = spd * seq, spd * enc
    waits = []

    def dp_peer(bit):
        return (flip(d, bit), t)

    def t_peer(j):
        return (d, flip(t, j))

    def slab(index, side=None):
        if side is None:
            return pl.ds(pl.multiple_of(index * rows_each, rows_each), rows_each)
        return pl.ds(pl.multiple_of(index * rows_each + side * half, half), half)

    def remote(src, dst, ssem, rsem, peer):
        return pltpu.make_async_remote_copy(
            src_ref=src,
            dst_ref=dst,
            send_sem=ssem,
            recv_sem=rsem,
            device_id=peer,
            device_id_type=MESH,
        )

    def send(*args):
        copy = remote(*args)
        copy.start()
        waits.append(copy)
        return copy

    def local(src, dst, sem):
        copy = pltpu.make_async_copy(src, dst, sem)
        copy.start()
        return copy

    greet([dp_peer(e) for e in range(1, ndp)] + [t_peer(j) for j in range(1, nt)])

    def to_peers(blocks, rx, ssem, rsem):
        return [
            send(blocks.at[flip(d, e)], rx.at[d], ssem.at[e], rsem.at[e], dp_peer(e))
            for e in range(1, ndp)
        ], local(blocks.at[d], rx.at[d], rsem.at[0])

    tok_copies, tok_own = to_peers(tok_blocks, rx_tok, tok_send, tok_recv)

    wq1, wk1, wv1, wo1, wq2, wk2, wv2, wo2, w_in, w_out = w_refs
    loads = [
        local(src, dst, load_sems.at[i])
        for i, (src, dst) in enumerate(
            [
                (wo1, raw_o.at[0]),
                (wq1, own.at[0, :, pl.ds(0, hc)]),
                (wk1, own.at[0, :, pl.ds(hc, hc)]),
                (wv1, own.at[0, :, pl.ds(2 * hc, hc)]),
                (wo2, raw_o.at[1]),
                (wq2, own.at[1, :, pl.ds(0, hc)]),
                (wk2, own.at[1, :, pl.ds(hc, hc)]),
                (wv2, own.at[1, :, pl.ds(2 * hc, hc)]),
                (w_in, own.at[2]),
                (w_out, raw_out),
            ]
        )
    ]

    chunks = [(g, j) for g in range(4) for j in range(1, nt)]

    def line_copy(g, step):
        there = t + step
        j = xor_of(t, there, nt)
        return remote(
            own.at[g, slab(d)],
            wg.at[j, g, slab(d)],
            line_send.at[g, (step + 1) // 2],
            recv_sems.at[g * (nt - 1) + j - 1, 0],
            (d, there),
        )

    def pass_copy(c, step):
        g, j = chunks[c]
        there = t + step
        j_there = xor_of(flip(t, j), there, nt)
        return remote(
            wg.at[j, g, slab(d)],
            wg.at[j_there, g, slab(d)],
            pass_send.at[c],
            recv_sems.at[g * (nt - 1) + j_there - 1, 0],
            (d, there),
        )

    def on_line(act, g):
        @pl.when(t + 1 < nt)
        def _():
            act(line_copy(g, 1))

        @pl.when(t >= 1)
        def _():
            act(line_copy(g, -1))

    def on_pass(act, c):
        s = flip(t, chunks[c][1])

        @pl.when((s < t) & (t + 1 < nt))
        def _():
            act(pass_copy(c, 1))

        @pl.when((s > t) & (t >= 1))
        def _():
            act(pass_copy(c, -1))

    def start(copy):
        copy.start()

    def arrived(c):
        g, j = chunks[c]
        at = wg.at[j, g, slab(d)]
        remote(at, at, pass_send.at[c], recv_sems.at[c, 0], t_peer(j)).wait_recv()
        on_pass(start, c)

    pending = {}

    def spread(c, level):
        g, j = chunks[c]
        if level == 0:
            arrived(c)
        else:
            for copy in pending.pop((c, level)):
                copy.wait_recv()
        slot = 1 + 2 * ((1 << level) - 1)
        copies = []
        if level < levels:
            for side, order in enumerate(orders):
                held = [0]
                for bit in order[:level]:
                    held += [e ^ bit for e in held]
                for e in held:
                    at = wg.at[j, g, slab(flip(d, e), side)]
                    copies.append(
                        send(
                            at,
                            at,
                            send_sems.at[c, slot],
                            recv_sems.at[c, slot],
                            dp_peer(order[level]),
                        )
                    )
                    slot += 1
        elif level == levels:
            for e in range(0, ndp, 2):
                at = wg.at[j, g, slab(flip(d, e))]
                copies.append(
                    send(at, at, send_sems.at[c, slot], recv_sems.at[c, slot], dp_peer(1))
                )
                slot += 1
        elif g < 2:
            fills[c] = local(wg.at[j, g], wbuf.at[c % 2], wbuf_sems.at[c % 2])
        if copies:
            pending[(c, level + 1)] = copies

    fills = {}

    def to_sequences(src, dst, rows, ssem, rsem):
        for j in range(1, nt):
            there = flip(t, j)
            send(
                src.at[pl.ds(there * spd, spd)],
                dst.at[:, pl.ds(pl.multiple_of(t * rows, rows), rows)],
                ssem.at[j],
                rsem.at[j],
                t_peer(j),
            )
        return local(
            src.at[pl.ds(t * spd, spd)],
            dst.at[:, pl.ds(pl.multiple_of(t * rows, rows), rows)],
            rsem.at[0],
        )

    def sequences_here(own_copy, src, dst, rows, ssem, rsem):
        own_copy.wait()
        for j in range(1, nt):
            there = flip(t, j)
            remote(
                src.at[pl.ds(t * spd, spd)],
                dst.at[:, pl.ds(pl.multiple_of(there * rows, rows), rows)],
                ssem.at[j],
                rsem.at[j],
                t_peer(j),
            ).wait_recv()

    def blocks_here(copies, own_copy, rx, zs):
        own_copy.wait()
        for copy in copies:
            copy.wait_recv()
        for i in range(seqs):
            zs[i] = rx[in_peer[i]]

    def self_norm():
        x = x_ref[...].reshape(n, dim).astype(F32)
        nh, _ = norm_parts(x)
        n1_ref[...] = (nh * gain[0:1] + bias[0:1]).astype(BF16)
        h1_ref[...] = x

    def self_part(j, w):
        qkv = dot_nn(n1_ref[...], w[:, : 3 * hc]).astype(BF16)
        q1_ref[j] = qkv[:, :hc]
        k1_ref[j] = qkv[:, hc : 2 * hc]
        v1_ref[j] = qkv[:, 2 * hc :]
        for i in range(spd):
            rows = slice(i * seq, (i + 1) * seq)
            o1_ref[j, rows] = attn_fwd(
                q1_ref[j, rows], k1_ref[j, rows], v1_ref[j, rows], tok_lens[i], True
            )
        h1_ref[...] += dot_nt(o1_ref[j], w[:, 3 * hc :])

    def cross_norm():
        h = h1_ref[...]
        nh, _ = norm_parts(h)
        n2_ref[...] = (nh * gain[1:2] + bias[1:2]).astype(BF16)
        h2_ref[...] = h

    def cross_part(j, w):
        q2_ref[j] = dot_nn(n2_ref[...], w[:, :hc]).astype(BF16)
        kv = dot_nn(ed_ref[...].reshape(m, dim), w[:, hc : 3 * hc]).astype(BF16)
        k2_ref[j] = kv[:, :hc]
        v2_ref[j] = kv[:, hc:]
        for i in range(spd):
            rows = slice(i * seq, (i + 1) * seq)
            keys = slice(i * enc, (i + 1) * enc)
            o2_ref[j, rows] = attn_fwd(
                q2_ref[j, rows], k2_ref[j, keys], v2_ref[j, keys], enc_lens[i], False
            )
        h2_ref[...] += dot_nt(o2_ref[j], w[:, 3 * hc :])

    for i in range(4):
        loads[i].wait()
    own[0, :, 3 * hc :] = raw_o[0].T
    on_line(start, 0)
    blocks_here(tok_copies, tok_own, rx_tok, zs_tok)
    own_x = to_sequences(zs_tok, x_ref, lr, zt_send, zt_recv)
    enc_copies, enc_own = to_peers(enc_blocks, rx_enc, enc_send, enc_recv)
    for i in range(4, 10):
        loads[i].wait()
    own[1, :, 3 * hc :] = raw_o[1].T
    block = min(256, width)
    for at in range(0, width, block):
        own[3, :, at : at + block] = raw_out[at : at + block].T
    own_copy = local(own, wg.at[0], own_sem)

    state = {}
    ready = levels + 1
    count = len(chunks)
    per = nt - 1
    for tick in range(count + ready):
        for level in range(ready + 1):
            c = tick - level
            if 0 <= c < count:
                spread(c, level)
                if level == 0 and c % per == 0 and c // per + 1 < 4:
                    on_line(start, c // per + 1)
        if tick == 0:
            blocks_here(enc_copies, enc_own, rx_enc, zs_enc)
            own_ed = to_sequences(zs_enc, ed_ref, le, ze_send, ze_recv)
        if tick == 2:
            sequences_here(own_x, zs_tok, x_ref, lr, zt_send, zt_recv)
            self_norm()
            self_part(0, own.at[0])
        c = tick - ready - 1
        if 0 <= c < 2 * per:
            g, j = chunks[c]
            fills[c].wait()
            (self_part if g == 0 else cross_part)(j, wbuf.at[c % 2])
            if c == per - 1:
                sequences_here(own_ed, zs_enc, ed_ref, le, ze_send, ze_recv)
                own_cot = to_sequences(cot_ref, cots_ref, lr, zc_send, zc_recv)
                cross_norm()
                cross_part(0, own.at[1])

    sequences_here(own_cot, cot_ref, cots_ref, lr, zc_send, zc_recv)
    own_copy.wait()
    for g in range(4):
        on_line(lambda copy: copy.wait_send(), g)
    for c in range(count):
        on_pass(lambda copy: copy.wait_send(), c)
    for copy in waits:
        copy.wait_send()


def front(ndp, nt, spd, tok_lens, enc_lens, in_peer, tok_blocks, enc_blocks, cot, weights, gain, bias):
    seqs, lr, dim = cot.shape
    le = enc_blocks.shape[1]
    seq, enc = nt * lr, nt * le
    n, m = spd * seq, spd * enc
    hc = weights[0].shape[1]
    width = 4 * hc
    count = 4 * (nt - 1)
    slots = 1 + 2 * (ndp // 2 - 1) + ndp // 2
    smem = pl.BlockSpec(memory_space=pltpu.SMEM)
    vmem = pl.BlockSpec(memory_space=pltpu.VMEM)
    any_space = pl.BlockSpec(memory_space=pl.ANY)
    dma = pltpu.SemaphoreType.DMA
    shape = jax.ShapeDtypeStruct
    part, keys = shape((nt, n, hc), BF16), shape((nt, m, hc), BF16)

    def body(*refs):
        front_kernel(ndp, nt, spd, *refs[:6], refs[6:16], *refs[16:])

    return pl.pallas_call(
        body,
        in_specs=[smem] * 3 + [any_space] * 13 + [vmem] * 2,
        out_specs=[any_space, vmem, vmem, any_space] + [vmem] * 12,
        out_shape=[
            shape((nt, 4, dim, width), BF16),
            shape((spd, seq, dim), BF16),
            shape((spd, enc, dim), BF16),
            shape((spd, seq, dim), BF16),
            shape((n, dim), BF16),
            part,
            part,
            part,
            part,
            shape((n, dim), F32),
            shape((n, dim), BF16),
            part,
            keys,
            keys,
            part,
            shape((n, dim), F32),
        ],
        scratch_shapes=[
            pltpu.VMEM((ndp, lr, dim), BF16),
            pltpu.VMEM((ndp, le, dim), BF16),
            pltpu.VMEM((seqs, lr, dim), BF16),
            pltpu.VMEM((seqs, le, dim), BF16),
            pltpu.VMEM((4, dim, width), BF16),
            pltpu.VMEM((2, hc, dim), BF16),
            pltpu.VMEM((width, dim), BF16),
            pltpu.VMEM((2, dim, width), BF16),
            dma((10,)),
            dma,
            dma((2,)),
            dma((ndp,)),
            dma((ndp,)),
            dma((ndp,)),
            dma((ndp,)),
            dma((nt,)),
            dma((nt,)),
            dma((nt,)),
            dma((nt,)),
            dma((nt,)),
            dma((nt,)),
            dma((4, 2)),
            dma((count,)),
            dma((count, slots)),
            dma((count, slots)),
        ],
        compiler_params=pltpu.CompilerParams(
            collective_id=0, has_side_effects=True, vmem_limit_bytes=VMEM_LIMIT
        ),
        name="front",
    )(tok_lens, enc_lens, in_peer, tok_blocks, enc_blocks, cot, *weights, gain, bias)


def reduce_kernel(
    ndp,
    nt,
    dws_ref,
    dwc_ref,
    dwi_ref,
    dwo_ref,
    sums_ref,
    out_ref,
    norm_ref,
    got_core,
    got_chip,
    got_z,
    got_sum,
    mine,
    work,
    final,
    total,
    load_sems,
    send_sems,
    recv_sems,
    z_send,
    z_recv,
    sum_send,
    sum_recv,
):
    d = lax.axis_index("dp")
    t = lax.axis_index("tensor")
    bits = ndp.bit_length() - 1
    tbits = nt.bit_length() - 1
    chips = ndp // 2
    rows, width = out_ref.shape[1], out_ref.shape[2]
    half = rows // 2
    core = lax.rem(d, 2)
    chip = lax.div(d, 2)
    chip_bits = [1 << b for b in range(bits - 1)]
    orders = (chip_bits, chip_bits[::-1])
    levels = len(chip_bits)

    def dp_peer(bit):
        return (flip(d, bit), t)

    def t_peer(j):
        return (d, flip(t, j))

    greet([dp_peer(1 << b) for b in range(bits)] + [t_peer(j) for j in range(1, nt)])

    sources = [dwo_ref, dwi_ref, dwc_ref, dws_ref]
    target = [3, 2, 1, 0]
    chunks = [(s, j) for s in range(4) for j in list(range(1, nt)) + [0]]
    started = []

    def send(src, dst, ssem, rsem, peer):
        copy = pltpu.make_async_remote_copy(
            src_ref=src,
            dst_ref=dst,
            send_sem=ssem,
            recv_sem=rsem,
            device_id=peer,
            device_id_type=MESH,
        )
        copy.start()
        started.append(copy)
        return copy

    state = {}

    def core_send(c):
        s, j = chunks[c]
        src = sources[s].at[j, :, 1 - core]
        return send(src, got_core.at[c], send_sems.at[c, 0], recv_sems.at[c, 0], dp_peer(1))

    def core_load(c):
        s, j = chunks[c]
        copy = pltpu.make_async_copy(
            sources[s].at[j, :, core], mine.at[c % 2], load_sems.at[c % 2]
        )
        copy.start()
        return copy

    def core_add(c):
        core_copies[c].wait_recv()
        load_copies[c].wait()
        slot = c % levels
        if c >= levels:
            for copy in state.pop(("busy", c - levels)):
                copy.wait_send()
                started[:] = [one for one in started if one is not copy]

        def body(e, carry):
            a = mine[c % 2, e].astype(F32) + got_core[c, e].astype(F32)
            work[slot, e] = a.astype(BF16)
            return carry

        lax.fori_loop(0, chips, body, 0)
        if c + 2 < len(chunks):
            load_copies[c + 2] = core_load(c + 2)
        state[("busy", c)] = []
        chip_step(c, 0)

    def chip_step(c, level):
        slot = 1 + 2 * ((chips - (chips >> level)))
        base = 2 * (chips - (chips >> level))
        copies = []
        for side, order in enumerate(orders):
            rest = [0]
            for bit in order[level + 1 :]:
                rest += [e ^ bit for e in rest]
            for e in rest:
                far = flip(chip, order[level] ^ e)
                copies.append(
                    send(
                        work.at[c % levels, far, pl.ds(side * half, half)],
                        got_chip.at[c, base + len(copies)],
                        send_sems.at[c, slot + len(copies)],
                        recv_sems.at[c, slot + len(copies)],
                        dp_peer(2 * order[level]),
                    )
                )
        state[("busy", c)] += copies
        state[(c, level)] = copies

    def chip_add(c, level):
        base = 2 * (chips - (chips >> level))
        at = 0
        for copy in state[(c, level)]:
            copy.wait_recv()
        last = level == len(chip_bits) - 1
        s, j = chunks[c]
        for side, order in enumerate(orders):
            rest = [0]
            for bit in order[level + 1 :]:
                rest += [e ^ bit for e in rest]
            span = pl.ds(side * half, half)
            for e in rest:
                near = flip(chip, e)
                a = work[c % levels, near, span].astype(F32) + got_chip[c, base + at].astype(F32)
                at += 1
                if last:
                    final[c, span] = a.astype(BF16)
                else:
                    work[c % levels, near, span] = a.astype(BF16)
        if last:
            if j:
                state[("z", s, j)] = send(
                    final.at[c],
                    got_z.at[s, j - 1],
                    z_send.at[s, j - 1],
                    z_recv.at[s, j - 1],
                    t_peer(j),
                )
        else:
            chip_step(c, level + 1)

    def finish(s):
        c = chunks.index((s, 0))
        a = final[c].astype(F32)
        for j in range(1, nt):
            state[("z", s, j)].wait_recv()
            a = a + got_z[s, j - 1].astype(F32)
        out_ref[target[s]] = a

    sum_peers = [dp_peer(1 << b) for b in range(bits)] + [t_peer(1 << b) for b in range(tbits)]
    sum_copies = {}

    def sum_start(i):
        sum_copies[i] = send(
            total.at[i], got_sum.at[i], sum_send.at[i], sum_recv.at[i], sum_peers[i]
        )

    def sum_finish(i):
        sum_copies[i].wait_recv()
        total[i + 1] = total[i] + got_sum[i]

    total[0] = sums_ref[...]
    core_copies = [core_send(c) for c in range(len(chunks))]
    load_copies = {c: core_load(c) for c in range(2)}
    ticks = len(chunks) + levels
    for tick in range(ticks + 1):
        if tick < len(sum_peers):
            sum_start(tick)
        for stage in range(levels, -1, -1):
            c = tick - stage
            if 0 <= c < len(chunks):
                if stage == 0:
                    core_add(c)
                else:
                    chip_add(c, stage - 1)
        if tick < len(sum_peers):
            sum_finish(tick)
        c = tick - levels - 1
        if 0 <= c < len(chunks) and chunks[c][1] == 0:
            finish(chunks[c][0])
    norm_ref[...] = total[len(sum_peers)]
    for copy in started:
        copy.wait_send()


def reduce_grads(dws, dwc, dwi, dwo, sums, ndp, nt):
    dim, width = dws.shape[1:]
    rows, chips = dim // ndp, ndp // 2
    levels = chips.bit_length() - 1
    count = 4 * nt
    steps = (ndp.bit_length() - 1) + (nt.bit_length() - 1)
    view = (nt, chips, 2, rows, width)
    any_space = pl.BlockSpec(memory_space=pl.ANY)
    vmem = pl.BlockSpec(memory_space=pltpu.VMEM)
    slots = 1 + 2 * (chips - 1)
    return pl.pallas_call(
        functools.partial(reduce_kernel, ndp, nt),
        in_specs=[any_space] * 4 + [vmem],
        out_specs=[vmem, vmem],
        out_shape=[
            jax.ShapeDtypeStruct((4, rows, width), F32),
            jax.ShapeDtypeStruct(sums.shape, F32),
        ],
        scratch_shapes=[
            pltpu.VMEM((count, chips, rows, width), BF16),
            pltpu.VMEM((count, 2 * (chips - 1), rows // 2, width), BF16),
            pltpu.VMEM((4, nt - 1, rows, width), BF16),
            pltpu.VMEM((steps,) + sums.shape, F32),
            pltpu.VMEM((2, chips, rows, width), BF16),
            pltpu.VMEM((levels, chips, rows, width), BF16),
            pltpu.VMEM((count, rows, width), BF16),
            pltpu.VMEM((steps + 1,) + sums.shape, F32),
            pltpu.SemaphoreType.DMA((2,)),
            pltpu.SemaphoreType.DMA((count, slots)),
            pltpu.SemaphoreType.DMA((count, slots)),
            pltpu.SemaphoreType.DMA((4, nt - 1)),
            pltpu.SemaphoreType.DMA((4, nt - 1)),
            pltpu.SemaphoreType.DMA((steps,)),
            pltpu.SemaphoreType.DMA((steps,)),
        ],
        compiler_params=pltpu.CompilerParams(
            collective_id=1, has_side_effects=True, vmem_limit_bytes=VMEM_LIMIT
        ),
        name="reduce_grads",
    )(dws.reshape(view), dwc.reshape(view), dwi.reshape(view), dwo.reshape(view), sums)


def select_rows(lookup, positions):
    matches = positions[:, None] == jnp.arange(lookup.shape[0], dtype=jnp.int32)[None, :]
    return jnp.sum(jnp.where(matches, lookup[None, :], 0), axis=1)


def route_rows(selector, value_entries):
    return jnp.einsum(
        "kj,jrd->krd", selector, value_entries, preferred_element_type=F32
    ).astype(BF16)


def swap_dp(selector_out, selector_in, a):
    sent = lax.all_to_all(
        route_rows(selector_out, a), "dp", split_axis=0, concat_axis=0, tiled=True
    )
    return route_rows(selector_in, sent)


def to_positions(a):
    return lax.all_to_all(a, "tensor", split_axis=1, concat_axis=0, tiled=True)


def per_device(
    ndp,
    nt,
    tokens,
    enc_states,
    cotangent,
    tok_len,
    enc_len,
    deal,
    w_q_self,
    w_k_self,
    w_v_self,
    w_o_self,
    w_q_cross,
    w_k_cross,
    w_v_cross,
    w_o_cross,
    w_in,
    w_out,
    gain,
    bias,
):
    d = lax.axis_index("dp")
    t = lax.axis_index("tensor")
    seqs, _, dim = tokens.shape
    spd = seqs // nt
    hc = w_q_self.shape[1]
    slots = d * seqs + jnp.arange(seqs, dtype=jnp.int32)
    sources = select_rows(deal, slots)
    every = jnp.arange(deal.shape[0], dtype=jnp.int32)
    targets = jnp.sum(jnp.where(deal[None, :] == slots[:, None], every[None, :], 0), axis=1)
    peers = jnp.arange(ndp, dtype=jnp.int32)
    outward = (targets[None, :] // seqs == peers[:, None]).astype(BF16)
    inward = (sources[:, None] // seqs == peers[None, :]).astype(BF16)
    tok_lens = lax.dynamic_slice(select_rows(tok_len, sources), (t * spd,), (spd,))
    enc_lens = lax.dynamic_slice(select_rows(enc_len, sources), (t * spd,), (spd,))

    weights = (
        w_q_self,
        w_k_self,
        w_v_self,
        w_o_self,
        w_q_cross,
        w_k_cross,
        w_v_cross,
        w_o_cross,
        w_in,
        w_out,
    )
    wg, x, ed, cot, n1, q1, k1, v1, o1, h1, n2, q2, k2, v2, o2, h2 = front(
        ndp,
        nt,
        spd,
        tok_lens,
        enc_lens,
        sources // seqs,
        route_rows(outward, tokens),
        route_rows(outward, enc_states),
        cotangent,
        weights,
        gain,
        bias,
    )
    x, ed, cot = x.reshape(-1, dim), ed.reshape(-1, dim), cot.reshape(-1, dim)
    res, dh2, sums3, dwi, dwo = feed(tok_lens, h2, cot, gain, bias, wg, spd, nt)
    ded, dh1, sums2, dwc = cross_bwd(
        enc_lens, dh2, h1, n2, ed, gain, q2, k2, v2, o2, wg, spd, nt
    )
    dx, sums1, dws = self_bwd(tok_lens, dh1, x, n1, gain, q1, k1, v1, o1, wg, spd, nt)

    sums = jnp.concatenate(
        [sums1[:1], sums2[:1], sums3[:1], sums1[1:], sums2[1:], sums3[1:], jnp.zeros((2, dim), F32)]
    )
    grads, norm = reduce_grads(dws, dwc, dwi, dwo, sums, ndp, nt)

    def back(a):
        return swap_dp(inward.T, outward.T, to_positions(a.reshape(spd, -1, dim)))

    def attention(g):
        return (g[:, :hc], g[:, hc : 2 * hc], g[:, 2 * hc : 3 * hc], g[:, 3 * hc :].T)

    return (
        to_positions(res.reshape(spd, -1, dim)),
        back(dx),
        back(ded),
        *attention(grads[0]),
        *attention(grads[1]),
        grads[2],
        grads[3].T,
        norm[0:3],
        norm[3:6],
    )


def solution(mesh):
    ndp, nt = mesh.shape["dp"], mesh.shape["tensor"]
    rows = P("dp", "tensor", None)
    columns = P(None, "tensor")
    split = P("tensor", None)
    grad = P("dp", "tensor")
    turned = P("tensor", "dp")
    return jax.shard_map(
        functools.partial(per_device, ndp, nt),
        mesh=mesh,
        in_specs=(
            (rows,) * 3
            + (P(),) * 3
            + (columns, columns, columns, split) * 2
            + (columns, split, P(), P())
        ),
        out_specs=(
            (rows,) * 3 + (grad, grad, grad, turned) * 2 + (grad, turned) + (P(), P())
        ),
        check_vma=False,
    )
```

```python
import functools

import jax
import jax.numpy as jnp
from jax import lax
from jax.experimental import pallas as pl
from jax.experimental.pallas import tpu as pltpu
from jax.sharding import PartitionSpec as P

HEAD_DIM = 64
SCALE = 0.125
MASKED = -1e30
EPSILON = 1e-05
MESH = pl.DeviceIdType.MESH
VMEM_LIMIT = 60 * 1024 * 1024
BF16 = jnp.bfloat16
F32 = jnp.float32


def dot_nn(a, b):
    return lax.dot_general(a, b, (((1,), (0,)), ((), ())), preferred_element_type=F32)


def dot_nt(a, b):
    return lax.dot_general(a, b, (((1,), (1,)), ((), ())), preferred_element_type=F32)


def dot_tn(a, b):
    return lax.dot_general(a, b, (((0,), (0,)), ((), ())), preferred_element_type=F32)


def norm_parts(v):
    mu = jnp.mean(v, axis=-1, keepdims=True)
    var = jnp.mean(v * v, axis=-1, keepdims=True) - mu * mu
    rstd = lax.rsqrt(var + EPSILON)
    return (v - mu) * rstd, rstd


def norm_back(dn, nh, rstd, gain):
    c = dn * gain
    return rstd * (
        c - jnp.mean(c, axis=-1, keepdims=True) - nh * jnp.mean(c * nh, axis=-1, keepdims=True)
    )


def head_stack(a, heads):
    lane = lax.broadcasted_iota(jnp.int32, a.shape, 1) // HEAD_DIM
    zero = jnp.zeros_like(a)
    return jnp.concatenate([jnp.where(lane == h, a, zero) for h in range(heads)], axis=0)


def attn_probs(q, k, limit, causal):
    heads = q.shape[1] // HEAD_DIM
    qs = head_stack(q, heads)
    s = dot_nt(qs, k) * SCALE
    key = lax.broadcasted_iota(jnp.int32, s.shape, 1)
    allowed = key < limit
    if causal:
        row = lax.rem(lax.broadcasted_iota(jnp.int32, s.shape, 0), q.shape[0])
        allowed = allowed & (key <= row)
    s = jnp.where(allowed, s, MASKED)
    e = jnp.exp(s - jnp.max(s, axis=-1, keepdims=True))
    return qs, e / jnp.sum(e, axis=-1, keepdims=True)


def lane_stack(a, heads):
    rows = a.shape[0] // heads
    return jnp.concatenate([a[h * rows : (h + 1) * rows] for h in range(heads)], axis=1)


def attn_fwd(q, k, v, limit, causal):
    heads = q.shape[1] // HEAD_DIM
    _, p = attn_probs(q, k, limit, causal)
    return dot_nn(lane_stack(p.astype(BF16), heads), head_stack(v, heads)).astype(BF16)


def attn_bwd(q, k, v, do, limit, causal):
    heads = q.shape[1] // HEAD_DIM
    qs, p = attn_probs(q, k, limit, causal)
    dos = head_stack(do, heads)
    dp = dot_nt(dos, v)
    delta = jnp.sum(p * dp, axis=-1, keepdims=True)
    ds = (p * (dp - delta) * SCALE).astype(BF16)
    dq = dot_nn(lane_stack(ds, heads), head_stack(k, heads)).astype(BF16)
    dk = dot_tn(ds, qs).astype(BF16)
    dv = dot_tn(p.astype(BF16), dos).astype(BF16)
    return dq, dk, dv


def row_valid(lens, spd, n):
    row = lax.broadcasted_iota(jnp.int32, (n, 1), 0)
    seq = n // spd
    end = jnp.full((n, 1), lens[0], jnp.int32)
    for i in range(1, spd):
        end = jnp.where(row >= i * seq, i * seq + lens[i], end)
    return row < end


def flip(index, mask):
    out = index
    bit = 1
    while bit <= mask:
        if mask & bit:
            out = out + bit - 2 * bit * lax.rem(lax.div(index, bit), 2)
        bit *= 2
    return out


def xor_of(a, b, size):
    out = 0
    bit = 1
    while bit < size:
        out = out + bit * lax.rem(lax.div(a, bit) + lax.div(b, bit), 2)
        bit *= 2
    return out


def greet(peers):
    barrier = pltpu.get_barrier_semaphore()
    for peer in peers:
        pl.semaphore_signal(barrier, inc=1, device_id=peer, device_id_type=MESH)
    pl.semaphore_wait(barrier, len(peers))


def front_kernel(
    ndp,
    nt,
    spd,
    tok_lens,
    enc_lens,
    in_peer,
    tok_blocks,
    enc_blocks,
    cot_ref,
    w_refs,
    gain,
    bias,
    wg,
    x_ref,
    ed_ref,
    cots_ref,
    n1_ref,
    q1_ref,
    k1_ref,
    v1_ref,
    o1_ref,
    h1_ref,
    n2_ref,
    q2_ref,
    k2_ref,
    v2_ref,
    o2_ref,
    h2_ref,
    rx_tok,
    rx_enc,
    zs_tok,
    zs_enc,
    own,
    raw_o,
    raw_out,
    wbuf,
    load_sems,
    own_sem,
    wbuf_sems,
    tok_send,
    tok_recv,
    enc_send,
    enc_recv,
    zt_send,
    zt_recv,
    ze_send,
    ze_recv,
    zc_send,
    zc_recv,
    line_send,
    pass_send,
    send_sems,
    recv_sems,
):
    d = lax.axis_index("dp")
    t = lax.axis_index("tensor")
    dim, width = own.shape[1:]
    hc = width // 4
    rows_each = dim // ndp
    half = rows_each // 2
    bits = ndp.bit_length() - 1
    chip_bits = [1 << b for b in range(1, bits)]
    orders = (chip_bits, chip_bits[::-1])
    levels = len(chip_bits)
    seqs, lr = cot_ref.shape[0], cot_ref.shape[1]
    le = enc_blocks.shape[1]
    seq, enc = nt * lr, nt * le
    n, m = spd * seq, spd * enc
    waits = []

    def dp_peer(bit):
        return (flip(d, bit), t)

    def t_peer(j):
        return (d, flip(t, j))

    def slab(index, side=None):
        if side is None:
            return pl.ds(pl.multiple_of(index * rows_each, rows_each), rows_each)
        return pl.ds(pl.multiple_of(index * rows_each + side * half, half), half)

    def remote(src, dst, ssem, rsem, peer):
        return pltpu.make_async_remote_copy(
            src_ref=src,
            dst_ref=dst,
            send_sem=ssem,
            recv_sem=rsem,
            device_id=peer,
            device_id_type=MESH,
        )

    def send(*args):
        copy = remote(*args)
        copy.start()
        waits.append(copy)
        return copy

    def local(src, dst, sem):
        copy = pltpu.make_async_copy(src, dst, sem)
        copy.start()
        return copy

    greet([dp_peer(e) for e in range(1, ndp)] + [t_peer(j) for j in range(1, nt)])

    def to_peers(blocks, rx, ssem, rsem):
        return [
            send(blocks.at[flip(d, e)], rx.at[d], ssem.at[e], rsem.at[e], dp_peer(e))
            for e in range(1, ndp)
        ], local(blocks.at[d], rx.at[d], rsem.at[0])

    tok_copies, tok_own = to_peers(tok_blocks, rx_tok, tok_send, tok_recv)

    wq1, wk1, wv1, wo1, wq2, wk2, wv2, wo2, w_in, w_out = w_refs
    loads = [
        local(src, dst, load_sems.at[i])
        for i, (src, dst) in enumerate(
            [
                (wo1, raw_o.at[0]),
                (wq1, own.at[0, :, pl.ds(0, hc)]),
                (wk1, own.at[0, :, pl.ds(hc, hc)]),
                (wv1, own.at[0, :, pl.ds(2 * hc, hc)]),
                (wo2, raw_o.at[1]),
                (wq2, own.at[1, :, pl.ds(0, hc)]),
                (wk2, own.at[1, :, pl.ds(hc, hc)]),
                (wv2, own.at[1, :, pl.ds(2 * hc, hc)]),
                (w_in, own.at[2]),
                (w_out, raw_out),
            ]
        )
    ]

    chunks = [(g, j) for g in range(4) for j in range(1, nt)]

    def line_copy(g, step):
        there = t + step
        j = xor_of(t, there, nt)
        return remote(
            own.at[g, slab(d)],
            wg.at[j, g, slab(d)],
            line_send.at[g, (step + 1) // 2],
            recv_sems.at[g * (nt - 1) + j - 1, 0],
            (d, there),
        )

    def pass_copy(c, step):
        g, j = chunks[c]
        there = t + step
        j_there = xor_of(flip(t, j), there, nt)
        return remote(
            wg.at[j, g, slab(d)],
            wg.at[j_there, g, slab(d)],
            pass_send.at[c],
            recv_sems.at[g * (nt - 1) + j_there - 1, 0],
            (d, there),
        )

    def on_line(act, g):
        @pl.when(t + 1 < nt)
        def _():
            act(line_copy(g, 1))

        @pl.when(t >= 1)
        def _():
            act(line_copy(g, -1))

    def on_pass(act, c):
        s = flip(t, chunks[c][1])

        @pl.when((s < t) & (t + 1 < nt))
        def _():
            act(pass_copy(c, 1))

        @pl.when((s > t) & (t >= 1))
        def _():
            act(pass_copy(c, -1))

    def start(copy):
        copy.start()

    def arrived(c):
        g, j = chunks[c]
        at = wg.at[j, g, slab(d)]
        remote(at, at, pass_send.at[c], recv_sems.at[c, 0], t_peer(j)).wait_recv()
        on_pass(start, c)

    pending = {}

    def spread(c, level):
        g, j = chunks[c]
        if level == 0:
            arrived(c)
        else:
            for copy in pending.pop((c, level)):
                copy.wait_recv()
        slot = 1 + 2 * ((1 << level) - 1)
        copies = []
        if level < levels:
            for side, order in enumerate(orders):
                held = [0]
                for bit in order[:level]:
                    held += [e ^ bit for e in held]
                for e in held:
                    at = wg.at[j, g, slab(flip(d, e), side)]
                    copies.append(
                        send(
                            at,
                            at,
                            send_sems.at[c, slot],
                            recv_sems.at[c, slot],
                            dp_peer(order[level]),
                        )
                    )
                    slot += 1
        elif level == levels:
            for e in range(0, ndp, 2):
                at = wg.at[j, g, slab(flip(d, e))]
                copies.append(
                    send(at, at, send_sems.at[c, slot], recv_sems.at[c, slot], dp_peer(1))
                )
                slot += 1
        elif g < 2:
            fills[c] = local(wg.at[j, g], wbuf.at[c % 2], wbuf_sems.at[c % 2])
        if copies:
            pending[(c, level + 1)] = copies

    fills = {}

    def to_sequences(src, dst, rows, ssem, rsem):
        for j in range(1, nt):
            there = flip(t, j)
            send(
                src.at[pl.ds(there * spd, spd)],
                dst.at[:, pl.ds(pl.multiple_of(t * rows, rows), rows)],
                ssem.at[j],
                rsem.at[j],
                t_peer(j),
            )
        return local(
            src.at[pl.ds(t * spd, spd)],
            dst.at[:, pl.ds(pl.multiple_of(t * rows, rows), rows)],
            rsem.at[0],
        )

    def sequences_here(own_copy, src, dst, rows, ssem, rsem):
        own_copy.wait()
        for j in range(1, nt):
            there = flip(t, j)
            remote(
                src.at[pl.ds(t * spd, spd)],
                dst.at[:, pl.ds(pl.multiple_of(there * rows, rows), rows)],
                ssem.at[j],
                rsem.at[j],
                t_peer(j),
            ).wait_recv()

    def blocks_here(copies, own_copy, rx, zs):
        own_copy.wait()
        for copy in copies:
            copy.wait_recv()
        for i in range(seqs):
            zs[i] = rx[in_peer[i]]

    def self_norm():
        x = x_ref[...].reshape(n, dim).astype(F32)
        nh, _ = norm_parts(x)
        n1_ref[...] = (nh * gain[0:1] + bias[0:1]).astype(BF16)
        h1_ref[...] = x

    def self_part(j, w):
        qkv = dot_nn(n1_ref[...], w[:, : 3 * hc]).astype(BF16)
        q1_ref[j] = qkv[:, :hc]
        k1_ref[j] = qkv[:, hc : 2 * hc]
        v1_ref[j] = qkv[:, 2 * hc :]
        for i in range(spd):
            rows = slice(i * seq, (i + 1) * seq)
            o1_ref[j, rows] = attn_fwd(
                q1_ref[j, rows], k1_ref[j, rows], v1_ref[j, rows], tok_lens[i], True
            )
        h1_ref[...] += dot_nt(o1_ref[j], w[:, 3 * hc :])

    def cross_norm():
        h = h1_ref[...]
        nh, _ = norm_parts(h)
        n2_ref[...] = (nh * gain[1:2] + bias[1:2]).astype(BF16)
        h2_ref[...] = h

    def cross_part(j, w):
        q2_ref[j] = dot_nn(n2_ref[...], w[:, :hc]).astype(BF16)
        kv = dot_nn(ed_ref[...].reshape(m, dim), w[:, hc : 3 * hc]).astype(BF16)
        k2_ref[j] = kv[:, :hc]
        v2_ref[j] = kv[:, hc:]
        for i in range(spd):
            rows = slice(i * seq, (i + 1) * seq)
            keys = slice(i * enc, (i + 1) * enc)
            o2_ref[j, rows] = attn_fwd(
                q2_ref[j, rows], k2_ref[j, keys], v2_ref[j, keys], enc_lens[i], False
            )
        h2_ref[...] += dot_nt(o2_ref[j], w[:, 3 * hc :])

    for i in range(4):
        loads[i].wait()
    own[0, :, 3 * hc :] = raw_o[0].T
    on_line(start, 0)
    blocks_here(tok_copies, tok_own, rx_tok, zs_tok)
    own_x = to_sequences(zs_tok, x_ref, lr, zt_send, zt_recv)
    enc_copies, enc_own = to_peers(enc_blocks, rx_enc, enc_send, enc_recv)
    for i in range(4, 10):
        loads[i].wait()
    own[1, :, 3 * hc :] = raw_o[1].T
    block = min(256, width)
    for at in range(0, width, block):
        own[3, :, at : at + block] = raw_out[at : at + block].T
    own_copy = local(own, wg.at[0], own_sem)

    state = {}
    ready = levels + 1
    count = len(chunks)
    per = nt - 1
    for tick in range(count + ready):
        for level in range(ready + 1):
            c = tick - level
            if 0 <= c < count:
                spread(c, level)
                if level == 0 and c % per == 0 and c // per + 1 < 4:
                    on_line(start, c // per + 1)
        if tick == 0:
            blocks_here(enc_copies, enc_own, rx_enc, zs_enc)
            own_ed = to_sequences(zs_enc, ed_ref, le, ze_send, ze_recv)
        if tick == 2:
            sequences_here(own_x, zs_tok, x_ref, lr, zt_send, zt_recv)
            self_norm()
            self_part(0, own.at[0])
        c = tick - ready - 1
        if 0 <= c < 2 * per:
            g, j = chunks[c]
            fills[c].wait()
            (self_part if g == 0 else cross_part)(j, wbuf.at[c % 2])
            if c == per - 1:
                sequences_here(own_ed, zs_enc, ed_ref, le, ze_send, ze_recv)
                own_cot = to_sequences(cot_ref, cots_ref, lr, zc_send, zc_recv)
                cross_norm()
                cross_part(0, own.at[1])

    sequences_here(own_cot, cot_ref, cots_ref, lr, zc_send, zc_recv)
    own_copy.wait()
    for g in range(4):
        on_line(lambda copy: copy.wait_send(), g)
    for c in range(count):
        on_pass(lambda copy: copy.wait_send(), c)
    for copy in waits:
        copy.wait_send()


def front(ndp, nt, spd, tok_lens, enc_lens, in_peer, tok_blocks, enc_blocks, cot, weights, gain, bias):
    seqs, lr, dim = cot.shape
    le = enc_blocks.shape[1]
    seq, enc = nt * lr, nt * le
    n, m = spd * seq, spd * enc
    hc = weights[0].shape[1]
    width = 4 * hc
    count = 4 * (nt - 1)
    slots = 1 + 2 * (ndp // 2 - 1) + ndp // 2
    smem = pl.BlockSpec(memory_space=pltpu.SMEM)
    vmem = pl.BlockSpec(memory_space=pltpu.VMEM)
    any_space = pl.BlockSpec(memory_space=pl.ANY)
    dma = pltpu.SemaphoreType.DMA
    shape = jax.ShapeDtypeStruct
    part, keys = shape((nt, n, hc), BF16), shape((nt, m, hc), BF16)

    def body(*refs):
        front_kernel(ndp, nt, spd, *refs[:6], refs[6:16], *refs[16:])

    return pl.pallas_call(
        body,
        in_specs=[smem] * 3 + [any_space] * 13 + [vmem] * 2,
        out_specs=[any_space, vmem, vmem, any_space] + [vmem] * 12,
        out_shape=[
            shape((nt, 4, dim, width), BF16),
            shape((spd, seq, dim), BF16),
            shape((spd, enc, dim), BF16),
            shape((spd, seq, dim), BF16),
            shape((n, dim), BF16),
            part,
            part,
            part,
            part,
            shape((n, dim), F32),
            shape((n, dim), BF16),
            part,
            keys,
            keys,
            part,
            shape((n, dim), F32),
        ],
        scratch_shapes=[
            pltpu.VMEM((ndp, lr, dim), BF16),
            pltpu.VMEM((ndp, le, dim), BF16),
            pltpu.VMEM((seqs, lr, dim), BF16),
            pltpu.VMEM((seqs, le, dim), BF16),
            pltpu.VMEM((4, dim, width), BF16),
            pltpu.VMEM((2, hc, dim), BF16),
            pltpu.VMEM((width, dim), BF16),
            pltpu.VMEM((2, dim, width), BF16),
            dma((10,)),
            dma,
            dma((2,)),
            dma((ndp,)),
            dma((ndp,)),
            dma((ndp,)),
            dma((ndp,)),
            dma((nt,)),
            dma((nt,)),
            dma((nt,)),
            dma((nt,)),
            dma((nt,)),
            dma((nt,)),
            dma((4, 2)),
            dma((count,)),
            dma((count, slots)),
            dma((count, slots)),
        ],
        compiler_params=pltpu.CompilerParams(
            collective_id=0, has_side_effects=True, vmem_limit_bytes=VMEM_LIMIT
        ),
        name="front",
    )(tok_lens, enc_lens, in_peer, tok_blocks, enc_blocks, cot, *weights, gain, bias)


CORE_SLOTS = 4
CHIP_SLOTS = 4
DW_SLOTS = 3
Z_SLOTS = 4
SPACING = 2


def back_kernel(
    ndp,
    nt,
    spd,
    tok_lens,
    enc_lens,
    back_slot,
    wg,
    x_hbm,
    ed_hbm,
    cot_hbm,
    n1_hbm,
    q1_hbm,
    k1_hbm,
    v1_hbm,
    o1_hbm,
    h1_hbm,
    n2_hbm,
    q2_hbm,
    k2_hbm,
    v2_hbm,
    o2_hbm,
    h2_hbm,
    gain,
    res_out,
    rx_tok,
    rx_enc,
    grad_ref,
    norm_ref,
    h2_ref,
    cot_ref,
    h1_ref,
    n2_ref,
    ed_ref,
    q2_ref,
    k2_ref,
    v2_ref,
    o2_ref,
    x_ref,
    n1_ref,
    q1_ref,
    k1_ref,
    v1_ref,
    o1_ref,
    low,
    low_t,
    grad_low,
    grad_low_t,
    edt,
    out_acc,
    dn_acc,
    ded_acc,
    dh_ref,
    res_ref,
    dx_ref,
    ded_ref,
    dq,
    dk,
    dv,
    panels,
    zrx_tok,
    zrx_enc,
    sb_tok,
    sb_enc,
    dw,
    got_core,
    got_chip,
    got_z,
    work,
    final,
    total,
    got_sum,
    load_sems,
    panel_sems,
    send_sems,
    recv_sems,
    z_send,
    z_recv,
    sum_send,
    sum_recv,
    zr_send,
    zr_recv,
    zt_send,
    zt_recv,
    ze_send,
    ze_recv,
    tok_send,
    tok_recv,
    enc_send,
    enc_recv,
    core_credit,
    chip_credit,
):
    d = lax.axis_index("dp")
    t = lax.axis_index("tensor")
    bits = ndp.bit_length() - 1
    tbits = nt.bit_length() - 1
    chips = ndp // 2
    rows_each, width = grad_ref.shape[1], grad_ref.shape[2]
    dim = wg.shape[2]
    hc = width // 4
    half = rows_each // 2
    core = lax.rem(d, 2)
    chip = lax.div(d, 2)
    chip_bits = [1 << b for b in range(bits - 1)]
    orders = (chip_bits, chip_bits[::-1])
    levels = len(chip_bits)
    work_slots = work.shape[0]
    seqs, lr = res_out.shape[0], res_out.shape[1]
    le = rx_enc.shape[1]
    seq, enc = nt * lr, nt * le
    n, m = spd * seq, spd * enc
    started = []

    def dp_peer(bit):
        return (flip(d, bit), t)

    def t_peer(j):
        return (d, flip(t, j))

    def remote(src, dst, ssem, rsem, peer):
        return pltpu.make_async_remote_copy(
            src_ref=src,
            dst_ref=dst,
            send_sem=ssem,
            recv_sem=rsem,
            device_id=peer,
            device_id_type=MESH,
        )

    def send(*args):
        copy = remote(*args)
        copy.start()
        started.append(copy)
        return copy

    def sent(copy):
        copy.wait_send()
        started[:] = [one for one in started if one is not copy]

    def local(src, dst, sem):
        copy = pltpu.make_async_copy(src, dst, sem)
        copy.start()
        return copy

    loads = [
        local(src, dst, load_sems.at[i])
        for i, (src, dst) in enumerate(
            [
                (h2_hbm, h2_ref),
                (cot_hbm, cot_ref),
                (n2_hbm, n2_ref),
                (ed_hbm, ed_ref),
                (q2_hbm, q2_ref),
                (k2_hbm, k2_ref),
                (v2_hbm, v2_ref),
                (o2_hbm, o2_ref),
                (h1_hbm, h1_ref),
                (n1_hbm, n1_ref),
                (q1_hbm, q1_ref),
                (k1_hbm, k1_ref),
                (v1_hbm, v1_ref),
                (o1_hbm, o1_ref),
                (x_hbm, x_ref),
            ]
        )
    ]

    def loaded(first, last):
        for i in range(first, last):
            loads[i].wait()

    shards = list(range(1, nt)) + [0]
    units = [("feed", j) for j in shards] + [("cross", j) for j in shards]
    units += [("self", j) for j in shards]
    made = {"feed": (3, 2), "cross": (1,), "self": (0,)}
    chunks = []
    unit_at = {}
    for u, (kind, j) in enumerate(units):
        unit_at[len(chunks)] = u
        chunks += [(g, j) for g in made[kind]]
    count = len(chunks)
    fetched = {}

    def fetch(u):
        if u < len(units):
            kind, j = units[u]
            fetched[u] = [
                local(wg.at[j, g], panels.at[2 * (u % 2) + i], panel_sems.at[2 * (u % 2) + i])
                for i, g in enumerate(made[kind])
            ]

    fetch(0)
    greet([dp_peer(e) for e in range(1, ndp)] + [t_peer(j) for j in range(1, nt)])

    def put(c, column, a, b):
        cols = b.shape[1]
        for e in range(chips):
            part = dot_nn(a[2 * e * rows_each : 2 * (e + 1) * rows_each], b)
            dw[c % DW_SLOTS, e, :, :, column : column + cols] = part.astype(BF16).reshape(
                2, rows_each, cols
            )

    def feed_init():
        loaded(0, 2)
        nh, _ = norm_parts(h2_ref[...])
        v = nh * gain[2:3] + gain[5:6]
        low[...] = v.astype(BF16)
        low_t[...] = v.T.astype(BF16)
        keep = row_valid(tok_lens, spd, n)
        dh = jnp.where(keep, cot_ref[...].reshape(n, dim).astype(F32), 0.0)
        grad_low[...] = dh.astype(BF16)
        grad_low_t[...] = dh.T.astype(BF16)
        out_acc[...] = jnp.zeros_like(out_acc)
        dn_acc[...] = jnp.zeros_like(dn_acc)

    def feed_part(c, wout_ref, win_ref):
        block = min(512, width)
        for at in range(0, width, block):
            win = win_ref[:, at : at + block]
            wout = wout_ref[:, at : at + block]
            u = dot_nn(low[...], win)
            ga = dot_nn(grad_low[...], wout)
            sg = 1.0 / (1.0 + jnp.exp(-u))
            r = (u * sg).astype(BF16)
            du = (ga * (sg * (1.0 + u * (1.0 - sg)))).astype(BF16)
            out_acc[...] += dot_nt(r, wout)
            dn_acc[...] += dot_nt(du, win)
            put(c, at, grad_low_t, r)
            put(c + 1, at, low_t, du)

    def norm_grads(row, v, gain_row):
        nh, rstd = norm_parts(v)
        dn = dn_acc[...]
        total[0, row : row + 1] = jnp.sum(dn * nh, axis=0, keepdims=True)
        total[0, 3 + row : 4 + row] = jnp.sum(dn, axis=0, keepdims=True)
        return norm_back(dn, nh, rstd, gain_row)

    def feed_end():
        keep = row_valid(tok_lens, spd, n)
        h2 = h2_ref[...]
        res = jnp.where(keep, h2 + out_acc[...], 0.0).astype(BF16)
        res_ref[...] = res.reshape(spd, seq, dim)
        dh = jnp.where(keep, cot_ref[...].reshape(n, dim).astype(F32), 0.0)
        dh_ref[...] = dh + norm_grads(2, h2, gain[2:3])

    def branch_init(kept):
        dh = dh_ref[...]
        grad_low[...] = dh.astype(BF16)
        grad_low_t[...] = dh.T.astype(BF16)
        low_t[...] = kept[...].T
        dn_acc[...] = jnp.zeros_like(dn_acc)

    def cross_init():
        loaded(2, 9)
        branch_init(n2_ref)
        edt[...] = ed_ref[...].reshape(m, dim).T
        ded_acc[...] = jnp.zeros_like(ded_acc)

    def cross_part(c, j, w):
        do = dot_nn(grad_low[...], w[:, 3 * hc :]).astype(BF16)
        for i in range(spd):
            rows = slice(i * seq, (i + 1) * seq)
            keys = slice(i * enc, (i + 1) * enc)
            dq[rows, :hc], dk[keys], dv[keys] = attn_bwd(
                q2_ref[j, rows], k2_ref[j, keys], v2_ref[j, keys], do[rows], enc_lens[i], False
            )
        dn_acc[...] += dot_nt(dq[:, :hc], w[:, :hc])
        ded_acc[...] += dot_nt(dk[...], w[:, hc : 2 * hc]) + dot_nt(dv[...], w[:, 2 * hc : 3 * hc])
        put(c, 0, low_t, dq[:, :hc])
        put(c, hc, edt, dk[...])
        put(c, 2 * hc, edt, dv[...])
        put(c, 3 * hc, grad_low_t, o2_ref[j])

    def cross_end():
        ded_ref[...] = ded_acc[...].astype(BF16).reshape(spd, enc, dim)
        dh_ref[...] += norm_grads(1, h1_ref[...], gain[1:2])

    def self_init():
        loaded(9, 15)
        branch_init(n1_ref)

    def self_part(c, j, w):
        do = dot_nn(grad_low[...], w[:, 3 * hc :]).astype(BF16)
        for i in range(spd):
            rows = slice(i * seq, (i + 1) * seq)
            dq[rows, :hc], dq[rows, hc : 2 * hc], dq[rows, 2 * hc :] = attn_bwd(
                q1_ref[j, rows], k1_ref[j, rows], v1_ref[j, rows], do[rows], tok_lens[i], True
            )
        dn_acc[...] += dot_nt(dq[...], w[:, : 3 * hc])
        put(c, 0, low_t, dq[...])
        put(c, 3 * hc, grad_low_t, o1_ref[j])

    def self_end():
        x = x_ref[...].reshape(n, dim).astype(F32)
        dx = dh_ref[...] + norm_grads(0, x, gain[0:1])
        dx_ref[...] = dx.astype(BF16).reshape(spd, seq, dim)

    def run_unit(c):
        u = unit_at[c]
        kind, j = units[u]
        for i in range(len(made[kind])):
            if c + i >= DW_SLOTS:
                sent(core_copies[c + i - DW_SLOTS])
        for copy in fetched.pop(u):
            copy.wait()
        fetch(u + 1)
        slot = 2 * (u % 2)
        first, last = j == shards[0], j == shards[-1]
        if kind == "feed":
            if first:
                feed_init()
            feed_part(c, panels.at[slot], panels.at[slot + 1])
            if last:
                feed_end()
        elif kind == "cross":
            if first:
                cross_init()
            cross_part(c, j, panels.at[slot])
            if last:
                cross_end()
        else:
            if first:
                self_init()
            self_part(c, j, panels.at[slot])
            if last:
                self_end()

    core_copies = {}
    chip_copies = {}
    z_copies = {}

    def core_send(c):
        if c >= CORE_SLOTS:
            pl.semaphore_wait(core_credit, 1)
        core_copies[c] = send(
            dw.at[c % DW_SLOTS, :, 1 - core],
            got_core.at[c % CORE_SLOTS],
            send_sems.at[c, 0],
            recv_sems.at[c, 0],
            dp_peer(1),
        )

    def core_add(c):
        core_copies[c].wait_recv()
        if c >= work_slots:
            for level in range(levels):
                for copy in chip_copies.pop((c - work_slots, level)):
                    sent(copy)

        def body(e, carry):
            a = dw[c % DW_SLOTS, e, core] + got_core[c % CORE_SLOTS, e]
            work[c % work_slots, e] = a
            return carry

        lax.fori_loop(0, chips, body, 0)
        if c + CORE_SLOTS < count:
            pl.semaphore_signal(core_credit, inc=1, device_id=dp_peer(1), device_id_type=MESH)
        chip_send(c, 0)

    def rest_of(order, level):
        rest = [0]
        for bit in order[level + 1 :]:
            rest += [e ^ bit for e in rest]
        return rest

    def chip_send(c, level):
        base = 2 * (chips - (chips >> level))
        copies = []
        for side, order in enumerate(orders):
            if c >= CHIP_SLOTS:
                pl.semaphore_wait(chip_credit.at[level, side], 1)
            for e in rest_of(order, level):
                at = base + len(copies)
                copies.append(
                    send(
                        work.at[
                            c % work_slots,
                            flip(chip, order[level] ^ e),
                            pl.ds(side * half, half),
                        ],
                        got_chip.at[c % CHIP_SLOTS, at],
                        send_sems.at[c, 1 + at],
                        recv_sems.at[c, 1 + at],
                        dp_peer(2 * order[level]),
                    )
                )
        chip_copies[(c, level)] = copies

    def chip_add(c, level):
        at = 2 * (chips - (chips >> level))
        g, j = chunks[c]
        copies = iter(chip_copies[(c, level)])
        last = level == levels - 1
        if last and j:
            zs = (c - c // len(shards)) % Z_SLOTS
            key = [k for k, v in z_copies.items() if v[1] == zs and not v[2]]
            for k in key:
                sent(z_copies[k][0])
                z_copies[k] = (z_copies[k][0], zs, True)
        for side, order in enumerate(orders):
            span = pl.ds(side * half, half)
            for e in rest_of(order, level):
                next(copies).wait_recv()
                near = flip(chip, e)
                a = work[c % work_slots, near, span]
                b = got_chip[c % CHIP_SLOTS, at]
                at += 1
                if not last:
                    work[c % work_slots, near, span] = a + b
                elif j:
                    final[zs, span] = a + b
                else:
                    grad_ref[g, span] = a.astype(F32) + b.astype(F32)
            if c + CHIP_SLOTS < count:
                pl.semaphore_signal(
                    chip_credit.at[level, side],
                    inc=1,
                    device_id=dp_peer(2 * order[level]),
                    device_id_type=MESH,
                )
        if not last:
            chip_send(c, level + 1)
        elif j:
            copy = send(
                final.at[zs],
                got_z.at[g, j - 1],
                z_send.at[g, j - 1],
                z_recv.at[g, j - 1],
                t_peer(j),
            )
            z_copies[(g, j)] = (copy, zs, False)

    def finish(c):
        g, j = chunks[c]
        if j == 0:
            a = grad_ref[g]
            for i in range(1, nt):
                z_copies[(g, i)][0].wait_recv()
                a = a + got_z[g, i - 1].astype(F32)
            grad_ref[g] = a

    def to_positions(src, dst, rows, ssem, rsem):
        for j in range(1, nt):
            there = flip(t, j)
            send(
                src.at[:, pl.ds(pl.multiple_of(there * rows, rows), rows)],
                dst.at[pl.ds(t * spd, spd)],
                ssem.at[j],
                rsem.at[j],
                t_peer(j),
            )
        return local(
            src.at[:, pl.ds(pl.multiple_of(t * rows, rows), rows)],
            dst.at[pl.ds(t * spd, spd)],
            rsem.at[0],
        )

    def positions_here(own_copy, src, dst, rows, ssem, rsem):
        own_copy.wait()
        for j in range(1, nt):
            remote(
                src.at[:, pl.ds(pl.multiple_of(t * rows, rows), rows)],
                dst.at[pl.ds(flip(t, j) * spd, spd)],
                ssem.at[j],
                rsem.at[j],
                t_peer(j),
            ).wait_recv()

    def to_inputs(zrx, sb, rx, ssem, rsem):
        for k in range(ndp):
            sb[k] = zrx[back_slot[k]]
        copies = [
            send(sb.at[flip(d, e)], rx.at[d], ssem.at[e], rsem.at[e], dp_peer(e))
            for e in range(1, ndp)
        ]
        return copies + [local(sb.at[d], rx.at[d], rsem.at[0])]

    def inputs_here(copies):
        for copy in copies[:-1]:
            copy.wait_recv()
        copies[-1].wait()

    sum_peers = [dp_peer(1 << b) for b in range(bits)] + [t_peer(1 << b) for b in range(tbits)]
    sum_copies = {}

    def sum_start(i):
        sum_copies[i] = send(
            total.at[i], got_sum.at[i], sum_send.at[i], sum_recv.at[i], sum_peers[i]
        )

    def sum_finish(i):
        sum_copies[i].wait_recv()
        total[i + 1] = total[i] + got_sum[i]

    total[0] = jnp.zeros_like(total[0])
    depth = SPACING * (levels + 1) + 2
    feed_last = count // 2 - 2
    cross_last = 3 * count // 4 - 1
    state = {}
    for tick in range(count + max(depth, len(sum_peers) + 3)):
        c = tick - depth
        if 0 <= c < count:
            finish(c)
        for level in range(levels - 1, -1, -1):
            c = tick - SPACING * (level + 2)
            if 0 <= c < count:
                chip_add(c, level)
        c = tick - SPACING
        if 0 <= c < count:
            core_add(c)
        if tick in unit_at:
            run_unit(tick)
        if tick < count:
            core_send(tick)
        if tick == feed_last:
            state["res"] = to_positions(res_ref, res_out, lr, zr_send, zr_recv)
        if tick == cross_last:
            state["ded"] = to_positions(ded_ref, zrx_enc, le, ze_send, ze_recv)
        if tick == cross_last + 2:
            positions_here(state["ded"], ded_ref, zrx_enc, le, ze_send, ze_recv)
            state["enc"] = to_inputs(zrx_enc, sb_enc, rx_enc, enc_send, enc_recv)
        if tick == count - 1:
            state["dx"] = to_positions(dx_ref, zrx_tok, lr, zt_send, zt_recv)
        if tick == count + 1:
            positions_here(state["dx"], dx_ref, zrx_tok, lr, zt_send, zt_recv)
            state["tok"] = to_inputs(zrx_tok, sb_tok, rx_tok, tok_send, tok_recv)
        i = tick - count
        if 0 <= i - 1 < len(sum_peers):
            sum_finish(i - 1)
        if 0 <= i < len(sum_peers):
            sum_start(i)
    norm_ref[...] = total[len(sum_peers)]
    positions_here(state["res"], res_ref, res_out, lr, zr_send, zr_recv)
    inputs_here(state["enc"])
    inputs_here(state["tok"])
    for copy in started:
        copy.wait_send()


def back(ndp, nt, spd, tok_lens, enc_lens, back_slot, wg, kept, norms):
    x, ed, cot, n1, q1, k1, v1, o1, h1, n2, q2, k2, v2, o2, h2 = kept
    _, _, dim, width = wg.shape
    _, seq, _ = x.shape
    enc = ed.shape[1]
    lr, le = seq // nt, enc // nt
    seqs = spd * nt
    n, m = spd * seq, spd * enc
    hc = width // 4
    rows, chips = dim // ndp, ndp // 2
    half = rows // 2
    levels = chips.bit_length() - 1
    count = 4 * nt
    steps = (ndp.bit_length() - 1) + (nt.bit_length() - 1)
    slots = 1 + 2 * (chips - 1)
    smem = pl.BlockSpec(memory_space=pltpu.SMEM)
    vmem = pl.BlockSpec(memory_space=pltpu.VMEM)
    any_space = pl.BlockSpec(memory_space=pl.ANY)
    dma = pltpu.SemaphoreType.DMA
    shape = jax.ShapeDtypeStruct

    def like(a):
        return pltpu.VMEM(a.shape, a.dtype)

    return pl.pallas_call(
        functools.partial(back_kernel, ndp, nt, spd),
        in_specs=[smem] * 3 + [any_space] * 16 + [vmem],
        out_specs=[any_space] * 3 + [vmem] * 2,
        out_shape=[
            shape((seqs, lr, dim), BF16),
            shape((ndp, lr, dim), BF16),
            shape((ndp, le, dim), BF16),
            shape((4, rows, width), F32),
            shape((8, dim), F32),
        ],
        scratch_shapes=[
            *[like(a) for a in (h2, cot, h1, n2, ed, q2, k2, v2, o2, x, n1, q1, k1, v1, o1)],
            pltpu.VMEM((n, dim), BF16),
            pltpu.VMEM((dim, n), BF16),
            pltpu.VMEM((n, dim), BF16),
            pltpu.VMEM((dim, n), BF16),
            pltpu.VMEM((dim, m), BF16),
            pltpu.VMEM((n, dim), F32),
            pltpu.VMEM((n, dim), F32),
            pltpu.VMEM((m, dim), F32),
            pltpu.VMEM((n, dim), F32),
            pltpu.VMEM((spd, seq, dim), BF16),
            pltpu.VMEM((spd, seq, dim), BF16),
            pltpu.VMEM((spd, enc, dim), BF16),
            pltpu.VMEM((n, 3 * hc), BF16),
            pltpu.VMEM((m, hc), BF16),
            pltpu.VMEM((m, hc), BF16),
            pltpu.VMEM((4, dim, width), BF16),
            pltpu.VMEM((seqs, lr, dim), BF16),
            pltpu.VMEM((seqs, le, dim), BF16),
            pltpu.VMEM((ndp, lr, dim), BF16),
            pltpu.VMEM((ndp, le, dim), BF16),
            pltpu.VMEM((DW_SLOTS, chips, 2, rows, width), BF16),
            pltpu.VMEM((CORE_SLOTS, chips, rows, width), BF16),
            pltpu.VMEM((CHIP_SLOTS, 2 * (chips - 1), half, width), BF16),
            pltpu.VMEM((4, nt - 1, rows, width), BF16),
            pltpu.VMEM((SPACING * levels, chips, rows, width), BF16),
            pltpu.VMEM((Z_SLOTS, rows, width), BF16),
            pltpu.VMEM((steps + 1, 8, dim), F32),
            pltpu.VMEM((steps, 8, dim), F32),
            dma((15,)),
            dma((4,)),
            dma((count, slots)),
            dma((count, slots)),
            dma((4, nt - 1)),
            dma((4, nt - 1)),
            dma((steps,)),
            dma((steps,)),
            *[dma((nt,)) for _ in range(6)],
            *[dma((ndp,)) for _ in range(4)],
            pltpu.SemaphoreType.REGULAR,
            pltpu.SemaphoreType.REGULAR((levels, 2)),
        ],
        compiler_params=pltpu.CompilerParams(
            collective_id=1, has_side_effects=True, vmem_limit_bytes=VMEM_LIMIT
        ),
        name="back",
    )(
        tok_lens,
        enc_lens,
        back_slot,
        wg,
        x,
        ed,
        cot,
        n1,
        q1,
        k1,
        v1,
        o1,
        h1,
        n2,
        q2,
        k2,
        v2,
        o2,
        h2,
        norms,
    )


def select_rows(lookup, positions):
    matches = positions[:, None] == jnp.arange(lookup.shape[0], dtype=jnp.int32)[None, :]
    return jnp.sum(jnp.where(matches, lookup[None, :], 0), axis=1)


def route_rows(selector, value_entries):
    return jnp.einsum(
        "kj,jrd->krd", selector, value_entries, preferred_element_type=F32
    ).astype(BF16)


def per_device(
    ndp,
    nt,
    tokens,
    enc_states,
    cotangent,
    tok_len,
    enc_len,
    deal,
    w_q_self,
    w_k_self,
    w_v_self,
    w_o_self,
    w_q_cross,
    w_k_cross,
    w_v_cross,
    w_o_cross,
    w_in,
    w_out,
    gain,
    bias,
):
    d = lax.axis_index("dp")
    t = lax.axis_index("tensor")
    seqs, _, dim = tokens.shape
    spd = seqs // nt
    hc = w_q_self.shape[1]
    slots = d * seqs + jnp.arange(seqs, dtype=jnp.int32)
    sources = select_rows(deal, slots)
    every = jnp.arange(deal.shape[0], dtype=jnp.int32)
    targets = jnp.sum(jnp.where(deal[None, :] == slots[:, None], every[None, :], 0), axis=1)
    peers = jnp.arange(ndp, dtype=jnp.int32)
    outward = (targets[None, :] // seqs == peers[:, None]).astype(BF16)
    tok_lens = lax.dynamic_slice(select_rows(tok_len, sources), (t * spd,), (spd,))
    enc_lens = lax.dynamic_slice(select_rows(enc_len, sources), (t * spd,), (spd,))

    weights = (
        w_q_self,
        w_k_self,
        w_v_self,
        w_o_self,
        w_q_cross,
        w_k_cross,
        w_v_cross,
        w_o_cross,
        w_in,
        w_out,
    )
    wg, *kept = front(
        ndp,
        nt,
        spd,
        tok_lens,
        enc_lens,
        sources // seqs,
        route_rows(outward, tokens),
        route_rows(outward, enc_states),
        cotangent,
        weights,
        gain,
        bias,
    )
    back_slot = jnp.sum(
        jnp.where(
            sources[None, :] // seqs == peers[:, None],
            jnp.arange(seqs, dtype=jnp.int32)[None, :],
            0,
        ),
        axis=1,
    )
    norms = jnp.concatenate([gain, bias, jnp.zeros((2, dim), F32)])
    res, tok_grads, enc_grads, grads, norm = back(
        ndp, nt, spd, tok_lens, enc_lens, back_slot, wg, kept, norms
    )

    def attention(g):
        return (g[:, :hc], g[:, hc : 2 * hc], g[:, 2 * hc : 3 * hc], g[:, 3 * hc :].T)

    return (
        res,
        route_rows(outward.T, tok_grads),
        route_rows(outward.T, enc_grads),
        *attention(grads[0]),
        *attention(grads[1]),
        grads[2],
        grads[3].T,
        norm[0:3],
        norm[3:6],
    )


def solution(mesh):
    ndp, nt = mesh.shape["dp"], mesh.shape["tensor"]
    rows = P("dp", "tensor", None)
    columns = P(None, "tensor")
    split = P("tensor", None)
    grad = P("dp", "tensor")
    turned = P("tensor", "dp")
    return jax.shard_map(
        functools.partial(per_device, ndp, nt),
        mesh=mesh,
        in_specs=(
            (rows,) * 3
            + (P(),) * 3
            + (columns, columns, columns, split) * 2
            + (columns, split, P(), P())
        ),
        out_specs=(
            (rows,) * 3 + (grad, grad, grad, turned) * 2 + (grad, turned) + (P(), P())
        ),
        check_vma=False,
    )
```

```python
import functools

import jax
import jax.numpy as jnp
from jax import lax
from jax.experimental import pallas as pl
from jax.experimental.pallas import tpu as pltpu
from jax.sharding import PartitionSpec as P

HEAD_DIM = 64
SCALE = 0.125
MASKED = -1e30
EPSILON = 1e-05
MESH = pl.DeviceIdType.MESH
VMEM_LIMIT = 60 * 1024 * 1024
SPACING = 2
Z_LEAD = 2
BF16 = jnp.bfloat16
F32 = jnp.float32


def dot_nn(a, b):
    return lax.dot_general(a, b, (((1,), (0,)), ((), ())), preferred_element_type=F32)


def dot_nt(a, b):
    return lax.dot_general(a, b, (((1,), (1,)), ((), ())), preferred_element_type=F32)


def dot_tn(a, b):
    return lax.dot_general(a, b, (((0,), (0,)), ((), ())), preferred_element_type=F32)


def norm_parts(v):
    mu = jnp.mean(v, axis=-1, keepdims=True)
    var = jnp.mean(v * v, axis=-1, keepdims=True) - mu * mu
    rstd = lax.rsqrt(var + EPSILON)
    return (v - mu) * rstd, rstd


def norm_back(dn, nh, rstd, gain):
    c = dn * gain
    return rstd * (
        c - jnp.mean(c, axis=-1, keepdims=True) - nh * jnp.mean(c * nh, axis=-1, keepdims=True)
    )


def head_stack(a, heads):
    lane = lax.broadcasted_iota(jnp.int32, a.shape, 1) // HEAD_DIM
    zero = jnp.zeros_like(a)
    return jnp.concatenate([jnp.where(lane == h, a, zero) for h in range(heads)], axis=0)


def attn_probs(q, k, limit, causal):
    heads = q.shape[1] // HEAD_DIM
    qs = head_stack(q, heads)
    s = dot_nt(qs, k) * SCALE
    key = lax.broadcasted_iota(jnp.int32, s.shape, 1)
    allowed = key < limit
    if causal:
        row = lax.rem(lax.broadcasted_iota(jnp.int32, s.shape, 0), q.shape[0])
        allowed = allowed & (key <= row)
    s = jnp.where(allowed, s, MASKED)
    e = jnp.exp(s - jnp.max(s, axis=-1, keepdims=True))
    return qs, e / jnp.sum(e, axis=-1, keepdims=True)


def lane_stack(a, heads):
    rows = a.shape[0] // heads
    return jnp.concatenate([a[h * rows : (h + 1) * rows] for h in range(heads)], axis=1)


def attn_fwd(q, k, v, limit, causal):
    heads = q.shape[1] // HEAD_DIM
    _, p = attn_probs(q, k, limit, causal)
    return dot_nn(lane_stack(p.astype(BF16), heads), head_stack(v, heads)).astype(BF16)


def attn_bwd(q, k, v, do, limit, causal):
    heads = q.shape[1] // HEAD_DIM
    qs, p = attn_probs(q, k, limit, causal)
    dos = head_stack(do, heads)
    dp = dot_nt(dos, v)
    delta = jnp.sum(p * dp, axis=-1, keepdims=True)
    ds = (p * (dp - delta) * SCALE).astype(BF16)
    dq = dot_nn(lane_stack(ds, heads), head_stack(k, heads)).astype(BF16)
    dk = dot_tn(ds, qs).astype(BF16)
    dv = dot_tn(p.astype(BF16), dos).astype(BF16)
    return dq, dk, dv


def row_valid(lens, spd, n):
    row = lax.broadcasted_iota(jnp.int32, (n, 1), 0)
    seq = n // spd
    end = jnp.full((n, 1), lens[0], jnp.int32)
    for i in range(1, spd):
        end = jnp.where(row >= i * seq, i * seq + lens[i], end)
    return row < end


def flip(index, mask):
    out = index
    bit = 1
    while bit <= mask:
        if mask & bit:
            out = out + bit - 2 * bit * lax.rem(lax.div(index, bit), 2)
        bit *= 2
    return out


def xor_of(a, b, size):
    out = 0
    bit = 1
    while bit < size:
        out = out + bit * lax.rem(lax.div(a, bit) + lax.div(b, bit), 2)
        bit *= 2
    return out


def greet(peers):
    barrier = pltpu.get_barrier_semaphore()
    for peer in peers:
        pl.semaphore_signal(barrier, inc=1, device_id=peer, device_id_type=MESH)
    pl.semaphore_wait(barrier, len(peers))


def front_kernel(
    ndp,
    nt,
    spd,
    deal_ref,
    tok_len_ref,
    enc_len_ref,
    tok_ref,
    enc_ref,
    cot_ref,
    w_refs,
    gain,
    bias,
    wg,
    x_ref,
    ed_ref,
    cots_ref,
    n1_ref,
    q1_ref,
    k1_ref,
    v1_ref,
    o1_ref,
    h1_ref,
    n2_ref,
    q2_ref,
    k2_ref,
    v2_ref,
    o2_ref,
    h2_ref,
    tx_tok,
    tx_enc,
    rx_tok,
    rx_enc,
    zs_tok,
    zs_enc,
    own,
    raw_o,
    raw_out,
    wbuf,
    load_sems,
    own_sem,
    wbuf_sems,
    tok_send,
    tok_recv,
    enc_send,
    enc_recv,
    zt_send,
    zt_recv,
    ze_send,
    ze_recv,
    zc_send,
    zc_recv,
    line_send,
    pass_send,
    send_sems,
    recv_sems,
):
    d = lax.axis_index("dp")
    t = lax.axis_index("tensor")
    dim, width = own.shape[1:]
    hc = width // 4
    rows_each = dim // ndp
    half = rows_each // 2
    bits = ndp.bit_length() - 1
    chip_bits = [1 << b for b in range(1, bits)]
    orders = (chip_bits, chip_bits[::-1])
    levels = len(chip_bits)
    seqs, lr = cot_ref.shape[0], cot_ref.shape[1]
    le = enc_ref.shape[1]
    seq, enc = nt * lr, nt * le
    n, m = spd * seq, spd * enc
    waits = []
    sources = [deal_ref[d * seqs + i] for i in range(seqs)]
    tok_lens = [tok_len_ref[deal_ref[d * seqs + t * spd + i]] for i in range(spd)]
    enc_lens = [enc_len_ref[deal_ref[d * seqs + t * spd + i]] for i in range(spd)]

    def dp_peer(bit):
        return (flip(d, bit), t)

    def t_peer(j):
        return (d, flip(t, j))

    def slab(index, side=None):
        if side is None:
            return pl.ds(pl.multiple_of(index * rows_each, rows_each), rows_each)
        return pl.ds(pl.multiple_of(index * rows_each + side * half, half), half)

    def remote(src, dst, ssem, rsem, peer):
        return pltpu.make_async_remote_copy(
            src_ref=src,
            dst_ref=dst,
            send_sem=ssem,
            recv_sem=rsem,
            device_id=peer,
            device_id_type=MESH,
        )

    def send(*args):
        copy = remote(*args)
        copy.start()
        waits.append(copy)
        return copy

    def local(src, dst, sem):
        copy = pltpu.make_async_copy(src, dst, sem)
        copy.start()
        return copy

    tok_load = local(tok_ref, zs_tok, load_sems.at[10])
    enc_load = local(enc_ref, zs_enc, load_sems.at[11])
    out_slot = []
    for k in range(ndp):
        slot = 0
        for i in range(seqs):
            slot = jnp.where(deal_ref[k * seqs + i] == d * seqs + i, i, slot)
        out_slot.append(slot)
    greet([dp_peer(e) for e in range(1, ndp)] + [t_peer(j) for j in range(1, nt)])

    def to_peers(load, held, blocks, rx, ssem, rsem):
        load.wait()
        for k in range(ndp):
            blocks[k] = held[out_slot[k]]
        return [
            send(blocks.at[flip(d, e)], rx.at[d], ssem.at[e], rsem.at[e], dp_peer(e))
            for e in range(1, ndp)
        ], local(blocks.at[d], rx.at[d], rsem.at[0])

    tok_copies, tok_own = to_peers(tok_load, zs_tok, tx_tok, rx_tok, tok_send, tok_recv)

    wq1, wk1, wv1, wo1, wq2, wk2, wv2, wo2, w_in, w_out = w_refs
    loads = [
        local(src, dst, load_sems.at[i])
        for i, (src, dst) in enumerate(
            [
                (wo1, raw_o.at[0]),
                (wq1, own.at[0, :, pl.ds(0, hc)]),
                (wk1, own.at[0, :, pl.ds(hc, hc)]),
                (wv1, own.at[0, :, pl.ds(2 * hc, hc)]),
                (wo2, raw_o.at[1]),
                (wq2, own.at[1, :, pl.ds(0, hc)]),
                (wk2, own.at[1, :, pl.ds(hc, hc)]),
                (wv2, own.at[1, :, pl.ds(2 * hc, hc)]),
                (w_in, own.at[2]),
                (w_out, raw_out),
            ]
        )
    ]

    chunks = [(g, j) for g in range(4) for j in range(1, nt)]

    def line_copy(g, step):
        there = t + step
        j = xor_of(t, there, nt)
        return remote(
            own.at[g, slab(d)],
            wg.at[j, g, slab(d)],
            line_send.at[g, (step + 1) // 2],
            recv_sems.at[g * (nt - 1) + j - 1, 0],
            (d, there),
        )

    def pass_copy(c, step):
        g, j = chunks[c]
        there = t + step
        j_there = xor_of(flip(t, j), there, nt)
        return remote(
            wg.at[j, g, slab(d)],
            wg.at[j_there, g, slab(d)],
            pass_send.at[c],
            recv_sems.at[g * (nt - 1) + j_there - 1, 0],
            (d, there),
        )

    def on_line(act, g):
        @pl.when(t + 1 < nt)
        def _():
            act(line_copy(g, 1))

        @pl.when(t >= 1)
        def _():
            act(line_copy(g, -1))

    def on_pass(act, c):
        s = flip(t, chunks[c][1])

        @pl.when((s < t) & (t + 1 < nt))
        def _():
            act(pass_copy(c, 1))

        @pl.when((s > t) & (t >= 1))
        def _():
            act(pass_copy(c, -1))

    def start(copy):
        copy.start()

    def arrived(c):
        g, j = chunks[c]
        at = wg.at[j, g, slab(d)]
        remote(at, at, pass_send.at[c], recv_sems.at[c, 0], t_peer(j)).wait_recv()
        on_pass(start, c)

    pending = {}

    def spread(c, level):
        g, j = chunks[c]
        if level:
            for copy in pending.pop((c, level)):
                copy.wait_recv()
        slot = 1 + 2 * ((1 << level) - 1)
        copies = []
        if level < levels:
            for side, order in enumerate(orders):
                held = [0]
                for bit in order[:level]:
                    held += [e ^ bit for e in held]
                for e in held:
                    at = wg.at[j, g, slab(flip(d, e), side)]
                    copies.append(
                        send(
                            at,
                            at,
                            send_sems.at[c, slot],
                            recv_sems.at[c, slot],
                            dp_peer(order[level]),
                        )
                    )
                    slot += 1
        elif level == levels:
            for e in range(0, ndp, 2):
                at = wg.at[j, g, slab(flip(d, e))]
                copies.append(
                    send(at, at, send_sems.at[c, slot], recv_sems.at[c, slot], dp_peer(1))
                )
                slot += 1
        elif g < 2:
            fills[c] = local(wg.at[j, g], wbuf.at[c % 2], wbuf_sems.at[c % 2])
        if copies:
            pending[(c, level + 1)] = copies

    fills = {}

    def to_sequences(src, dst, rows, ssem, rsem):
        for j in range(1, nt):
            there = flip(t, j)
            send(
                src.at[pl.ds(there * spd, spd)],
                dst.at[:, pl.ds(pl.multiple_of(t * rows, rows), rows)],
                ssem.at[j],
                rsem.at[j],
                t_peer(j),
            )
        return local(
            src.at[pl.ds(t * spd, spd)],
            dst.at[:, pl.ds(pl.multiple_of(t * rows, rows), rows)],
            rsem.at[0],
        )

    def sequences_here(own_copy, src, dst, rows, ssem, rsem):
        own_copy.wait()
        for j in range(1, nt):
            there = flip(t, j)
            remote(
                src.at[pl.ds(t * spd, spd)],
                dst.at[:, pl.ds(pl.multiple_of(there * rows, rows), rows)],
                ssem.at[j],
                rsem.at[j],
                t_peer(j),
            ).wait_recv()

    def blocks_here(copies, own_copy, rx, zs):
        own_copy.wait()
        for copy in copies:
            copy.wait_recv()
        for i in range(seqs):
            zs[i] = rx[lax.div(sources[i], seqs)]

    def self_norm():
        x = x_ref[...].reshape(n, dim).astype(F32)
        nh, _ = norm_parts(x)
        n1_ref[...] = (nh * gain[0:1] + bias[0:1]).astype(BF16)
        h1_ref[...] = x

    def self_part(j, w):
        qkv = dot_nn(n1_ref[...], w[:, : 3 * hc]).astype(BF16)
        q1_ref[j] = qkv[:, :hc]
        k1_ref[j] = qkv[:, hc : 2 * hc]
        v1_ref[j] = qkv[:, 2 * hc :]
        for i in range(spd):
            rows = slice(i * seq, (i + 1) * seq)
            o1_ref[j, rows] = attn_fwd(
                q1_ref[j, rows], k1_ref[j, rows], v1_ref[j, rows], tok_lens[i], True
            )
        h1_ref[...] += dot_nt(o1_ref[j], w[:, 3 * hc :])

    def cross_norm():
        h = h1_ref[...]
        nh, _ = norm_parts(h)
        n2_ref[...] = (nh * gain[1:2] + bias[1:2]).astype(BF16)
        h2_ref[...] = h

    def cross_part(j, w):
        q2_ref[j] = dot_nn(n2_ref[...], w[:, :hc]).astype(BF16)
        kv = dot_nn(ed_ref[...].reshape(m, dim), w[:, hc : 3 * hc]).astype(BF16)
        k2_ref[j] = kv[:, :hc]
        v2_ref[j] = kv[:, hc:]
        for i in range(spd):
            rows = slice(i * seq, (i + 1) * seq)
            keys = slice(i * enc, (i + 1) * enc)
            o2_ref[j, rows] = attn_fwd(
                q2_ref[j, rows], k2_ref[j, keys], v2_ref[j, keys], enc_lens[i], False
            )
        h2_ref[...] += dot_nt(o2_ref[j], w[:, 3 * hc :])

    for i in range(4):
        loads[i].wait()
    own[0, :, 3 * hc :] = raw_o[0].T
    on_line(start, 0)
    blocks_here(tok_copies, tok_own, rx_tok, zs_tok)
    own_x = to_sequences(zs_tok, x_ref, lr, zt_send, zt_recv)
    enc_copies, enc_own = to_peers(enc_load, zs_enc, tx_enc, rx_enc, enc_send, enc_recv)
    for i in range(4, 10):
        loads[i].wait()
    own[1, :, 3 * hc :] = raw_o[1].T
    block = min(256, width)
    for at in range(0, width, block):
        own[3, :, at : at + block] = raw_out[at : at + block].T
    own_copy = local(own, wg.at[0], own_sem)

    state = {}
    count = len(chunks)
    per = nt - 1
    stage_at = [SPACING * level for level in range(levels + 1)]
    stage_at.append(stage_at[-1] + 1)

    def line_stage(c):
        arrived(c)
        if c % per == 0 and c // per + 1 < 4:
            on_line(start, c // per + 1)

    for c in range(min(Z_LEAD, count)):
        line_stage(c)
    part_at = stage_at[-1] + 1
    for tick in range(count + part_at):
        if tick + Z_LEAD < count:
            line_stage(tick + Z_LEAD)
        for level in range(levels + 1, -1, -1):
            c = tick - stage_at[level]
            if 0 <= c < count:
                spread(c, level)
        if tick == 0:
            blocks_here(enc_copies, enc_own, rx_enc, zs_enc)
            own_ed = to_sequences(zs_enc, ed_ref, le, ze_send, ze_recv)
        if tick == 1:
            sequences_here(own_x, zs_tok, x_ref, lr, zt_send, zt_recv)
            self_norm()
            self_part(0, own.at[0])
        c = tick - part_at
        if 0 <= c < 2 * per:
            g, j = chunks[c]
            fills[c].wait()
            (self_part if g == 0 else cross_part)(j, wbuf.at[c % 2])
            if c == per - 1:
                sequences_here(own_ed, zs_enc, ed_ref, le, ze_send, ze_recv)
                own_cot = to_sequences(cot_ref, cots_ref, lr, zc_send, zc_recv)
                cross_norm()
                cross_part(0, own.at[1])

    sequences_here(own_cot, cot_ref, cots_ref, lr, zc_send, zc_recv)
    own_copy.wait()
    for g in range(4):
        on_line(lambda copy: copy.wait_send(), g)
    for c in range(count):
        on_pass(lambda copy: copy.wait_send(), c)
    for copy in waits:
        copy.wait_send()


def front(ndp, nt, spd, deal, tok_len, enc_len, tokens, enc_states, cot, weights, gain, bias):
    seqs, lr, dim = cot.shape
    le = enc_states.shape[1]
    seq, enc = nt * lr, nt * le
    n, m = spd * seq, spd * enc
    hc = weights[0].shape[1]
    width = 4 * hc
    count = 4 * (nt - 1)
    slots = 1 + 2 * (ndp // 2 - 1) + ndp // 2
    smem = pl.BlockSpec(memory_space=pltpu.SMEM)
    vmem = pl.BlockSpec(memory_space=pltpu.VMEM)
    any_space = pl.BlockSpec(memory_space=pl.ANY)
    dma = pltpu.SemaphoreType.DMA
    shape = jax.ShapeDtypeStruct
    part, keys = shape((nt, n, hc), BF16), shape((nt, m, hc), BF16)

    def body(*refs):
        front_kernel(ndp, nt, spd, *refs[:6], refs[6:16], *refs[16:])

    return pl.pallas_call(
        body,
        in_specs=[smem] * 3 + [any_space] * 13 + [vmem] * 2,
        out_specs=[any_space, vmem, vmem, any_space] + [vmem] * 12,
        out_shape=[
            shape((nt, 4, dim, width), BF16),
            shape((spd, seq, dim), BF16),
            shape((spd, enc, dim), BF16),
            shape((spd, seq, dim), BF16),
            shape((n, dim), BF16),
            part,
            part,
            part,
            part,
            shape((n, dim), F32),
            shape((n, dim), BF16),
            part,
            keys,
            keys,
            part,
            shape((n, dim), F32),
        ],
        scratch_shapes=[
            pltpu.VMEM((ndp, lr, dim), BF16),
            pltpu.VMEM((ndp, le, dim), BF16),
            pltpu.VMEM((ndp, lr, dim), BF16),
            pltpu.VMEM((ndp, le, dim), BF16),
            pltpu.VMEM((seqs, lr, dim), BF16),
            pltpu.VMEM((seqs, le, dim), BF16),
            pltpu.VMEM((4, dim, width), BF16),
            pltpu.VMEM((2, hc, dim), BF16),
            pltpu.VMEM((width, dim), BF16),
            pltpu.VMEM((2, dim, width), BF16),
            dma((12,)),
            dma,
            dma((2,)),
            dma((ndp,)),
            dma((ndp,)),
            dma((ndp,)),
            dma((ndp,)),
            dma((nt,)),
            dma((nt,)),
            dma((nt,)),
            dma((nt,)),
            dma((nt,)),
            dma((nt,)),
            dma((4, 2)),
            dma((count,)),
            dma((count, slots)),
            dma((count, slots)),
        ],
        compiler_params=pltpu.CompilerParams(
            collective_id=0, has_side_effects=True, vmem_limit_bytes=VMEM_LIMIT
        ),
        name="front",
    )(deal, tok_len, enc_len, tokens, enc_states, cot, *weights, gain, bias)


CORE_SLOTS = 4
CHIP_SLOTS = 4
DW_SLOTS = 3
Z_SLOTS = 4


def back_kernel(
    ndp,
    nt,
    spd,
    deal_ref,
    tok_len_ref,
    enc_len_ref,
    wg,
    x_hbm,
    ed_hbm,
    cot_hbm,
    n1_hbm,
    q1_hbm,
    k1_hbm,
    v1_hbm,
    o1_hbm,
    h1_hbm,
    n2_hbm,
    q2_hbm,
    k2_hbm,
    v2_hbm,
    o2_hbm,
    h2_hbm,
    gain,
    bias,
    res_out,
    rx_tok,
    rx_enc,
    grad_ref,
    norm_ref,
    h2_ref,
    cot_ref,
    h1_ref,
    n2_ref,
    ed_ref,
    q2_ref,
    k2_ref,
    v2_ref,
    o2_ref,
    x_ref,
    n1_ref,
    q1_ref,
    k1_ref,
    v1_ref,
    o1_ref,
    low,
    low_t,
    grad_low,
    grad_low_t,
    edt,
    out_acc,
    dn_acc,
    ded_acc,
    dh_ref,
    res_ref,
    dx_ref,
    ded_ref,
    dq,
    dk,
    dv,
    panels,
    zrx_tok,
    zrx_enc,
    sb_tok,
    sb_enc,
    dw,
    got_core,
    got_chip,
    got_z,
    work,
    final,
    total,
    got_sum,
    load_sems,
    panel_sems,
    send_sems,
    recv_sems,
    z_send,
    z_recv,
    sum_send,
    sum_recv,
    zr_send,
    zr_recv,
    zt_send,
    zt_recv,
    ze_send,
    ze_recv,
    tok_send,
    tok_recv,
    enc_send,
    enc_recv,
    core_credit,
    chip_credit,
):
    d = lax.axis_index("dp")
    t = lax.axis_index("tensor")
    bits = ndp.bit_length() - 1
    tbits = nt.bit_length() - 1
    chips = ndp // 2
    rows_each, width = grad_ref.shape[1], grad_ref.shape[2]
    dim = wg.shape[2]
    hc = width // 4
    half = rows_each // 2
    core = lax.rem(d, 2)
    chip = lax.div(d, 2)
    chip_bits = [1 << b for b in range(bits - 1)]
    orders = (chip_bits, chip_bits[::-1])
    levels = len(chip_bits)
    work_slots = work.shape[0]
    seqs, lr = res_out.shape[0], res_out.shape[1]
    le = rx_enc.shape[1]
    seq, enc = nt * lr, nt * le
    n, m = spd * seq, spd * enc
    started = []
    sources = [deal_ref[d * seqs + i] for i in range(seqs)]
    tok_lens = [tok_len_ref[deal_ref[d * seqs + t * spd + i]] for i in range(spd)]
    enc_lens = [enc_len_ref[deal_ref[d * seqs + t * spd + i]] for i in range(spd)]

    def dp_peer(bit):
        return (flip(d, bit), t)

    def t_peer(j):
        return (d, flip(t, j))

    def remote(src, dst, ssem, rsem, peer):
        return pltpu.make_async_remote_copy(
            src_ref=src,
            dst_ref=dst,
            send_sem=ssem,
            recv_sem=rsem,
            device_id=peer,
            device_id_type=MESH,
        )

    def send(*args):
        copy = remote(*args)
        copy.start()
        started.append(copy)
        return copy

    def sent(copy):
        copy.wait_send()
        started[:] = [one for one in started if one is not copy]

    def local(src, dst, sem):
        copy = pltpu.make_async_copy(src, dst, sem)
        copy.start()
        return copy

    loads = [
        local(src, dst, load_sems.at[i])
        for i, (src, dst) in enumerate(
            [
                (h2_hbm, h2_ref),
                (cot_hbm, cot_ref),
                (n2_hbm, n2_ref),
                (ed_hbm, ed_ref),
                (q2_hbm, q2_ref),
                (k2_hbm, k2_ref),
                (v2_hbm, v2_ref),
                (o2_hbm, o2_ref),
                (h1_hbm, h1_ref),
                (n1_hbm, n1_ref),
                (q1_hbm, q1_ref),
                (k1_hbm, k1_ref),
                (v1_hbm, v1_ref),
                (o1_hbm, o1_ref),
                (x_hbm, x_ref),
            ]
        )
    ]

    def loaded(first, last):
        for i in range(first, last):
            loads[i].wait()

    shards = list(range(1, nt)) + [0]
    units = [("feed", j) for j in shards] + [("cross", j) for j in shards]
    units += [("self", j) for j in shards]
    made = {"feed": (3, 2), "cross": (1,), "self": (0,)}
    chunks = []
    unit_at = {}
    for u, (kind, j) in enumerate(units):
        unit_at[len(chunks)] = u
        chunks += [(g, j) for g in made[kind]]
    count = len(chunks)
    fetched = {}

    def fetch(u):
        if u < len(units):
            kind, j = units[u]
            fetched[u] = [
                local(wg.at[j, g], panels.at[2 * (u % 2) + i], panel_sems.at[2 * (u % 2) + i])
                for i, g in enumerate(made[kind])
            ]

    fetch(0)
    greet([dp_peer(e) for e in range(1, ndp)] + [t_peer(j) for j in range(1, nt)])

    def put(c, column, a, b):
        cols = b.shape[1]
        for e in range(chips):
            part = dot_nn(a[2 * e * rows_each : 2 * (e + 1) * rows_each], b)
            dw[c % DW_SLOTS, e, :, :, column : column + cols] = part.astype(BF16).reshape(
                2, rows_each, cols
            )

    def feed_init():
        loaded(0, 2)
        nh, _ = norm_parts(h2_ref[...])
        v = nh * gain[2:3] + bias[2:3]
        low[...] = v.astype(BF16)
        low_t[...] = v.T.astype(BF16)
        keep = row_valid(tok_lens, spd, n)
        dh = jnp.where(keep, cot_ref[...].reshape(n, dim).astype(F32), 0.0)
        grad_low[...] = dh.astype(BF16)
        grad_low_t[...] = dh.T.astype(BF16)
        out_acc[...] = jnp.zeros_like(out_acc)
        dn_acc[...] = jnp.zeros_like(dn_acc)

    def feed_part(c, wout_ref, win_ref):
        block = min(512, width)
        for at in range(0, width, block):
            win = win_ref[:, at : at + block]
            wout = wout_ref[:, at : at + block]
            u = dot_nn(low[...], win)
            ga = dot_nn(grad_low[...], wout)
            sg = 1.0 / (1.0 + jnp.exp(-u))
            r = (u * sg).astype(BF16)
            du = (ga * (sg * (1.0 + u * (1.0 - sg)))).astype(BF16)
            out_acc[...] += dot_nt(r, wout)
            dn_acc[...] += dot_nt(du, win)
            put(c, at, grad_low_t, r)
            put(c + 1, at, low_t, du)

    def norm_grads(row, v, gain_row):
        nh, rstd = norm_parts(v)
        dn = dn_acc[...]
        total[0, row : row + 1] = jnp.sum(dn * nh, axis=0, keepdims=True)
        total[0, 3 + row : 4 + row] = jnp.sum(dn, axis=0, keepdims=True)
        return norm_back(dn, nh, rstd, gain_row)

    def feed_end():
        keep = row_valid(tok_lens, spd, n)
        h2 = h2_ref[...]
        res = jnp.where(keep, h2 + out_acc[...], 0.0).astype(BF16)
        res_ref[...] = res.reshape(spd, seq, dim)
        dh = jnp.where(keep, cot_ref[...].reshape(n, dim).astype(F32), 0.0)
        dh_ref[...] = dh + norm_grads(2, h2, gain[2:3])

    def branch_init(kept):
        dh = dh_ref[...]
        grad_low[...] = dh.astype(BF16)
        grad_low_t[...] = dh.T.astype(BF16)
        low_t[...] = kept[...].T
        dn_acc[...] = jnp.zeros_like(dn_acc)

    def cross_init():
        loaded(2, 9)
        branch_init(n2_ref)
        edt[...] = ed_ref[...].reshape(m, dim).T
        ded_acc[...] = jnp.zeros_like(ded_acc)

    def cross_part(c, j, w):
        do = dot_nn(grad_low[...], w[:, 3 * hc :]).astype(BF16)
        for i in range(spd):
            rows = slice(i * seq, (i + 1) * seq)
            keys = slice(i * enc, (i + 1) * enc)
            dq[rows, :hc], dk[keys], dv[keys] = attn_bwd(
                q2_ref[j, rows], k2_ref[j, keys], v2_ref[j, keys], do[rows], enc_lens[i], False
            )
        dn_acc[...] += dot_nt(dq[:, :hc], w[:, :hc])
        ded_acc[...] += dot_nt(dk[...], w[:, hc : 2 * hc]) + dot_nt(dv[...], w[:, 2 * hc : 3 * hc])
        put(c, 0, low_t, dq[:, :hc])
        put(c, hc, edt, dk[...])
        put(c, 2 * hc, edt, dv[...])
        put(c, 3 * hc, grad_low_t, o2_ref[j])

    def cross_end():
        ded_ref[...] = ded_acc[...].astype(BF16).reshape(spd, enc, dim)
        dh_ref[...] += norm_grads(1, h1_ref[...], gain[1:2])

    def self_init():
        loaded(9, 15)
        branch_init(n1_ref)

    def self_part(c, j, w):
        do = dot_nn(grad_low[...], w[:, 3 * hc :]).astype(BF16)
        for i in range(spd):
            rows = slice(i * seq, (i + 1) * seq)
            dq[rows, :hc], dq[rows, hc : 2 * hc], dq[rows, 2 * hc :] = attn_bwd(
                q1_ref[j, rows], k1_ref[j, rows], v1_ref[j, rows], do[rows], tok_lens[i], True
            )
        dn_acc[...] += dot_nt(dq[...], w[:, : 3 * hc])
        put(c, 0, low_t, dq[...])
        put(c, 3 * hc, grad_low_t, o1_ref[j])

    def self_end():
        x = x_ref[...].reshape(n, dim).astype(F32)
        dx = dh_ref[...] + norm_grads(0, x, gain[0:1])
        dx_ref[...] = dx.astype(BF16).reshape(spd, seq, dim)

    def run_unit(c):
        u = unit_at[c]
        kind, j = units[u]
        for i in range(len(made[kind])):
            if c + i >= DW_SLOTS:
                sent(core_copies[c + i - DW_SLOTS])
        for copy in fetched.pop(u):
            copy.wait()
        fetch(u + 1)
        slot = 2 * (u % 2)
        first, last = j == shards[0], j == shards[-1]
        if kind == "feed":
            if first:
                feed_init()
            feed_part(c, panels.at[slot], panels.at[slot + 1])
            if last:
                feed_end()
        elif kind == "cross":
            if first:
                cross_init()
            cross_part(c, j, panels.at[slot])
            if last:
                cross_end()
        else:
            if first:
                self_init()
            self_part(c, j, panels.at[slot])
            if last:
                self_end()

    core_copies = {}
    chip_copies = {}
    z_copies = {}

    def core_send(c):
        if c >= CORE_SLOTS:
            pl.semaphore_wait(core_credit, 1)
        core_copies[c] = send(
            dw.at[c % DW_SLOTS, :, 1 - core],
            got_core.at[c % CORE_SLOTS],
            send_sems.at[c, 0],
            recv_sems.at[c, 0],
            dp_peer(1),
        )

    def core_add(c):
        core_copies[c].wait_recv()
        if c >= work_slots:
            for level in range(levels):
                for copy in chip_copies.pop((c - work_slots, level)):
                    sent(copy)

        def body(e, carry):
            a = dw[c % DW_SLOTS, e, core] + got_core[c % CORE_SLOTS, e]
            work[c % work_slots, e] = a
            return carry

        lax.fori_loop(0, chips, body, 0)
        if c + CORE_SLOTS < count:
            pl.semaphore_signal(core_credit, inc=1, device_id=dp_peer(1), device_id_type=MESH)
        chip_send(c, 0)

    def rest_of(order, level):
        rest = [0]
        for bit in order[level + 1 :]:
            rest += [e ^ bit for e in rest]
        return rest

    def chip_send(c, level):
        base = 2 * (chips - (chips >> level))
        copies = []
        for side, order in enumerate(orders):
            if c >= CHIP_SLOTS:
                pl.semaphore_wait(chip_credit.at[level, side], 1)
            for e in rest_of(order, level):
                at = base + len(copies)
                copies.append(
                    send(
                        work.at[
                            c % work_slots,
                            flip(chip, order[level] ^ e),
                            pl.ds(side * half, half),
                        ],
                        got_chip.at[c % CHIP_SLOTS, at],
                        send_sems.at[c, 1 + at],
                        recv_sems.at[c, 1 + at],
                        dp_peer(2 * order[level]),
                    )
                )
        chip_copies[(c, level)] = copies

    def chip_add(c, level):
        at = 2 * (chips - (chips >> level))
        g, j = chunks[c]
        copies = iter(chip_copies[(c, level)])
        last = level == levels - 1
        if last and j:
            zs = (c - c // len(shards)) % Z_SLOTS
            key = [k for k, v in z_copies.items() if v[1] == zs and not v[2]]
            for k in key:
                sent(z_copies[k][0])
                z_copies[k] = (z_copies[k][0], zs, True)
        for side, order in enumerate(orders):
            span = pl.ds(side * half, half)
            for e in rest_of(order, level):
                next(copies).wait_recv()
                near = flip(chip, e)
                a = work[c % work_slots, near, span]
                b = got_chip[c % CHIP_SLOTS, at]
                at += 1
                if not last:
                    work[c % work_slots, near, span] = a + b
                elif j:
                    final[zs, span] = a + b
                else:
                    grad_ref[g, span] = a.astype(F32) + b.astype(F32)
            if c + CHIP_SLOTS < count:
                pl.semaphore_signal(
                    chip_credit.at[level, side],
                    inc=1,
                    device_id=dp_peer(2 * order[level]),
                    device_id_type=MESH,
                )
        if not last:
            chip_send(c, level + 1)
        elif j:
            copy = send(
                final.at[zs],
                got_z.at[g, j - 1],
                z_send.at[g, j - 1],
                z_recv.at[g, j - 1],
                t_peer(j),
            )
            z_copies[(g, j)] = (copy, zs, False)

    def finish(c):
        g, j = chunks[c]
        if j == 0:
            a = grad_ref[g]
            for i in range(1, nt):
                z_copies[(g, i)][0].wait_recv()
                a = a + got_z[g, i - 1].astype(F32)
            grad_ref[g] = a

    def to_positions(src, dst, rows, ssem, rsem):
        for j in range(1, nt):
            there = flip(t, j)
            send(
                src.at[:, pl.ds(pl.multiple_of(there * rows, rows), rows)],
                dst.at[pl.ds(t * spd, spd)],
                ssem.at[j],
                rsem.at[j],
                t_peer(j),
            )
        return local(
            src.at[:, pl.ds(pl.multiple_of(t * rows, rows), rows)],
            dst.at[pl.ds(t * spd, spd)],
            rsem.at[0],
        )

    def positions_here(own_copy, src, dst, rows, ssem, rsem):
        own_copy.wait()
        for j in range(1, nt):
            remote(
                src.at[:, pl.ds(pl.multiple_of(t * rows, rows), rows)],
                dst.at[pl.ds(flip(t, j) * spd, spd)],
                ssem.at[j],
                rsem.at[j],
                t_peer(j),
            ).wait_recv()

    def to_inputs(zrx, sb, rx, ssem, rsem):
        for k in range(ndp):
            slot = 0
            for i in range(seqs):
                slot = jnp.where(lax.div(sources[i], seqs) == k, i, slot)
            sb[k] = zrx[slot]
        copies = [
            send(sb.at[flip(d, e)], rx.at[d], ssem.at[e], rsem.at[e], dp_peer(e))
            for e in range(1, ndp)
        ]
        return copies + [local(sb.at[d], rx.at[d], rsem.at[0])]

    def inputs_here(copies):
        for copy in copies[:-1]:
            copy.wait_recv()
        copies[-1].wait()

    sum_peers = [dp_peer(1 << b) for b in range(bits)] + [t_peer(1 << b) for b in range(tbits)]
    sum_copies = {}

    def sum_start(i):
        sum_copies[i] = send(
            total.at[i], got_sum.at[i], sum_send.at[i], sum_recv.at[i], sum_peers[i]
        )

    def sum_finish(i):
        sum_copies[i].wait_recv()
        total[i + 1] = total[i] + got_sum[i]

    total[0] = jnp.zeros_like(total[0])
    depth = SPACING * (levels + 1) + 2
    feed_last = count // 2 - 2
    cross_last = 3 * count // 4 - 1
    state = {}
    for tick in range(count + max(depth, len(sum_peers) + 3)):
        c = tick - depth
        if 0 <= c < count:
            finish(c)
        for level in range(levels - 1, -1, -1):
            c = tick - SPACING * (level + 2)
            if 0 <= c < count:
                chip_add(c, level)
        c = tick - SPACING
        if 0 <= c < count:
            core_add(c)
        if tick in unit_at:
            run_unit(tick)
        if tick < count:
            core_send(tick)
        if tick == feed_last:
            state["res"] = to_positions(res_ref, res_out, lr, zr_send, zr_recv)
        if tick == cross_last:
            state["ded"] = to_positions(ded_ref, zrx_enc, le, ze_send, ze_recv)
        if tick == cross_last + 2:
            positions_here(state["ded"], ded_ref, zrx_enc, le, ze_send, ze_recv)
            state["enc"] = to_inputs(zrx_enc, sb_enc, rx_enc, enc_send, enc_recv)
        if tick == count - 1:
            state["dx"] = to_positions(dx_ref, zrx_tok, lr, zt_send, zt_recv)
        if tick == count + 1:
            positions_here(state["dx"], dx_ref, zrx_tok, lr, zt_send, zt_recv)
            state["tok"] = to_inputs(zrx_tok, sb_tok, rx_tok, tok_send, tok_recv)
        i = tick - count
        if 0 <= i - 1 < len(sum_peers):
            sum_finish(i - 1)
        if 0 <= i < len(sum_peers):
            sum_start(i)
    norm_ref[...] = total[len(sum_peers)]
    positions_here(state["res"], res_ref, res_out, lr, zr_send, zr_recv)
    inputs_here(state["enc"])
    inputs_here(state["tok"])
    for copy in started:
        copy.wait_send()


def back(ndp, nt, spd, deal, tok_len, enc_len, wg, kept, gain, bias):
    x, ed, cot, n1, q1, k1, v1, o1, h1, n2, q2, k2, v2, o2, h2 = kept
    _, _, dim, width = wg.shape
    _, seq, _ = x.shape
    enc = ed.shape[1]
    lr, le = seq // nt, enc // nt
    seqs = spd * nt
    n, m = spd * seq, spd * enc
    hc = width // 4
    rows, chips = dim // ndp, ndp // 2
    half = rows // 2
    levels = chips.bit_length() - 1
    count = 4 * nt
    steps = (ndp.bit_length() - 1) + (nt.bit_length() - 1)
    slots = 1 + 2 * (chips - 1)
    smem = pl.BlockSpec(memory_space=pltpu.SMEM)
    vmem = pl.BlockSpec(memory_space=pltpu.VMEM)
    any_space = pl.BlockSpec(memory_space=pl.ANY)
    dma = pltpu.SemaphoreType.DMA
    shape = jax.ShapeDtypeStruct

    def like(a):
        return pltpu.VMEM(a.shape, a.dtype)

    return pl.pallas_call(
        functools.partial(back_kernel, ndp, nt, spd),
        in_specs=[smem] * 3 + [any_space] * 16 + [vmem] * 2,
        out_specs=[any_space] * 3 + [vmem] * 2,
        out_shape=[
            shape((seqs, lr, dim), BF16),
            shape((ndp, lr, dim), BF16),
            shape((ndp, le, dim), BF16),
            shape((4, rows, width), F32),
            shape((8, dim), F32),
        ],
        scratch_shapes=[
            *[like(a) for a in (h2, cot, h1, n2, ed, q2, k2, v2, o2, x, n1, q1, k1, v1, o1)],
            pltpu.VMEM((n, dim), BF16),
            pltpu.VMEM((dim, n), BF16),
            pltpu.VMEM((n, dim), BF16),
            pltpu.VMEM((dim, n), BF16),
            pltpu.VMEM((dim, m), BF16),
            pltpu.VMEM((n, dim), F32),
            pltpu.VMEM((n, dim), F32),
            pltpu.VMEM((m, dim), F32),
            pltpu.VMEM((n, dim), F32),
            pltpu.VMEM((spd, seq, dim), BF16),
            pltpu.VMEM((spd, seq, dim), BF16),
            pltpu.VMEM((spd, enc, dim), BF16),
            pltpu.VMEM((n, 3 * hc), BF16),
            pltpu.VMEM((m, hc), BF16),
            pltpu.VMEM((m, hc), BF16),
            pltpu.VMEM((4, dim, width), BF16),
            pltpu.VMEM((seqs, lr, dim), BF16),
            pltpu.VMEM((seqs, le, dim), BF16),
            pltpu.VMEM((ndp, lr, dim), BF16),
            pltpu.VMEM((ndp, le, dim), BF16),
            pltpu.VMEM((DW_SLOTS, chips, 2, rows, width), BF16),
            pltpu.VMEM((CORE_SLOTS, chips, rows, width), BF16),
            pltpu.VMEM((CHIP_SLOTS, 2 * (chips - 1), half, width), BF16),
            pltpu.VMEM((4, nt - 1, rows, width), BF16),
            pltpu.VMEM((SPACING * levels, chips, rows, width), BF16),
            pltpu.VMEM((Z_SLOTS, rows, width), BF16),
            pltpu.VMEM((steps + 1, 8, dim), F32),
            pltpu.VMEM((steps, 8, dim), F32),
            dma((15,)),
            dma((4,)),
            dma((count, slots)),
            dma((count, slots)),
            dma((4, nt - 1)),
            dma((4, nt - 1)),
            dma((steps,)),
            dma((steps,)),
            *[dma((nt,)) for _ in range(6)],
            *[dma((ndp,)) for _ in range(4)],
            pltpu.SemaphoreType.REGULAR,
            pltpu.SemaphoreType.REGULAR((levels, 2)),
        ],
        compiler_params=pltpu.CompilerParams(
            collective_id=1, has_side_effects=True, vmem_limit_bytes=VMEM_LIMIT
        ),
        name="back",
    )(
        deal,
        tok_len,
        enc_len,
        wg,
        x,
        ed,
        cot,
        n1,
        q1,
        k1,
        v1,
        o1,
        h1,
        n2,
        q2,
        k2,
        v2,
        o2,
        h2,
        gain,
        bias,
    )


def tail_kernel(seqs, deal_ref, res, rx_tok, rx_enc, grads, norm, *outs):
    d = lax.axis_index("dp")
    result, d_tok, d_enc = outs[:3]
    hc = outs[3].shape[1]
    result[...] = res[...]
    for i in range(seqs):
        peer = 0
        for k in range(rx_tok.shape[0]):
            peer = jnp.where(deal_ref[k * seqs + i] == d * seqs + i, k, peer)
        d_tok[i] = rx_tok[peer]
        d_enc[i] = rx_enc[peer]
    for g in range(2):
        for i in range(3):
            outs[3 + 4 * g + i][...] = grads[g, :, i * hc : (i + 1) * hc]
        outs[6 + 4 * g][...] = grads[g, :, 3 * hc :].T
    outs[11][...] = grads[2]
    outs[12][...] = grads[3].T
    outs[13][...] = norm[0:3]
    outs[14][...] = norm[3:6]


def tail(deal, res, rx_tok, rx_enc, grads, norm):
    seqs, lr, dim = res.shape
    le = rx_enc.shape[1]
    rows, width = grads.shape[1:]
    hc = width // 4
    vmem = pl.BlockSpec(memory_space=pltpu.VMEM)
    straight, turned = ((rows, hc), F32), ((hc, rows), F32)
    shapes = [((seqs, lr, dim), BF16), ((seqs, lr, dim), BF16), ((seqs, le, dim), BF16)]
    shapes += ([straight] * 3 + [turned]) * 2
    shapes += [((rows, width), F32), ((width, rows), F32), ((3, dim), F32), ((3, dim), F32)]
    return pl.pallas_call(
        functools.partial(tail_kernel, seqs),
        in_specs=[pl.BlockSpec(memory_space=pltpu.SMEM)] + [vmem] * 5,
        out_specs=[vmem] * len(shapes),
        out_shape=[jax.ShapeDtypeStruct(*one) for one in shapes],
        compiler_params=pltpu.CompilerParams(vmem_limit_bytes=VMEM_LIMIT),
        name="tail",
    )(deal, res, rx_tok, rx_enc, grads, norm)


def per_device(ndp, nt, tokens, enc_states, cotangent, tok_len, enc_len, deal, *rest):
    *weights, gain, bias = rest
    spd = tokens.shape[0] // nt
    wg, *kept = front(
        ndp, nt, spd, deal, tok_len, enc_len, tokens, enc_states, cotangent, weights, gain, bias
    )
    return tail(deal, *back(ndp, nt, spd, deal, tok_len, enc_len, wg, kept, gain, bias))


def solution(mesh):
    ndp, nt = mesh.shape["dp"], mesh.shape["tensor"]
    rows = P("dp", "tensor", None)
    columns = P(None, "tensor")
    split = P("tensor", None)
    grad = P("dp", "tensor")
    turned = P("tensor", "dp")
    return jax.shard_map(
        functools.partial(per_device, ndp, nt),
        mesh=mesh,
        in_specs=(
            (rows,) * 3
            + (P(),) * 3
            + (columns, columns, columns, split) * 2
            + (columns, split, P(), P())
        ),
        out_specs=(
            (rows,) * 3 + (grad, grad, grad, turned) * 2 + (grad, turned) + (P(), P())
        ),
        check_vma=False,
    )
```

```python
import functools

import jax
import jax.numpy as jnp
from jax import lax
from jax.experimental import pallas as pl
from jax.experimental.pallas import tpu as pltpu
from jax.sharding import PartitionSpec as P

HEAD_DIM = 64
SCALE = 0.125
MASKED = -1e30
EPSILON = 1e-05
MESH = pl.DeviceIdType.MESH
VMEM_LIMIT = 60 * 1024 * 1024
CORE_SLOTS = 4
CHIP_SLOTS = 4
DW_SLOTS = 3
Z_SLOTS = 4
SPACING = 2
Z_LEAD = 2
BF16 = jnp.bfloat16
F32 = jnp.float32


def dot_nn(a, b):
    return lax.dot_general(a, b, (((1,), (0,)), ((), ())), preferred_element_type=F32)


def dot_nt(a, b):
    return lax.dot_general(a, b, (((1,), (1,)), ((), ())), preferred_element_type=F32)


def dot_tn(a, b):
    return lax.dot_general(a, b, (((0,), (0,)), ((), ())), preferred_element_type=F32)


def norm_parts(v):
    mu = jnp.mean(v, axis=-1, keepdims=True)
    var = jnp.mean(v * v, axis=-1, keepdims=True) - mu * mu
    rstd = lax.rsqrt(var + EPSILON)
    return (v - mu) * rstd, rstd


def norm_back(dn, nh, rstd, gain):
    c = dn * gain
    return rstd * (
        c - jnp.mean(c, axis=-1, keepdims=True) - nh * jnp.mean(c * nh, axis=-1, keepdims=True)
    )


def head_stack(a, heads):
    lane = lax.broadcasted_iota(jnp.int32, a.shape, 1) // HEAD_DIM
    zero = jnp.zeros_like(a)
    return jnp.concatenate([jnp.where(lane == h, a, zero) for h in range(heads)], axis=0)


def attn_probs(q, k, limit, causal):
    heads = q.shape[1] // HEAD_DIM
    qs = head_stack(q, heads)
    s = dot_nt(qs, k) * SCALE
    key = lax.broadcasted_iota(jnp.int32, s.shape, 1)
    allowed = key < limit
    if causal:
        row = lax.rem(lax.broadcasted_iota(jnp.int32, s.shape, 0), q.shape[0])
        allowed = allowed & (key <= row)
    s = jnp.where(allowed, s, MASKED)
    e = jnp.exp(s - jnp.max(s, axis=-1, keepdims=True))
    return qs, e / jnp.sum(e, axis=-1, keepdims=True)


def lane_stack(a, heads):
    rows = a.shape[0] // heads
    return jnp.concatenate([a[h * rows : (h + 1) * rows] for h in range(heads)], axis=1)


def attn_fwd(q, k, v, limit, causal):
    heads = q.shape[1] // HEAD_DIM
    _, p = attn_probs(q, k, limit, causal)
    return dot_nn(lane_stack(p.astype(BF16), heads), head_stack(v, heads)).astype(BF16)


def attn_bwd(q, k, v, do, limit, causal):
    heads = q.shape[1] // HEAD_DIM
    qs, p = attn_probs(q, k, limit, causal)
    dos = head_stack(do, heads)
    dp = dot_nt(dos, v)
    delta = jnp.sum(p * dp, axis=-1, keepdims=True)
    ds = (p * (dp - delta) * SCALE).astype(BF16)
    dq = dot_nn(lane_stack(ds, heads), head_stack(k, heads)).astype(BF16)
    dk = dot_tn(ds, qs).astype(BF16)
    dv = dot_tn(p.astype(BF16), dos).astype(BF16)
    return dq, dk, dv


def row_valid(lens, spd, n):
    row = lax.broadcasted_iota(jnp.int32, (n, 1), 0)
    seq = n // spd
    end = jnp.full((n, 1), lens[0], jnp.int32)
    for i in range(1, spd):
        end = jnp.where(row >= i * seq, i * seq + lens[i], end)
    return row < end


def flip(index, mask):
    out = index
    bit = 1
    while bit <= mask:
        if mask & bit:
            out = out + bit - 2 * bit * lax.rem(lax.div(index, bit), 2)
        bit *= 2
    return out


def xor_of(a, b, size):
    out = 0
    bit = 1
    while bit < size:
        out = out + bit * lax.rem(lax.div(a, bit) + lax.div(b, bit), 2)
        bit *= 2
    return out


def nearest(t, nt):
    out = []
    for k in range(nt - 1):
        at = 0
        for place in range(nt):
            others = sorted((s for s in range(nt) if s != place), key=lambda s: abs(s - place))
            at = jnp.where(t == place, others[k], at)
        out.append(at)
    return out


def greet(peers):
    barrier = pltpu.get_barrier_semaphore()
    for peer in peers:
        pl.semaphore_signal(barrier, inc=1, device_id=peer, device_id_type=MESH)
    pl.semaphore_wait(barrier, len(peers))


def layer_kernel(
    ndp,
    nt,
    spd,
    deal_ref,
    tok_len_ref,
    enc_len_ref,
    tok_hbm,
    enc_hbm,
    cot_hbm,
    w_refs,
    gain,
    bias,
    wg,
    res_out,
    back_tok,
    back_enc,
    grad_ref,
    norm_ref,
    x_ref,
    ed_ref,
    cot_ref,
    n1_ref,
    q1_ref,
    k1_ref,
    v1_ref,
    o1_ref,
    h1_ref,
    n2_ref,
    q2_ref,
    k2_ref,
    v2_ref,
    o2_ref,
    h2_ref,
    low,
    low_t,
    grad_low,
    grad_low_t,
    edt,
    dn_acc,
    ded_acc,
    dh_ref,
    res_ref,
    dx_ref,
    ded_ref,
    dq,
    dk,
    dv,
    panels,
    tx_tok,
    tx_enc,
    rx_tok,
    rx_enc,
    zs_tok,
    zs_enc,
    dw,
    got_core,
    got_chip,
    got_z,
    work,
    final,
    total,
    got_sum,
    load_sems,
    own_sems,
    panel_sems,
    tok_send,
    tok_recv,
    enc_send,
    enc_recv,
    zt_send,
    zt_recv,
    ze_send,
    ze_recv,
    zc_send,
    zc_recv,
    line_send,
    line_recv,
    pass_send,
    gather_send,
    gather_recv,
    send_sems,
    recv_sems,
    z_send,
    z_recv,
    sum_send,
    sum_recv,
    br_send,
    br_recv,
    bt_send,
    bt_recv,
    be_send,
    be_recv,
    btok_send,
    btok_recv,
    benc_send,
    benc_recv,
    core_credit,
    chip_credit,
    left_sems,
):
    d = lax.axis_index("dp")
    t = lax.axis_index("tensor")
    dim, width = panels.shape[1:]
    hc = width // 4
    rows_each = dim // ndp
    half = rows_each // 2
    bits = ndp.bit_length() - 1
    tbits = nt.bit_length() - 1
    chips = ndp // 2
    core = lax.rem(d, 2)
    chip = lax.div(d, 2)
    chip_bits = [1 << b for b in range(bits - 1)]
    orders = (chip_bits, chip_bits[::-1])
    levels = len(chip_bits)
    work_slots = work.shape[0]
    seqs, lr = cot_hbm.shape[0], cot_hbm.shape[1]
    le = enc_hbm.shape[1]
    seq, enc = nt * lr, nt * le
    n, m = spd * seq, spd * enc
    out_acc = dh_ref
    near = nearest(t, nt)
    sources = [deal_ref[d * seqs + i] for i in range(seqs)]
    tok_lens = [tok_len_ref[deal_ref[d * seqs + t * spd + i]] for i in range(spd)]
    enc_lens = [enc_len_ref[deal_ref[d * seqs + t * spd + i]] for i in range(spd)]
    started = []

    def dp_peer(bit):
        return (flip(d, bit), t)

    def t_peer(j):
        return (d, flip(t, j))

    def rel(k):
        return 0 if k is None else xor_of(near[k], t, nt)

    def slab(index, side=None):
        if side is None:
            return pl.ds(pl.multiple_of(index * rows_each, rows_each), rows_each)
        return pl.ds(pl.multiple_of(index * rows_each + side * half, half), half)

    def remote(src, dst, ssem, rsem, peer):
        return pltpu.make_async_remote_copy(
            src_ref=src,
            dst_ref=dst,
            send_sem=ssem,
            recv_sem=rsem,
            device_id=peer,
            device_id_type=MESH,
        )

    def send(*args):
        copy = remote(*args)
        copy.start()
        started.append(copy)
        return copy

    def sent(copy):
        copy.wait_send()
        started[:] = [one for one in started if one is not copy]

    def local(src, dst, sem):
        copy = pltpu.make_async_copy(src, dst, sem)
        copy.start()
        return copy

    wq1, wk1, wv1, wo1, wq2, wk2, wv2, wo2, w_in, w_out = w_refs
    tok_load = local(tok_hbm, zs_tok, load_sems.at[0])
    raw = [low, grad_low]

    def load_raw(i):
        src = [wo1, wo2] + [w_out.at[pl.ds(b * hc, hc)] for b in range(4)]
        return local(src[i], raw[i % 2], load_sems.at[2 + i])

    raw_loads = {0: load_raw(0)}
    loads = [
        local(src, panels.at[g, :, pl.ds(i * hc, hc)], load_sems.at[8 + 3 * g + i])
        for g, three in enumerate(((wq1, wk1, wv1), (wq2, wk2, wv2)))
        for i, src in enumerate(three)
    ]
    enc_load = local(enc_hbm, zs_enc, load_sems.at[1])
    raw_loads[1] = load_raw(1)
    loads.append(local(w_in, panels.at[2], load_sems.at[14]))
    out_slot = []
    for k in range(ndp):
        slot = 0
        for i in range(seqs):
            slot = jnp.where(deal_ref[k * seqs + i] == d * seqs + i, i, slot)
        out_slot.append(slot)
    greet([dp_peer(e) for e in range(1, ndp)] + [t_peer(j) for j in range(1, nt)])

    def to_peers(held, slots, blocks, rx, ssem, rsem):
        for k in range(ndp):
            blocks[k] = held[slots[k]]
        return [
            send(blocks.at[flip(d, e)], rx.at[d], ssem.at[e], rsem.at[e], dp_peer(e))
            for e in range(1, ndp)
        ] + [local(blocks.at[d], rx.at[d], rsem.at[0])]

    def peers_here(copies):
        for copy in copies[:-1]:
            copy.wait_recv()
        copies[-1].wait()

    def blocks_here(copies, rx, zs):
        peers_here(copies)
        for i in range(seqs):
            zs[i] = rx[lax.div(sources[i], seqs)]

    def to_sequences(src, dst, rows, ssem, rsem):
        span = pl.ds(pl.multiple_of(t * rows, rows), rows)
        copies = [
            send(
                src.at[pl.ds(flip(t, j) * spd, spd)],
                dst.at[:, span],
                ssem.at[j],
                rsem.at[j],
                t_peer(j),
            )
            for j in range(1, nt)
        ]
        return copies + [local(src.at[pl.ds(t * spd, spd)], dst.at[:, span], rsem.at[0])]

    def free(copies, which):
        for copy in copies[:-1]:
            sent(copy)
        for j in range(1, nt):
            pl.semaphore_signal(
                left_sems.at[which], inc=1, device_id=t_peer(j), device_id_type=MESH
            )

    def sequences_here(copies, src, dst, rows, ssem, rsem):
        copies[-1].wait()
        for j in range(1, nt):
            there = flip(t, j)
            remote(
                src.at[pl.ds(t * spd, spd)],
                dst.at[:, pl.ds(pl.multiple_of(there * rows, rows), rows)],
                ssem.at[j],
                rsem.at[j],
                t_peer(j),
            ).wait_recv()

    gathered = [(g, k) for g in range(2) for k in range(nt - 1)]
    gathered += [(g, k) for k in range(nt - 1) for g in (2, 3)]

    def line_copy(g, step):
        there = t + step
        j = xor_of(t, there, nt)
        return remote(
            wg.at[0, g, slab(d)],
            wg.at[j, g, slab(d)],
            line_send.at[g, (step + 1) // 2],
            line_recv.at[g, j],
            (d, there),
        )

    def pass_copy(c, step):
        g, k = gathered[c]
        there = t + step
        j_there = xor_of(near[k], there, nt)
        return remote(
            wg.at[rel(k), g, slab(d)],
            wg.at[j_there, g, slab(d)],
            pass_send.at[c],
            line_recv.at[g, j_there],
            (d, there),
        )

    def on_line(act, g):
        @pl.when(t + 1 < nt)
        def _():
            act(line_copy(g, 1))

        @pl.when(t >= 1)
        def _():
            act(line_copy(g, -1))

    def on_pass(act, c):
        s = near[gathered[c][1]]

        @pl.when((s < t) & (t + 1 < nt))
        def _():
            act(pass_copy(c, 1))

        @pl.when((s > t) & (t >= 1))
        def _():
            act(pass_copy(c, -1))

    def start(copy):
        copy.start()

    def line_start(g):
        own_copies[g].wait()
        on_line(start, g)

    per = nt - 1
    line_after = {min(1, per - 1): 1, per + min(1, per - 1): 2, 2 * per - 1: 3}

    def line_stage(c):
        g, k = gathered[c]
        j = rel(k)
        at = wg.at[j, g, slab(d)]
        remote(at, at, pass_send.at[c], line_recv.at[g, j], (d, near[k])).wait_recv()
        on_pass(start, c)
        if c in line_after:
            line_start(line_after[c])

    pending = {}
    fills = {}

    def spread(c, level):
        g, k = gathered[c]
        j = rel(k)
        if level:
            for copy in pending.pop((c, level)):
                copy.wait_recv()
        slot = 2 * ((1 << level) - 1)
        copies = []
        if level < levels:
            for side, order in enumerate(orders):
                held = [0]
                for bit in order[:level]:
                    held += [e ^ bit for e in held]
                for e in held:
                    at = wg.at[j, g, slab(flip(d, 2 * e), side)]
                    sems = gather_send.at[c, slot], gather_recv.at[c, slot]
                    copies.append(send(at, at, *sems, dp_peer(2 * order[level])))
                    slot += 1
        elif level == levels:
            for e in range(0, ndp, 2):
                at = wg.at[j, g, slab(flip(d, e))]
                sems = gather_send.at[c, slot], gather_recv.at[c, slot]
                copies.append(send(at, at, *sems, dp_peer(1)))
                slot += 1
        elif g < 2:
            slot = 2 + c % 2
            fills[c] = local(wg.at[j, g], panels.at[slot], panel_sems.at[slot])
        if copies:
            pending[(c, level + 1)] = copies

    def self_norm():
        x = x_ref[...].reshape(n, dim).astype(F32)
        nh, _ = norm_parts(x)
        n1_ref[...] = (nh * gain[0:1] + bias[0:1]).astype(BF16)
        h1_ref[...] = x

    def self_forward(j, w):
        qkv = dot_nn(n1_ref[...], w[:, : 3 * hc]).astype(BF16)
        q1_ref[j] = qkv[:, :hc]
        k1_ref[j] = qkv[:, hc : 2 * hc]
        v1_ref[j] = qkv[:, 2 * hc :]
        for i in range(spd):
            rows = slice(i * seq, (i + 1) * seq)
            o1_ref[j, rows] = attn_fwd(
                q1_ref[j, rows], k1_ref[j, rows], v1_ref[j, rows], tok_lens[i], True
            )
        h1_ref[...] += dot_nt(o1_ref[j], w[:, 3 * hc :])

    def cross_norm():
        h = h1_ref[...]
        nh, _ = norm_parts(h)
        n2_ref[...] = (nh * gain[1:2] + bias[1:2]).astype(BF16)
        h2_ref[...] = h

    def cross_forward(j, w):
        q2_ref[j] = dot_nn(n2_ref[...], w[:, :hc]).astype(BF16)
        kv = dot_nn(ed_ref[...].reshape(m, dim), w[:, hc : 3 * hc]).astype(BF16)
        k2_ref[j] = kv[:, :hc]
        v2_ref[j] = kv[:, hc:]
        for i in range(spd):
            rows = slice(i * seq, (i + 1) * seq)
            keys = slice(i * enc, (i + 1) * enc)
            o2_ref[j, rows] = attn_fwd(
                q2_ref[j, rows], k2_ref[j, keys], v2_ref[j, keys], enc_lens[i], False
            )
        h2_ref[...] += dot_nt(o2_ref[j], w[:, 3 * hc :])

    nearby = list(range(nt - 1))
    units = [("feed", k) for k in [None] + nearby]
    units += [("cross", k) for k in nearby + [None]] + [("self", k) for k in nearby + [None]]
    made = {"feed": (3, 2), "cross": (1,), "self": (0,)}
    chunks = []
    unit_at = {}
    for u, (kind, k) in enumerate(units):
        unit_at[len(chunks)] = u
        chunks += [(g, k) for g in made[kind]]
    count = len(chunks)
    last_of = {g: c for c, (g, _) in enumerate(chunks)}
    fetched = {}

    def fetch(u):
        if u < len(units):
            kind, k = units[u]
            fetched[u] = [
                local(
                    wg.at[rel(k), g],
                    panels.at[2 * (u % 2) + i],
                    panel_sems.at[2 * (u % 2) + i],
                )
                for i, g in enumerate(made[kind])
            ]

    def put(c, column, a, b):
        cols = b.shape[1]
        for e in range(chips):
            part = dot_nn(a[2 * e * rows_each : 2 * (e + 1) * rows_each], b)
            dw[c % DW_SLOTS, e, :, :, column : column + cols] = part.astype(BF16).reshape(
                2, rows_each, cols
            )

    def feed_init():
        nh, _ = norm_parts(h2_ref[...])
        v = nh * gain[2:3] + bias[2:3]
        low[...] = v.astype(BF16)
        low_t[...] = v.T.astype(BF16)
        keep = row_valid(tok_lens, spd, n)
        dh = jnp.where(keep, cot_ref[...].reshape(n, dim).astype(F32), 0.0)
        grad_low[...] = dh.astype(BF16)
        grad_low_t[...] = dh.T.astype(BF16)
        out_acc[...] = jnp.zeros_like(out_acc)
        dn_acc[...] = jnp.zeros_like(dn_acc)

    def feed_part(c, wout_ref, win_ref):
        block = min(512, width)
        for at in range(0, width, block):
            win = win_ref[:, at : at + block]
            wout = wout_ref[:, at : at + block]
            u = dot_nn(low[...], win)
            ga = dot_nn(grad_low[...], wout)
            sg = 1.0 / (1.0 + jnp.exp(-u))
            r = (u * sg).astype(BF16)
            du = (ga * (sg * (1.0 + u * (1.0 - sg)))).astype(BF16)
            out_acc[...] += dot_nt(r, wout)
            dn_acc[...] += dot_nt(du, win)
            put(c, at, grad_low_t, r)
            put(c + 1, at, low_t, du)

    def norm_grads(row, v, gain_row):
        nh, rstd = norm_parts(v)
        dn = dn_acc[...]
        total[0, row : row + 1] = jnp.sum(dn * nh, axis=0, keepdims=True)
        total[0, 3 + row : 4 + row] = jnp.sum(dn, axis=0, keepdims=True)
        return norm_back(dn, nh, rstd, gain_row)

    def feed_end():
        keep = row_valid(tok_lens, spd, n)
        h2 = h2_ref[...]
        res = jnp.where(keep, h2 + out_acc[...], 0.0).astype(BF16)
        res_ref[...] = res.reshape(spd, seq, dim)
        dh = jnp.where(keep, cot_ref[...].reshape(n, dim).astype(F32), 0.0)
        dh_ref[...] = dh + norm_grads(2, h2, gain[2:3])

    def branch_init(kept):
        dh = dh_ref[...]
        grad_low[...] = dh.astype(BF16)
        grad_low_t[...] = dh.T.astype(BF16)
        low_t[...] = kept[...].T
        dn_acc[...] = jnp.zeros_like(dn_acc)

    def cross_init():
        branch_init(n2_ref)
        edt[...] = ed_ref[...].reshape(m, dim).T
        ded_acc[...] = jnp.zeros_like(ded_acc)

    def cross_backward(c, j, w):
        do = dot_nn(grad_low[...], w[:, 3 * hc :]).astype(BF16)
        for i in range(spd):
            rows = slice(i * seq, (i + 1) * seq)
            keys = slice(i * enc, (i + 1) * enc)
            dq[rows, :hc], dk[keys], dv[keys] = attn_bwd(
                q2_ref[j, rows], k2_ref[j, keys], v2_ref[j, keys], do[rows], enc_lens[i], False
            )
        dn_acc[...] += dot_nt(dq[:, :hc], w[:, :hc])
        ded_acc[...] += dot_nt(dk[...], w[:, hc : 2 * hc]) + dot_nt(dv[...], w[:, 2 * hc : 3 * hc])
        put(c, 0, low_t, dq[:, :hc])
        put(c, hc, edt, dk[...])
        put(c, 2 * hc, edt, dv[...])
        put(c, 3 * hc, grad_low_t, o2_ref[j])

    def cross_end():
        ded_ref[...] = ded_acc[...].astype(BF16).reshape(spd, enc, dim)
        dh_ref[...] += norm_grads(1, h1_ref[...], gain[1:2])

    def self_init():
        branch_init(n1_ref)

    def self_backward(c, j, w):
        do = dot_nn(grad_low[...], w[:, 3 * hc :]).astype(BF16)
        for i in range(spd):
            rows = slice(i * seq, (i + 1) * seq)
            dq[rows, :hc], dq[rows, hc : 2 * hc], dq[rows, 2 * hc :] = attn_bwd(
                q1_ref[j, rows], k1_ref[j, rows], v1_ref[j, rows], do[rows], tok_lens[i], True
            )
        dn_acc[...] += dot_nt(dq[...], w[:, : 3 * hc])
        put(c, 0, low_t, dq[...])
        put(c, 3 * hc, grad_low_t, o1_ref[j])

    def self_end():
        x = x_ref[...].reshape(n, dim).astype(F32)
        dx = dh_ref[...] + norm_grads(0, x, gain[0:1])
        dx_ref[...] = dx.astype(BF16).reshape(spd, seq, dim)

    def run_unit(c):
        u = unit_at[c]
        kind, k = units[u]
        j = rel(k)
        for i in range(len(made[kind])):
            if c + i >= DW_SLOTS:
                sent(core_copies[c + i - DW_SLOTS])
        for copy in fetched.pop(u):
            copy.wait()
        fetch(u + 1)
        w = panels.at[2 * (u % 2)]
        first, last = u % nt == 0, u % nt == nt - 1
        if kind == "feed":
            if first:
                feed_init()
            feed_part(c, w, panels.at[2 * (u % 2) + 1])
            if last:
                feed_end()
        elif kind == "cross":
            if first:
                cross_init()
            cross_backward(c, j, w)
            if last:
                cross_end()
        else:
            if first:
                self_init()
            self_backward(c, j, w)
            if last:
                self_end()

    core_copies = {}
    chip_copies = {}
    z_copies = []

    def core_send(c):
        if c >= CORE_SLOTS:
            pl.semaphore_wait(core_credit, 1)
        core_copies[c] = send(
            dw.at[c % DW_SLOTS, :, 1 - core],
            got_core.at[c % CORE_SLOTS],
            send_sems.at[c, 0],
            recv_sems.at[c, 0],
            dp_peer(1),
        )

    def core_add(c):
        core_copies[c].wait_recv()
        if c >= work_slots:
            for level in range(levels):
                for copy in chip_copies.pop((c - work_slots, level)):
                    sent(copy)

        def body(e, carry):
            a = dw[c % DW_SLOTS, e, core] + got_core[c % CORE_SLOTS, e]
            work[c % work_slots, e] = a
            return carry

        lax.fori_loop(0, chips, body, 0)
        if c + CORE_SLOTS < count:
            pl.semaphore_signal(core_credit, inc=1, device_id=dp_peer(1), device_id_type=MESH)
        chip_send(c, 0)

    def rest_of(order, level):
        rest = [0]
        for bit in order[level + 1 :]:
            rest += [e ^ bit for e in rest]
        return rest

    def chip_send(c, level):
        base = 2 * (chips - (chips >> level))
        copies = []
        for side, order in enumerate(orders):
            if c >= CHIP_SLOTS:
                pl.semaphore_wait(chip_credit.at[level, side], 1)
            for e in rest_of(order, level):
                at = base + len(copies)
                copies.append(
                    send(
                        work.at[
                            c % work_slots,
                            flip(chip, order[level] ^ e),
                            pl.ds(side * half, half),
                        ],
                        got_chip.at[c % CHIP_SLOTS, at],
                        send_sems.at[c, 1 + at],
                        recv_sems.at[c, 1 + at],
                        dp_peer(2 * order[level]),
                    )
                )
        chip_copies[(c, level)] = copies

    def chip_add(c, level):
        at = 2 * (chips - (chips >> level))
        g, k = chunks[c]
        copies = iter(chip_copies[(c, level)])
        last = level == levels - 1
        if last and k is not None:
            slot = len(z_copies) % Z_SLOTS
            if len(z_copies) >= Z_SLOTS:
                sent(z_copies[len(z_copies) - Z_SLOTS])
        for side, order in enumerate(orders):
            span = pl.ds(side * half, half)
            for e in rest_of(order, level):
                next(copies).wait_recv()
                place = flip(chip, e)
                a = work[c % work_slots, place, span]
                b = got_chip[c % CHIP_SLOTS, at]
                at += 1
                if not last:
                    work[c % work_slots, place, span] = a + b
                elif k is not None:
                    final[slot, span] = a + b
                else:
                    grad_ref[g, span] = a.astype(F32) + b.astype(F32)
            if c + CHIP_SLOTS < count:
                pl.semaphore_signal(
                    chip_credit.at[level, side],
                    inc=1,
                    device_id=dp_peer(2 * order[level]),
                    device_id_type=MESH,
                )
        if not last:
            chip_send(c, level + 1)
        elif k is not None:
            j = rel(k)
            z_copies.append(
                send(
                    final.at[slot],
                    got_z.at[g, j - 1],
                    z_send.at[g, j - 1],
                    z_recv.at[g, j - 1],
                    (d, near[k]),
                )
            )

    def finish(g):
        a = grad_ref[g]
        for j in range(1, nt):
            remote(
                final.at[0], got_z.at[g, j - 1], z_send.at[g, j - 1], z_recv.at[g, j - 1], t_peer(j)
            ).wait_recv()
            a = a + got_z[g, j - 1].astype(F32)
        grad_ref[g] = a

    def to_positions(src, dst, rows, ssem, rsem):
        for j in range(1, nt):
            there = flip(t, j)
            send(
                src.at[:, pl.ds(pl.multiple_of(there * rows, rows), rows)],
                dst.at[pl.ds(t * spd, spd)],
                ssem.at[j],
                rsem.at[j],
                t_peer(j),
            )
        return local(
            src.at[:, pl.ds(pl.multiple_of(t * rows, rows), rows)],
            dst.at[pl.ds(t * spd, spd)],
            rsem.at[0],
        )

    def positions_here(own_copy, src, dst, rows, ssem, rsem):
        own_copy.wait()
        for j in range(1, nt):
            remote(
                src.at[:, pl.ds(pl.multiple_of(t * rows, rows), rows)],
                dst.at[pl.ds(flip(t, j) * spd, spd)],
                ssem.at[j],
                rsem.at[j],
                t_peer(j),
            ).wait_recv()

    sum_peers = [dp_peer(1 << b) for b in range(bits)] + [t_peer(1 << b) for b in range(tbits)]
    sum_copies = {}

    def sum_start(i):
        sum_copies[i] = send(
            total.at[i], got_sum.at[i], sum_send.at[i], sum_recv.at[i], sum_peers[i]
        )

    def sum_finish(i):
        sum_copies[i].wait_recv()
        total[i + 1] = total[i] + got_sum[i]

    back_slot = []
    for peer in range(ndp):
        slot = 0
        for i in range(seqs):
            slot = jnp.where(lax.div(sources[i], seqs) == peer, i, slot)
        back_slot.append(slot)
    raw_loads[0].wait()
    panels[0, :, 3 * hc :] = low[...].T
    raw_loads[2] = load_raw(2)
    for copy in loads[:3]:
        copy.wait()
    own_copies = {0: local(panels.at[0], wg.at[0, 0], own_sems.at[0])}
    tok_load.wait()
    tok_copies = to_peers(zs_tok, out_slot, tx_tok, rx_tok, tok_send, tok_recv)
    line_start(0)
    enc_load.wait()
    enc_copies = to_peers(zs_enc, out_slot, tx_enc, rx_enc, enc_send, enc_recv)
    blocks_here(tok_copies, rx_tok, zs_tok)
    own_x = to_sequences(zs_tok, x_ref, lr, zt_send, zt_recv)
    raw_loads[1].wait()
    panels[1, :, 3 * hc :] = grad_low[...].T
    raw_loads[3] = load_raw(3)
    for copy in loads[3:6]:
        copy.wait()
    own_copies[1] = local(panels.at[1], wg.at[0, 1], own_sems.at[1])
    loads[6].wait()
    own_copies[2] = local(panels.at[2], wg.at[0, 2], own_sems.at[2])
    for i in range(2, 6):
        raw_loads[i].wait()
        panels[3, :, (i - 2) * hc : (i - 1) * hc] = raw[i % 2][...].T
        if i + 2 < 6:
            raw_loads[i + 2] = load_raw(i + 2)
    own_copies[3] = local(panels.at[3], wg.at[0, 3], own_sems.at[3])

    total[0] = jnp.zeros_like(total[0])
    gather_count = len(gathered)
    gather_at = [SPACING * level for level in range(levels + 1)]
    gather_at.append(gather_at[-1] + 1)
    part_at = gather_at[-1] + 1
    base = part_at + 2 * per
    depth = SPACING * (levels + 1) + 2
    feed_last = base + count // 2 - 2
    cross_last = base + 3 * count // 4 - 1
    end = base + count
    for c in range(min(Z_LEAD, gather_count)):
        line_stage(c)
    for tick in range(end + max(depth, len(sum_peers) + 3)):
        at = tick - base
        for g, c in last_of.items():
            if at - depth == c:
                finish(g)
        for level in range(levels - 1, -1, -1):
            c = at - SPACING * (level + 2)
            if 0 <= c < count:
                chip_add(c, level)
        if 0 <= at - SPACING < count:
            core_add(at - SPACING)
        for level in range(levels + 1, -1, -1):
            c = tick - gather_at[level]
            if 0 <= c < gather_count:
                spread(c, level)
        if Z_LEAD <= tick + Z_LEAD < gather_count:
            line_stage(tick + Z_LEAD)
        if tick == part_at - 1:
            blocks_here(enc_copies, rx_enc, zs_enc)
            own_ed = to_sequences(zs_enc, ed_ref, le, ze_send, ze_recv)
            sequences_here(own_x, zs_tok, x_ref, lr, zt_send, zt_recv)
            free(own_x, 0)
            self_norm()
            self_forward(0, panels.at[0])
        c = tick - part_at
        if 0 <= c < 2 * per:
            g, k = gathered[c]
            fills[c].wait()
            (self_forward if g == 0 else cross_forward)(rel(k), panels.at[2 + c % 2])
            if c == per - 1:
                sequences_here(own_ed, zs_enc, ed_ref, le, ze_send, ze_recv)
                free(own_ed, 1)
                own_cot = to_sequences(cot_hbm, cot_ref, lr, zc_send, zc_recv)
                cross_norm()
                cross_forward(0, panels.at[1])
                fetch(0)
        if tick == base:
            sequences_here(own_cot, cot_hbm, cot_ref, lr, zc_send, zc_recv)
        if at in unit_at:
            run_unit(at)
        if 0 <= at < count:
            core_send(at)
        if tick == feed_last:
            res_copy = to_positions(res_ref, res_out, lr, br_send, br_recv)
        if tick == cross_last:
            pl.semaphore_wait(left_sems.at[1], nt - 1)
            enc_copy = to_positions(ded_ref, zs_enc, le, be_send, be_recv)
        if tick == cross_last + 2:
            positions_here(enc_copy, ded_ref, zs_enc, le, be_send, be_recv)
            for copy in enc_copies[:-1]:
                sent(copy)
            enc_copies = to_peers(zs_enc, back_slot, tx_enc, back_enc, benc_send, benc_recv)
        if tick == end - 1:
            pl.semaphore_wait(left_sems.at[0], nt - 1)
            tok_copy = to_positions(dx_ref, zs_tok, lr, bt_send, bt_recv)
        if tick == end + 1:
            positions_here(tok_copy, dx_ref, zs_tok, lr, bt_send, bt_recv)
            for copy in tok_copies[:-1]:
                sent(copy)
            tok_copies = to_peers(zs_tok, back_slot, tx_tok, back_tok, btok_send, btok_recv)
        i = tick - end
        if 0 <= i - 1 < len(sum_peers):
            sum_finish(i - 1)
        if 0 <= i < len(sum_peers):
            sum_start(i)
    norm_ref[...] = total[len(sum_peers)]
    positions_here(res_copy, res_ref, res_out, lr, br_send, br_recv)
    peers_here(enc_copies)
    peers_here(tok_copies)
    for g in range(4):
        on_line(lambda copy: copy.wait_send(), g)
    for c in range(gather_count):
        on_pass(lambda copy: copy.wait_send(), c)
    for copy in started:
        copy.wait_send()


def layer(ndp, nt, spd, deal, tok_len, enc_len, tokens, enc_states, cot, weights, gain, bias):
    seqs, lr, dim = cot.shape
    le = enc_states.shape[1]
    seq, enc = nt * lr, nt * le
    n, m = spd * seq, spd * enc
    hc = weights[0].shape[1]
    width = 4 * hc
    assert n == hc and weights[8].shape[1] == width
    rows, chips = dim // ndp, ndp // 2
    half = rows // 2
    levels = chips.bit_length() - 1
    count = 4 * nt
    gathers = 4 * (nt - 1)
    steps = (ndp.bit_length() - 1) + (nt.bit_length() - 1)
    slots = 1 + 2 * (chips - 1)
    gather_slots = 2 * (chips - 1) + chips
    smem = pl.BlockSpec(memory_space=pltpu.SMEM)
    vmem = pl.BlockSpec(memory_space=pltpu.VMEM)
    any_space = pl.BlockSpec(memory_space=pl.ANY)
    dma = pltpu.SemaphoreType.DMA
    shape = jax.ShapeDtypeStruct

    def body(*refs):
        layer_kernel(ndp, nt, spd, *refs[:6], refs[6:16], *refs[16:])

    part, keys = pltpu.VMEM((nt, n, hc), BF16), pltpu.VMEM((nt, m, hc), BF16)
    tokens_low, tokens_wide = pltpu.VMEM((n, dim), BF16), pltpu.VMEM((n, dim), F32)
    sequences = pltpu.VMEM((spd, seq, dim), BF16)
    return pl.pallas_call(
        body,
        in_specs=[smem] * 3 + [any_space] * 13 + [vmem] * 2,
        out_specs=[any_space] * 4 + [vmem] * 2,
        out_shape=[
            shape((nt, 4, dim, width), BF16),
            shape((seqs, lr, dim), BF16),
            shape((ndp, lr, dim), BF16),
            shape((ndp, le, dim), BF16),
            shape((4, rows, width), F32),
            shape((8, dim), F32),
        ],
        scratch_shapes=[
            sequences,
            pltpu.VMEM((spd, enc, dim), BF16),
            sequences,
            tokens_low,
            *[part] * 4,
            tokens_wide,
            tokens_low,
            part,
            keys,
            keys,
            part,
            tokens_wide,
            tokens_low,
            pltpu.VMEM((dim, n), BF16),
            tokens_low,
            pltpu.VMEM((dim, n), BF16),
            pltpu.VMEM((dim, m), BF16),
            tokens_wide,
            pltpu.VMEM((m, dim), F32),
            tokens_wide,
            sequences,
            sequences,
            pltpu.VMEM((spd, enc, dim), BF16),
            pltpu.VMEM((n, 3 * hc), BF16),
            pltpu.VMEM((m, hc), BF16),
            pltpu.VMEM((m, hc), BF16),
            pltpu.VMEM((4, dim, width), BF16),
            pltpu.VMEM((ndp, lr, dim), BF16),
            pltpu.VMEM((ndp, le, dim), BF16),
            pltpu.VMEM((ndp, lr, dim), BF16),
            pltpu.VMEM((ndp, le, dim), BF16),
            pltpu.VMEM((seqs, lr, dim), BF16),
            pltpu.VMEM((seqs, le, dim), BF16),
            pltpu.VMEM((DW_SLOTS, chips, 2, rows, width), BF16),
            pltpu.VMEM((CORE_SLOTS, chips, rows, width), BF16),
            pltpu.VMEM((CHIP_SLOTS, 2 * (chips - 1), half, width), BF16),
            pltpu.VMEM((4, nt - 1, rows, width), BF16),
            pltpu.VMEM((SPACING * levels, chips, rows, width), BF16),
            pltpu.VMEM((Z_SLOTS, rows, width), BF16),
            pltpu.VMEM((steps + 1, 8, dim), F32),
            pltpu.VMEM((steps, 8, dim), F32),
            dma((15,)),
            dma((4,)),
            dma((4,)),
            *[dma((ndp,)) for _ in range(4)],
            *[dma((nt,)) for _ in range(6)],
            dma((4, 2)),
            dma((4, nt)),
            dma((gathers,)),
            dma((gathers, gather_slots)),
            dma((gathers, gather_slots)),
            dma((count, slots)),
            dma((count, slots)),
            dma((4, nt - 1)),
            dma((4, nt - 1)),
            dma((steps,)),
            dma((steps,)),
            *[dma((nt,)) for _ in range(6)],
            *[dma((ndp,)) for _ in range(4)],
            pltpu.SemaphoreType.REGULAR,
            pltpu.SemaphoreType.REGULAR((levels, 2)),
            pltpu.SemaphoreType.REGULAR((2,)),
        ],
        compiler_params=pltpu.CompilerParams(
            collective_id=0, has_side_effects=True, vmem_limit_bytes=VMEM_LIMIT
        ),
        name="layer",
    )(deal, tok_len, enc_len, tokens, enc_states, cot, *weights, gain, bias)


def tail_kernel(seqs, deal_ref, res, rx_tok, rx_enc, grads, norm, *outs):
    d = lax.axis_index("dp")
    result, d_tok, d_enc = outs[:3]
    hc = outs[3].shape[1]
    result[...] = res[...]
    for i in range(seqs):
        peer = 0
        for k in range(rx_tok.shape[0]):
            peer = jnp.where(deal_ref[k * seqs + i] == d * seqs + i, k, peer)
        d_tok[i] = rx_tok[peer]
        d_enc[i] = rx_enc[peer]
    for g in range(2):
        for i in range(3):
            outs[3 + 4 * g + i][...] = grads[g, :, i * hc : (i + 1) * hc]
        outs[6 + 4 * g][...] = grads[g, :, 3 * hc :].T
    outs[11][...] = grads[2]
    outs[12][...] = grads[3].T
    outs[13][...] = norm[0:3]
    outs[14][...] = norm[3:6]


def tail(deal, res, rx_tok, rx_enc, grads, norm):
    seqs, lr, dim = res.shape
    le = rx_enc.shape[1]
    rows, width = grads.shape[1:]
    hc = width // 4
    vmem = pl.BlockSpec(memory_space=pltpu.VMEM)
    straight, turned = ((rows, hc), F32), ((hc, rows), F32)
    shapes = [((seqs, lr, dim), BF16), ((seqs, lr, dim), BF16), ((seqs, le, dim), BF16)]
    shapes += ([straight] * 3 + [turned]) * 2
    shapes += [((rows, width), F32), ((width, rows), F32), ((3, dim), F32), ((3, dim), F32)]
    return pl.pallas_call(
        functools.partial(tail_kernel, seqs),
        in_specs=[pl.BlockSpec(memory_space=pltpu.SMEM)] + [vmem] * 5,
        out_specs=[vmem] * len(shapes),
        out_shape=[jax.ShapeDtypeStruct(*one) for one in shapes],
        compiler_params=pltpu.CompilerParams(vmem_limit_bytes=VMEM_LIMIT),
        name="tail",
    )(deal, res, rx_tok, rx_enc, grads, norm)


def per_device(ndp, nt, tokens, enc_states, cotangent, tok_len, enc_len, deal, *rest):
    *weights, gain, bias = rest
    spd = tokens.shape[0] // nt
    _, *made = layer(
        ndp, nt, spd, deal, tok_len, enc_len, tokens, enc_states, cotangent, weights, gain, bias
    )
    return tail(deal, *made)


def solution(mesh):
    ndp, nt = mesh.shape["dp"], mesh.shape["tensor"]
    rows = P("dp", "tensor", None)
    columns = P(None, "tensor")
    split = P("tensor", None)
    grad = P("dp", "tensor")
    turned = P("tensor", "dp")
    return jax.shard_map(
        functools.partial(per_device, ndp, nt),
        mesh=mesh,
        in_specs=(
            (rows,) * 3
            + (P(),) * 3
            + (columns, columns, columns, split) * 2
            + (columns, split, P(), P())
        ),
        out_specs=(
            (rows,) * 3 + (grad, grad, grad, turned) * 2 + (grad, turned) + (P(), P())
        ),
        check_vma=False,
    )
```

```python
import functools

import jax
import jax.numpy as jnp
from jax import lax
from jax.experimental import pallas as pl
from jax.experimental.pallas import tpu as pltpu
from jax.sharding import PartitionSpec as P

HEAD_DIM = 64
SCALE = 0.125
MASKED = -1e30
EPSILON = 1e-05
MESH = pl.DeviceIdType.MESH
VMEM_LIMIT = 60 * 1024 * 1024
CORE_SLOTS = 3
CHIP_SLOTS = 4
DW_SLOTS = 2
Z_SLOTS = 4
GATHER_GAP = 2
CORE_GAP = 1
CHIP_GAP = 2
Z_LEAD = 1
BF16 = jnp.bfloat16
F32 = jnp.float32


def dot_nn(a, b):
    return lax.dot_general(a, b, (((1,), (0,)), ((), ())), preferred_element_type=F32)


def dot_nt(a, b):
    return lax.dot_general(a, b, (((1,), (1,)), ((), ())), preferred_element_type=F32)


def dot_tn(a, b):
    return lax.dot_general(a, b, (((0,), (0,)), ((), ())), preferred_element_type=F32)


def norm_parts(v):
    mu = jnp.mean(v, axis=-1, keepdims=True)
    var = jnp.mean(v * v, axis=-1, keepdims=True) - mu * mu
    rstd = lax.rsqrt(var + EPSILON)
    return (v - mu) * rstd, rstd


def norm_back(dn, nh, rstd, gain):
    c = dn * gain
    return rstd * (
        c - jnp.mean(c, axis=-1, keepdims=True) - nh * jnp.mean(c * nh, axis=-1, keepdims=True)
    )


def head_stack(a, heads):
    lane = lax.broadcasted_iota(jnp.int32, a.shape, 1) // HEAD_DIM
    zero = jnp.zeros_like(a)
    return jnp.concatenate([jnp.where(lane == h, a, zero) for h in range(heads)], axis=0)


def attn_probs(q, k, limit, causal):
    heads = q.shape[1] // HEAD_DIM
    qs = head_stack(q, heads)
    s = dot_nt(qs, k) * SCALE
    key = lax.broadcasted_iota(jnp.int32, s.shape, 1)
    allowed = key < limit
    if causal:
        row = lax.rem(lax.broadcasted_iota(jnp.int32, s.shape, 0), q.shape[0])
        allowed = allowed & (key <= row)
    s = jnp.where(allowed, s, MASKED)
    e = jnp.exp(s - jnp.max(s, axis=-1, keepdims=True))
    return qs, e / jnp.sum(e, axis=-1, keepdims=True)


def lane_stack(a, heads):
    rows = a.shape[0] // heads
    return jnp.concatenate([a[h * rows : (h + 1) * rows] for h in range(heads)], axis=1)


def attn_fwd(q, k, v, limit, causal):
    heads = q.shape[1] // HEAD_DIM
    _, p = attn_probs(q, k, limit, causal)
    return dot_nn(lane_stack(p.astype(BF16), heads), head_stack(v, heads)).astype(BF16)


def attn_bwd(q, k, v, do, limit, causal):
    heads = q.shape[1] // HEAD_DIM
    qs, p = attn_probs(q, k, limit, causal)
    dos = head_stack(do, heads)
    dp = dot_nt(dos, v)
    delta = jnp.sum(p * dp, axis=-1, keepdims=True)
    ds = (p * (dp - delta) * SCALE).astype(BF16)
    dq = dot_nn(lane_stack(ds, heads), head_stack(k, heads)).astype(BF16)
    dk = dot_tn(ds, qs).astype(BF16)
    dv = dot_tn(p.astype(BF16), dos).astype(BF16)
    return dq, dk, dv


def row_valid(lens, spd, n):
    row = lax.broadcasted_iota(jnp.int32, (n, 1), 0)
    seq = n // spd
    end = jnp.full((n, 1), lens[0], jnp.int32)
    for i in range(1, spd):
        end = jnp.where(row >= i * seq, i * seq + lens[i], end)
    return row < end


def flip(index, mask):
    out = index
    bit = 1
    while bit <= mask:
        if mask & bit:
            out = out + bit - 2 * bit * lax.rem(lax.div(index, bit), 2)
        bit *= 2
    return out


def xor_of(a, b, size):
    out = 0
    bit = 1
    while bit < size:
        out = out + bit * lax.rem(lax.div(a, bit) + lax.div(b, bit), 2)
        bit *= 2
    return out


def nearest(t, nt):
    out = []
    for k in range(nt - 1):
        at = 0
        for place in range(nt):
            others = [s for s in range(nt) if s != place]
            others.sort(key=lambda s: (abs(s - place), s ^ place))
            at = jnp.where(t == place, others[k], at)
        out.append(at)
    return out


def greet(peers):
    barrier = pltpu.get_barrier_semaphore()
    for peer in peers:
        pl.semaphore_signal(barrier, inc=1, device_id=peer, device_id_type=MESH)
    pl.semaphore_wait(barrier, len(peers))


def layer_kernel(
    ndp,
    nt,
    spd,
    deal_ref,
    tok_len_ref,
    enc_len_ref,
    tok_hbm,
    enc_hbm,
    cot_hbm,
    w_refs,
    gain,
    bias,
    wg,
    res_out,
    back_tok,
    back_enc,
    grad_ref,
    norm_ref,
    x_ref,
    ed_ref,
    cot_ref,
    n1_ref,
    q1_ref,
    k1_ref,
    v1_ref,
    o1_ref,
    h1_ref,
    n2_ref,
    q2_ref,
    k2_ref,
    v2_ref,
    o2_ref,
    h2_ref,
    low,
    low_t,
    grad_low,
    grad_low_t,
    edt,
    dn_acc,
    ded_acc,
    dh_ref,
    res_ref,
    dx_ref,
    ded_ref,
    dq,
    dk,
    dv,
    panels,
    tx_tok,
    tx_enc,
    rx_tok,
    rx_enc,
    zs_tok,
    zs_enc,
    dw,
    got_core,
    got_chip,
    got_z,
    work,
    final,
    total,
    got_sum,
    load_sems,
    own_sems,
    panel_sems,
    tok_send,
    tok_recv,
    enc_send,
    enc_recv,
    zt_send,
    zt_recv,
    ze_send,
    ze_recv,
    zc_send,
    zc_recv,
    line_send,
    line_recv,
    pass_send,
    gather_send,
    gather_recv,
    send_sems,
    recv_sems,
    z_send,
    z_recv,
    sum_send,
    sum_recv,
    br_send,
    br_recv,
    bt_send,
    bt_recv,
    be_send,
    be_recv,
    btok_send,
    btok_recv,
    benc_send,
    benc_recv,
    core_credit,
    chip_credit,
    left_sems,
):
    d = lax.axis_index("dp")
    t = lax.axis_index("tensor")
    dim, width = panels.shape[1:]
    hc = width // 4
    rows_each = dim // ndp
    half = rows_each // 2
    bits = ndp.bit_length() - 1
    tbits = nt.bit_length() - 1
    chips = ndp // 2
    core = lax.rem(d, 2)
    chip = lax.div(d, 2)
    chip_bits = [1 << b for b in range(bits - 1)]
    orders = (chip_bits, chip_bits[::-1])
    levels = len(chip_bits)
    work_slots = work.shape[0]
    seqs, lr = cot_hbm.shape[0], cot_hbm.shape[1]
    le = enc_hbm.shape[1]
    seq, enc = nt * lr, nt * le
    n, m = spd * seq, spd * enc
    out_acc = dh_ref
    near = nearest(t, nt)
    sources = [deal_ref[d * seqs + i] for i in range(seqs)]
    tok_lens = [tok_len_ref[deal_ref[d * seqs + t * spd + i]] for i in range(spd)]
    enc_lens = [enc_len_ref[deal_ref[d * seqs + t * spd + i]] for i in range(spd)]
    started = []

    def dp_peer(bit):
        return (flip(d, bit), t)

    def t_peer(j):
        return (d, flip(t, j))

    def rel(k):
        return 0 if k is None else xor_of(near[k], t, nt)

    def slab(index, side=None):
        if side is None:
            return pl.ds(pl.multiple_of(index * rows_each, rows_each), rows_each)
        return pl.ds(pl.multiple_of(index * rows_each + side * half, half), half)

    def remote(src, dst, ssem, rsem, peer):
        return pltpu.make_async_remote_copy(
            src_ref=src,
            dst_ref=dst,
            send_sem=ssem,
            recv_sem=rsem,
            device_id=peer,
            device_id_type=MESH,
        )

    def send(*args):
        copy = remote(*args)
        copy.start()
        started.append(copy)
        return copy

    def sent(copy):
        copy.wait_send()
        started[:] = [one for one in started if one is not copy]

    def local(src, dst, sem):
        copy = pltpu.make_async_copy(src, dst, sem)
        copy.start()
        return copy

    wq1, wk1, wv1, wo1, wq2, wk2, wv2, wo2, w_in, w_out = w_refs
    tok_load = local(tok_hbm, zs_tok, load_sems.at[0])
    raw = [low, grad_low]

    def load_raw(i):
        src = [wo1, wo2] + [w_out.at[pl.ds(b * hc, hc)] for b in range(4)]
        return local(src[i], raw[i % 2], load_sems.at[2 + i])

    raw_loads = {0: load_raw(0)}
    loads = [
        local(src, panels.at[g, :, pl.ds(i * hc, hc)], load_sems.at[8 + 3 * g + i])
        for g, three in enumerate(((wq1, wk1, wv1), (wq2, wk2, wv2)))
        for i, src in enumerate(three)
    ]
    enc_load = local(enc_hbm, zs_enc, load_sems.at[1])
    raw_loads[1] = load_raw(1)
    loads.append(local(w_in, panels.at[2], load_sems.at[14]))
    out_slot = []
    for k in range(ndp):
        slot = 0
        for i in range(seqs):
            slot = jnp.where(deal_ref[k * seqs + i] == d * seqs + i, i, slot)
        out_slot.append(slot)
    greet([dp_peer(e) for e in range(1, ndp)] + [t_peer(j) for j in range(1, nt)])

    def to_peers(held, slots, blocks, rx, ssem, rsem):
        for k in range(ndp):
            blocks[k] = held[slots[k]]
        return [
            send(blocks.at[flip(d, e)], rx.at[d], ssem.at[e], rsem.at[e], dp_peer(e))
            for e in range(1, ndp)
        ] + [local(blocks.at[d], rx.at[d], rsem.at[0])]

    def peers_here(copies):
        for copy in copies[:-1]:
            copy.wait_recv()
        copies[-1].wait()

    def blocks_here(copies, rx, zs):
        peers_here(copies)
        for i in range(seqs):
            zs[i] = rx[lax.div(sources[i], seqs)]

    def to_sequences(src, dst, rows, ssem, rsem):
        span = pl.ds(pl.multiple_of(t * rows, rows), rows)
        copies = [
            send(
                src.at[pl.ds(flip(t, j) * spd, spd)],
                dst.at[:, span],
                ssem.at[j],
                rsem.at[j],
                t_peer(j),
            )
            for j in range(1, nt)
        ]
        return copies + [local(src.at[pl.ds(t * spd, spd)], dst.at[:, span], rsem.at[0])]

    def free(copies, which):
        for copy in copies[:-1]:
            sent(copy)
        for j in range(1, nt):
            pl.semaphore_signal(
                left_sems.at[which], inc=1, device_id=t_peer(j), device_id_type=MESH
            )

    def sequences_here(copies, src, dst, rows, ssem, rsem):
        copies[-1].wait()
        for j in range(1, nt):
            there = flip(t, j)
            remote(
                src.at[pl.ds(t * spd, spd)],
                dst.at[:, pl.ds(pl.multiple_of(there * rows, rows), rows)],
                ssem.at[j],
                rsem.at[j],
                t_peer(j),
            ).wait_recv()

    gathered = [(g, k) for g in range(2) for k in range(nt - 1)]
    gathered += [(g, k) for k in range(nt - 1) for g in (2, 3)]

    def line_copy(g, step):
        there = t + step
        j = xor_of(t, there, nt)
        return remote(
            wg.at[0, g, slab(d)],
            wg.at[j, g, slab(d)],
            line_send.at[g, (step + 1) // 2],
            line_recv.at[g, j],
            (d, there),
        )

    def pass_copy(c, step):
        g, k = gathered[c]
        there = t + step
        j_there = xor_of(near[k], there, nt)
        return remote(
            wg.at[rel(k), g, slab(d)],
            wg.at[j_there, g, slab(d)],
            pass_send.at[c],
            line_recv.at[g, j_there],
            (d, there),
        )

    def on_line(act, g):
        @pl.when(t + 1 < nt)
        def _():
            act(line_copy(g, 1))

        @pl.when(t >= 1)
        def _():
            act(line_copy(g, -1))

    def on_pass(act, c):
        s = near[gathered[c][1]]

        @pl.when((s < t) & (t + 1 < nt))
        def _():
            act(pass_copy(c, 1))

        @pl.when((s > t) & (t >= 1))
        def _():
            act(pass_copy(c, -1))

    def start(copy):
        copy.start()

    def line_start(g):
        own_copies[g].wait()
        on_line(start, g)

    per = nt - 1
    line_after = {min(1, per - 1): 1, per + min(1, per - 1): 2, 2 * per - 1: 3}

    def line_stage(c):
        g, k = gathered[c]
        j = rel(k)
        at = wg.at[j, g, slab(d)]
        remote(at, at, pass_send.at[c], line_recv.at[g, j], (d, near[k])).wait_recv()
        on_pass(start, c)
        if c in line_after:
            line_start(line_after[c])

    pending = {}
    fills = {}

    def spread(c, level):
        g, k = gathered[c]
        j = rel(k)
        if level:
            for copy in pending.pop((c, level)):
                copy.wait_recv()
        slot = 2 * ((1 << level) - 1)
        copies = []
        if level < levels:
            for side, order in enumerate(orders):
                held = [0]
                for bit in order[:level]:
                    held += [e ^ bit for e in held]
                for e in held:
                    at = wg.at[j, g, slab(flip(d, 2 * e), side)]
                    sems = gather_send.at[c, slot], gather_recv.at[c, slot]
                    copies.append(send(at, at, *sems, dp_peer(2 * order[level])))
                    slot += 1
        elif level == levels:
            for e in range(0, ndp, 2):
                at = wg.at[j, g, slab(flip(d, e))]
                sems = gather_send.at[c, slot], gather_recv.at[c, slot]
                copies.append(send(at, at, *sems, dp_peer(1)))
                slot += 1
        elif g < 2:
            slot = 2 + c % 2
            fills[c] = local(wg.at[j, g], panels.at[slot], panel_sems.at[slot])
        if copies:
            pending[(c, level + 1)] = copies

    def self_norm():
        x = x_ref[...].reshape(n, dim).astype(F32)
        nh, _ = norm_parts(x)
        n1_ref[...] = (nh * gain[0:1] + bias[0:1]).astype(BF16)
        h1_ref[...] = x

    def self_forward(j, w):
        qkv = dot_nn(n1_ref[...], w[:, : 3 * hc]).astype(BF16)
        q1_ref[j] = qkv[:, :hc]
        k1_ref[j] = qkv[:, hc : 2 * hc]
        v1_ref[j] = qkv[:, 2 * hc :]
        for i in range(spd):
            rows = slice(i * seq, (i + 1) * seq)
            o1_ref[j, rows] = attn_fwd(
                q1_ref[j, rows], k1_ref[j, rows], v1_ref[j, rows], tok_lens[i], True
            )
        h1_ref[...] += dot_nt(o1_ref[j], w[:, 3 * hc :])

    def cross_norm():
        h = h1_ref[...]
        nh, _ = norm_parts(h)
        n2_ref[...] = (nh * gain[1:2] + bias[1:2]).astype(BF16)
        h2_ref[...] = h

    def cross_forward(j, w):
        q2_ref[j] = dot_nn(n2_ref[...], w[:, :hc]).astype(BF16)
        kv = dot_nn(ed_ref[...].reshape(m, dim), w[:, hc : 3 * hc]).astype(BF16)
        k2_ref[j] = kv[:, :hc]
        v2_ref[j] = kv[:, hc:]
        for i in range(spd):
            rows = slice(i * seq, (i + 1) * seq)
            keys = slice(i * enc, (i + 1) * enc)
            o2_ref[j, rows] = attn_fwd(
                q2_ref[j, rows], k2_ref[j, keys], v2_ref[j, keys], enc_lens[i], False
            )
        h2_ref[...] += dot_nt(o2_ref[j], w[:, 3 * hc :])

    def low_bit(j):
        return j & -j

    others = sorted(range(1, nt), key=lambda j: (low_bit(j), j))
    units = [("feed", j) for j in [0] + others]
    units += [("cross", j) for j in others + [0]] + [("self", j) for j in others + [0]]
    made = {"feed": (3, 2), "cross": (1,), "self": (0,)}
    chunks = []
    unit_at = {}
    for u, (kind, j) in enumerate(units):
        unit_at[len(chunks)] = u
        chunks += [(g, j) for g in made[kind]]
    count = len(chunks)
    last_of = {g: c for c, (g, _) in enumerate(chunks)}
    fetched = {}

    def fetch(u):
        if u < len(units):
            kind, j = units[u]
            fetched[u] = [
                local(
                    wg.at[j, g],
                    panels.at[2 * (u % 2) + i],
                    panel_sems.at[2 * (u % 2) + i],
                )
                for i, g in enumerate(made[kind])
            ]

    def put(c, column, a, b):
        cols = b.shape[1]
        for e in range(chips):
            part = dot_nn(a[2 * e * rows_each : 2 * (e + 1) * rows_each], b)
            dw[c % DW_SLOTS, e, :, :, column : column + cols] = part.astype(BF16).reshape(
                2, rows_each, cols
            )

    def feed_init():
        nh, _ = norm_parts(h2_ref[...])
        v = nh * gain[2:3] + bias[2:3]
        low[...] = v.astype(BF16)
        low_t[...] = v.T.astype(BF16)
        keep = row_valid(tok_lens, spd, n)
        dh = jnp.where(keep, cot_ref[...].reshape(n, dim).astype(F32), 0.0)
        grad_low[...] = dh.astype(BF16)
        grad_low_t[...] = dh.T.astype(BF16)
        out_acc[...] = jnp.zeros_like(out_acc)
        dn_acc[...] = jnp.zeros_like(dn_acc)

    def feed_part(c, wout_ref, win_ref):
        block = min(512, width)
        for at in range(0, width, block):
            win = win_ref[:, at : at + block]
            wout = wout_ref[:, at : at + block]
            u = dot_nn(low[...], win)
            ga = dot_nn(grad_low[...], wout)
            sg = 1.0 / (1.0 + jnp.exp(-u))
            r = (u * sg).astype(BF16)
            du = (ga * (sg * (1.0 + u * (1.0 - sg)))).astype(BF16)
            out_acc[...] += dot_nt(r, wout)
            dn_acc[...] += dot_nt(du, win)
            put(c, at, grad_low_t, r)
            put(c + 1, at, low_t, du)

    def norm_grads(row, v, gain_row):
        nh, rstd = norm_parts(v)
        dn = dn_acc[...]
        total[0, row : row + 1] = jnp.sum(dn * nh, axis=0, keepdims=True)
        total[0, 3 + row : 4 + row] = jnp.sum(dn, axis=0, keepdims=True)
        return norm_back(dn, nh, rstd, gain_row)

    def feed_end():
        keep = row_valid(tok_lens, spd, n)
        h2 = h2_ref[...]
        res = jnp.where(keep, h2 + out_acc[...], 0.0).astype(BF16)
        res_ref[...] = res.reshape(spd, seq, dim)
        dh = jnp.where(keep, cot_ref[...].reshape(n, dim).astype(F32), 0.0)
        dh_ref[...] = dh + norm_grads(2, h2, gain[2:3])

    def branch_init(kept):
        dh = dh_ref[...]
        grad_low[...] = dh.astype(BF16)
        grad_low_t[...] = dh.T.astype(BF16)
        low_t[...] = kept[...].T
        dn_acc[...] = jnp.zeros_like(dn_acc)

    def cross_init():
        branch_init(n2_ref)
        edt[...] = ed_ref[...].reshape(m, dim).T
        ded_acc[...] = jnp.zeros_like(ded_acc)

    def cross_backward(c, j, w):
        do = dot_nn(grad_low[...], w[:, 3 * hc :]).astype(BF16)
        for i in range(spd):
            rows = slice(i * seq, (i + 1) * seq)
            keys = slice(i * enc, (i + 1) * enc)
            dq[rows, :hc], dk[keys], dv[keys] = attn_bwd(
                q2_ref[j, rows], k2_ref[j, keys], v2_ref[j, keys], do[rows], enc_lens[i], False
            )
        dn_acc[...] += dot_nt(dq[:, :hc], w[:, :hc])
        ded_acc[...] += dot_nt(dk[...], w[:, hc : 2 * hc]) + dot_nt(dv[...], w[:, 2 * hc : 3 * hc])
        put(c, 0, low_t, dq[:, :hc])
        put(c, hc, edt, dk[...])
        put(c, 2 * hc, edt, dv[...])
        put(c, 3 * hc, grad_low_t, o2_ref[j])

    def cross_end():
        ded_ref[...] = ded_acc[...].astype(BF16).reshape(spd, enc, dim)
        dh_ref[...] += norm_grads(1, h1_ref[...], gain[1:2])

    def self_init():
        branch_init(n1_ref)

    def self_backward(c, j, w):
        do = dot_nn(grad_low[...], w[:, 3 * hc :]).astype(BF16)
        for i in range(spd):
            rows = slice(i * seq, (i + 1) * seq)
            dq[rows, :hc], dq[rows, hc : 2 * hc], dq[rows, 2 * hc :] = attn_bwd(
                q1_ref[j, rows], k1_ref[j, rows], v1_ref[j, rows], do[rows], tok_lens[i], True
            )
        dn_acc[...] += dot_nt(dq[...], w[:, : 3 * hc])
        put(c, 0, low_t, dq[...])
        put(c, 3 * hc, grad_low_t, o1_ref[j])

    def self_end():
        x = x_ref[...].reshape(n, dim).astype(F32)
        dx = dh_ref[...] + norm_grads(0, x, gain[0:1])
        dx_ref[...] = dx.astype(BF16).reshape(spd, seq, dim)

    def run_unit(c):
        u = unit_at[c]
        kind, j = units[u]
        for i in range(len(made[kind])):
            if c + i >= DW_SLOTS:
                sent(core_copies[c + i - DW_SLOTS])
        if 1 < u < nt:
            fetch(u)
        for copy in fetched.pop(u):
            copy.wait()
        if not 1 < u + 1 < nt:
            fetch(u + 1)
        w = panels.at[2 * (u % 2)]
        first, last = u % nt == 0, u % nt == nt - 1
        if kind == "feed":
            if first:
                feed_init()
            feed_part(c, w, panels.at[2 * (u % 2) + 1])
            if last:
                feed_end()
        elif kind == "cross":
            if first:
                cross_init()
            cross_backward(c, j, w)
            if last:
                cross_end()
        else:
            if first:
                self_init()
            self_backward(c, j, w)
            if last:
                self_end()

    core_copies = {}
    chip_copies = {}
    z_copies = []

    def core_send(c):
        if c >= CORE_SLOTS:
            pl.semaphore_wait(core_credit, 1)
        core_copies[c] = send(
            dw.at[c % DW_SLOTS, :, 1 - core],
            got_core.at[c % CORE_SLOTS],
            send_sems.at[c, 0],
            recv_sems.at[c, 0],
            dp_peer(1),
        )

    def core_add(c):
        core_copies[c].wait_recv()
        if c >= work_slots:
            for level in range(levels):
                for copy in chip_copies.pop((c - work_slots, level)):
                    sent(copy)

        def body(e, carry):
            a = dw[c % DW_SLOTS, e, core] + got_core[c % CORE_SLOTS, e]
            work[c % work_slots, e] = a
            return carry

        lax.fori_loop(0, chips, body, 0)
        if c + CORE_SLOTS < count:
            pl.semaphore_signal(core_credit, inc=1, device_id=dp_peer(1), device_id_type=MESH)
        chip_send(c, 0)

    def rest_of(order, level):
        rest = [0]
        for bit in order[level + 1 :]:
            rest += [e ^ bit for e in rest]
        return rest

    def chip_send(c, level):
        base = 2 * (chips - (chips >> level))
        copies = []
        for side, order in enumerate(orders):
            if c >= CHIP_SLOTS:
                pl.semaphore_wait(chip_credit.at[level, side], 1)
            for e in rest_of(order, level):
                at = base + len(copies)
                copies.append(
                    send(
                        work.at[
                            c % work_slots,
                            flip(chip, order[level] ^ e),
                            pl.ds(side * half, half),
                        ],
                        got_chip.at[c % CHIP_SLOTS, at],
                        send_sems.at[c, 1 + at],
                        recv_sems.at[c, 1 + at],
                        dp_peer(2 * order[level]),
                    )
                )
        chip_copies[(c, level)] = copies

    def chip_add(c, level):
        at = 2 * (chips - (chips >> level))
        g, j = chunks[c]
        copies = iter(chip_copies[(c, level)])
        last = level == levels - 1
        if last and j:
            slot = len(z_copies) % Z_SLOTS
            if len(z_copies) >= Z_SLOTS:
                sent(z_copies[len(z_copies) - Z_SLOTS])
        for side, order in enumerate(orders):
            span = pl.ds(side * half, half)
            for e in rest_of(order, level):
                next(copies).wait_recv()
                place = flip(chip, e)
                a = work[c % work_slots, place, span]
                b = got_chip[c % CHIP_SLOTS, at]
                at += 1
                if not last:
                    work[c % work_slots, place, span] = a + b
                elif j:
                    final[slot, span] = a + b
                else:
                    grad_ref[g, span] = a.astype(F32) + b.astype(F32)
            if c + CHIP_SLOTS < count:
                pl.semaphore_signal(
                    chip_credit.at[level, side],
                    inc=1,
                    device_id=dp_peer(2 * order[level]),
                    device_id_type=MESH,
                )
        if not last:
            chip_send(c, level + 1)
        elif j:
            if low_bit(j) > 1:
                final[slot] = with_others(final[slot].astype(F32), g, j).astype(BF16)
            z_copies.append(z_copy(slot, g, j))
            z_copies[-1].start()
            started.append(z_copies[-1])

    def z_copy(slot, g, j):
        sems = z_send.at[g, j - 1], z_recv.at[g, j - 1]
        return remote(final.at[slot], got_z.at[g, j - 1], *sems, t_peer(low_bit(j)))

    def with_others(a, g, j):
        bit = 1
        while bit < (low_bit(j) or nt):
            z_copy(0, g, j | bit).wait_recv()
            a = a + got_z[g, (j | bit) - 1].astype(F32)
            bit *= 2
        return a

    def finish(g):
        grad_ref[g] = with_others(grad_ref[g], g, 0)

    def to_positions(src, dst, rows, ssem, rsem):
        for j in range(1, nt):
            there = flip(t, j)
            send(
                src.at[:, pl.ds(pl.multiple_of(there * rows, rows), rows)],
                dst.at[pl.ds(t * spd, spd)],
                ssem.at[j],
                rsem.at[j],
                t_peer(j),
            )
        return local(
            src.at[:, pl.ds(pl.multiple_of(t * rows, rows), rows)],
            dst.at[pl.ds(t * spd, spd)],
            rsem.at[0],
        )

    def positions_here(own_copy, src, dst, rows, ssem, rsem):
        own_copy.wait()
        for j in range(1, nt):
            remote(
                src.at[:, pl.ds(pl.multiple_of(t * rows, rows), rows)],
                dst.at[pl.ds(flip(t, j) * spd, spd)],
                ssem.at[j],
                rsem.at[j],
                t_peer(j),
            ).wait_recv()

    sum_peers = [dp_peer(1 << b) for b in range(bits)] + [t_peer(1 << b) for b in range(tbits)]
    sum_copies = {}

    def sum_start(i):
        sum_copies[i] = send(
            total.at[i], got_sum.at[i], sum_send.at[i], sum_recv.at[i], sum_peers[i]
        )

    def sum_finish(i):
        sum_copies[i].wait_recv()
        total[i + 1] = total[i] + got_sum[i]

    back_slot = []
    for peer in range(ndp):
        slot = 0
        for i in range(seqs):
            slot = jnp.where(lax.div(sources[i], seqs) == peer, i, slot)
        back_slot.append(slot)
    raw_loads[0].wait()
    panels[0, :, 3 * hc :] = low[...].T
    raw_loads[2] = load_raw(2)
    for copy in loads[:3]:
        copy.wait()
    own_copies = {0: local(panels.at[0], wg.at[0, 0], own_sems.at[0])}
    tok_load.wait()
    tok_copies = to_peers(zs_tok, out_slot, tx_tok, rx_tok, tok_send, tok_recv)
    line_start(0)
    enc_load.wait()
    enc_copies = to_peers(zs_enc, out_slot, tx_enc, rx_enc, enc_send, enc_recv)
    blocks_here(tok_copies, rx_tok, zs_tok)
    own_x = to_sequences(zs_tok, x_ref, lr, zt_send, zt_recv)
    raw_loads[1].wait()
    panels[1, :, 3 * hc :] = grad_low[...].T
    raw_loads[3] = load_raw(3)
    for copy in loads[3:6]:
        copy.wait()
    own_copies[1] = local(panels.at[1], wg.at[0, 1], own_sems.at[1])
    loads[6].wait()
    own_copies[2] = local(panels.at[2], wg.at[0, 2], own_sems.at[2])
    for i in range(2, 6):
        raw_loads[i].wait()
        panels[3, :, (i - 2) * hc : (i - 1) * hc] = raw[i % 2][...].T
        if i + 2 < 6:
            raw_loads[i + 2] = load_raw(i + 2)
    own_copies[3] = local(panels.at[3], wg.at[0, 3], own_sems.at[3])

    total[0] = jnp.zeros_like(total[0])
    gather_count = len(gathered)
    gather_at = [GATHER_GAP * level for level in range(levels + 1)]
    gather_at.append(gather_at[-1] + 1)
    part_at = gather_at[-1] + 1
    base = max(part_at + 2 * per, gather_count + gather_at[-1] - 5)
    depth = CORE_GAP + CHIP_GAP * levels + 2
    feed_last = base + count // 2 - 2
    cross_last = base + 3 * count // 4 - 1
    end = base + count
    for c in range(min(Z_LEAD, gather_count)):
        line_stage(c)
    for tick in range(end + max(depth, len(sum_peers) + 3)):
        at = tick - base
        for g, c in last_of.items():
            if at - depth == c:
                finish(g)
        for level in range(levels - 1, -1, -1):
            c = at - CORE_GAP - CHIP_GAP * (level + 1)
            if 0 <= c < count:
                chip_add(c, level)
        if 0 <= at - CORE_GAP < count:
            core_add(at - CORE_GAP)
        for level in range(levels + 1, -1, -1):
            c = tick - gather_at[level]
            if 0 <= c < gather_count:
                spread(c, level)
        if Z_LEAD <= tick + Z_LEAD < gather_count:
            line_stage(tick + Z_LEAD)
        if tick == part_at - 1:
            blocks_here(enc_copies, rx_enc, zs_enc)
            own_ed = to_sequences(zs_enc, ed_ref, le, ze_send, ze_recv)
            sequences_here(own_x, zs_tok, x_ref, lr, zt_send, zt_recv)
            free(own_x, 0)
            self_norm()
            self_forward(0, panels.at[0])
        c = tick - part_at
        if 0 <= c < 2 * per:
            g, k = gathered[c]
            fills[c].wait()
            (self_forward if g == 0 else cross_forward)(rel(k), panels.at[2 + c % 2])
            if c == per - 1:
                sequences_here(own_ed, zs_enc, ed_ref, le, ze_send, ze_recv)
                free(own_ed, 1)
                own_cot = to_sequences(cot_hbm, cot_ref, lr, zc_send, zc_recv)
                cross_norm()
                cross_forward(0, panels.at[1])
                fetch(0)
        if tick == base:
            sequences_here(own_cot, cot_hbm, cot_ref, lr, zc_send, zc_recv)
        if at in unit_at:
            run_unit(at)
        if 0 <= at < count:
            core_send(at)
        if tick == feed_last:
            res_copy = to_positions(res_ref, res_out, lr, br_send, br_recv)
        if tick == cross_last:
            pl.semaphore_wait(left_sems.at[1], nt - 1)
            enc_copy = to_positions(ded_ref, zs_enc, le, be_send, be_recv)
        if tick == cross_last + 2:
            positions_here(enc_copy, ded_ref, zs_enc, le, be_send, be_recv)
            for copy in enc_copies[:-1]:
                sent(copy)
            enc_copies = to_peers(zs_enc, back_slot, tx_enc, back_enc, benc_send, benc_recv)
        if tick == end - 1:
            pl.semaphore_wait(left_sems.at[0], nt - 1)
            tok_copy = to_positions(dx_ref, zs_tok, lr, bt_send, bt_recv)
        if tick == end + 1:
            positions_here(tok_copy, dx_ref, zs_tok, lr, bt_send, bt_recv)
            for copy in tok_copies[:-1]:
                sent(copy)
            tok_copies = to_peers(zs_tok, back_slot, tx_tok, back_tok, btok_send, btok_recv)
        i = tick - end
        if 0 <= i - 1 < len(sum_peers):
            sum_finish(i - 1)
        if 0 <= i < len(sum_peers):
            sum_start(i)
    norm_ref[...] = total[len(sum_peers)]
    positions_here(res_copy, res_ref, res_out, lr, br_send, br_recv)
    peers_here(enc_copies)
    peers_here(tok_copies)
    for g in range(4):
        on_line(lambda copy: copy.wait_send(), g)
    for c in range(gather_count):
        on_pass(lambda copy: copy.wait_send(), c)
    for copy in started:
        copy.wait_send()


def layer(ndp, nt, spd, deal, tok_len, enc_len, tokens, enc_states, cot, weights, gain, bias):
    seqs, lr, dim = cot.shape
    le = enc_states.shape[1]
    seq, enc = nt * lr, nt * le
    n, m = spd * seq, spd * enc
    hc = weights[0].shape[1]
    width = 4 * hc
    assert n == hc and weights[8].shape[1] == width
    rows, chips = dim // ndp, ndp // 2
    half = rows // 2
    levels = chips.bit_length() - 1
    count = 4 * nt
    gathers = 4 * (nt - 1)
    steps = (ndp.bit_length() - 1) + (nt.bit_length() - 1)
    slots = 1 + 2 * (chips - 1)
    gather_slots = 2 * (chips - 1) + chips
    smem = pl.BlockSpec(memory_space=pltpu.SMEM)
    vmem = pl.BlockSpec(memory_space=pltpu.VMEM)
    any_space = pl.BlockSpec(memory_space=pl.ANY)
    dma = pltpu.SemaphoreType.DMA
    shape = jax.ShapeDtypeStruct

    def body(*refs):
        layer_kernel(ndp, nt, spd, *refs[:6], refs[6:16], *refs[16:])

    part, keys = pltpu.VMEM((nt, n, hc), BF16), pltpu.VMEM((nt, m, hc), BF16)
    tokens_low, tokens_wide = pltpu.VMEM((n, dim), BF16), pltpu.VMEM((n, dim), F32)
    sequences = pltpu.VMEM((spd, seq, dim), BF16)
    return pl.pallas_call(
        body,
        in_specs=[smem] * 3 + [any_space] * 13 + [vmem] * 2,
        out_specs=[any_space] * 4 + [vmem] * 2,
        out_shape=[
            shape((nt, 4, dim, width), BF16),
            shape((seqs, lr, dim), BF16),
            shape((ndp, lr, dim), BF16),
            shape((ndp, le, dim), BF16),
            shape((4, rows, width), F32),
            shape((8, dim), F32),
        ],
        scratch_shapes=[
            sequences,
            pltpu.VMEM((spd, enc, dim), BF16),
            sequences,
            tokens_low,
            *[part] * 4,
            tokens_wide,
            tokens_low,
            part,
            keys,
            keys,
            part,
            tokens_wide,
            tokens_low,
            pltpu.VMEM((dim, n), BF16),
            tokens_low,
            pltpu.VMEM((dim, n), BF16),
            pltpu.VMEM((dim, m), BF16),
            tokens_wide,
            pltpu.VMEM((m, dim), F32),
            tokens_wide,
            sequences,
            sequences,
            pltpu.VMEM((spd, enc, dim), BF16),
            pltpu.VMEM((n, 3 * hc), BF16),
            pltpu.VMEM((m, hc), BF16),
            pltpu.VMEM((m, hc), BF16),
            pltpu.VMEM((4, dim, width), BF16),
            pltpu.VMEM((ndp, lr, dim), BF16),
            pltpu.VMEM((ndp, le, dim), BF16),
            pltpu.VMEM((ndp, lr, dim), BF16),
            pltpu.VMEM((ndp, le, dim), BF16),
            pltpu.VMEM((seqs, lr, dim), BF16),
            pltpu.VMEM((seqs, le, dim), BF16),
            pltpu.VMEM((DW_SLOTS, chips, 2, rows, width), BF16),
            pltpu.VMEM((CORE_SLOTS, chips, rows, width), BF16),
            pltpu.VMEM((CHIP_SLOTS, 2 * (chips - 1), half, width), BF16),
            pltpu.VMEM((4, nt - 1, rows, width), BF16),
            pltpu.VMEM((CHIP_GAP * levels, chips, rows, width), BF16),
            pltpu.VMEM((Z_SLOTS, rows, width), BF16),
            pltpu.VMEM((steps + 1, 8, dim), F32),
            pltpu.VMEM((steps, 8, dim), F32),
            dma((15,)),
            dma((4,)),
            dma((4,)),
            *[dma((ndp,)) for _ in range(4)],
            *[dma((nt,)) for _ in range(6)],
            dma((4, 2)),
            dma((4, nt)),
            dma((gathers,)),
            dma((gathers, gather_slots)),
            dma((gathers, gather_slots)),
            dma((count, slots)),
            dma((count, slots)),
            dma((4, nt - 1)),
            dma((4, nt - 1)),
            dma((steps,)),
            dma((steps,)),
            *[dma((nt,)) for _ in range(6)],
            *[dma((ndp,)) for _ in range(4)],
            pltpu.SemaphoreType.REGULAR,
            pltpu.SemaphoreType.REGULAR((levels, 2)),
            pltpu.SemaphoreType.REGULAR((2,)),
        ],
        compiler_params=pltpu.CompilerParams(
            collective_id=0, has_side_effects=True, vmem_limit_bytes=VMEM_LIMIT
        ),
        name="layer",
    )(deal, tok_len, enc_len, tokens, enc_states, cot, *weights, gain, bias)


def tail_kernel(seqs, deal_ref, res, rx_tok, rx_enc, grads, norm, *outs):
    d = lax.axis_index("dp")
    result, d_tok, d_enc = outs[:3]
    hc = outs[3].shape[1]
    result[...] = res[...]
    for i in range(seqs):
        peer = 0
        for k in range(rx_tok.shape[0]):
            peer = jnp.where(deal_ref[k * seqs + i] == d * seqs + i, k, peer)
        d_tok[i] = rx_tok[peer]
        d_enc[i] = rx_enc[peer]
    for g in range(2):
        for i in range(3):
            outs[3 + 4 * g + i][...] = grads[g, :, i * hc : (i + 1) * hc]
        outs[6 + 4 * g][...] = grads[g, :, 3 * hc :].T
    outs[11][...] = grads[2]
    outs[12][...] = grads[3].T
    outs[13][...] = norm[0:3]
    outs[14][...] = norm[3:6]


def tail(deal, res, rx_tok, rx_enc, grads, norm):
    seqs, lr, dim = res.shape
    le = rx_enc.shape[1]
    rows, width = grads.shape[1:]
    hc = width // 4
    vmem = pl.BlockSpec(memory_space=pltpu.VMEM)
    straight, turned = ((rows, hc), F32), ((hc, rows), F32)
    shapes = [((seqs, lr, dim), BF16), ((seqs, lr, dim), BF16), ((seqs, le, dim), BF16)]
    shapes += ([straight] * 3 + [turned]) * 2
    shapes += [((rows, width), F32), ((width, rows), F32), ((3, dim), F32), ((3, dim), F32)]
    return pl.pallas_call(
        functools.partial(tail_kernel, seqs),
        in_specs=[pl.BlockSpec(memory_space=pltpu.SMEM)] + [vmem] * 5,
        out_specs=[vmem] * len(shapes),
        out_shape=[jax.ShapeDtypeStruct(*one) for one in shapes],
        compiler_params=pltpu.CompilerParams(vmem_limit_bytes=VMEM_LIMIT),
        name="tail",
    )(deal, res, rx_tok, rx_enc, grads, norm)


def per_device(ndp, nt, tokens, enc_states, cotangent, tok_len, enc_len, deal, *rest):
    *weights, gain, bias = rest
    spd = tokens.shape[0] // nt
    _, *made = layer(
        ndp, nt, spd, deal, tok_len, enc_len, tokens, enc_states, cotangent, weights, gain, bias
    )
    return tail(deal, *made)


def solution(mesh):
    ndp, nt = mesh.shape["dp"], mesh.shape["tensor"]
    rows = P("dp", "tensor", None)
    columns = P(None, "tensor")
    split = P("tensor", None)
    grad = P("dp", "tensor")
    turned = P("tensor", "dp")
    return jax.shard_map(
        functools.partial(per_device, ndp, nt),
        mesh=mesh,
        in_specs=(
            (rows,) * 3
            + (P(),) * 3
            + (columns, columns, columns, split) * 2
            + (columns, split, P(), P())
        ),
        out_specs=(
            (rows,) * 3 + (grad, grad, grad, turned) * 2 + (grad, turned) + (P(), P())
        ),
        check_vma=False,
    )
```
